256 devices in a mesh: region: 32 (over x_hi, z, core), panel: 8 (over x_lo, y).
Axes of the slice: x: 4 (x_hi: 2, x_lo: 2; x = x_hi * 2 + x_lo), y: 4, z: 8, core: 2. Of those that a mesh axis runs over, the one named last changes fastest.
Arguments:
- latents: bfloat16 [262144, 128], P(('region', 'panel')), may hold values from -6 to 6
- edge_feats: bfloat16 [786432, 128], P(('region', 'panel')), may hold values from -6 to 6
- weights: bfloat16 [9, 128, 128], replicated, may hold values from -0.5 to 0.5
- cotangent: bfloat16 [262144, 128], P(('region', 'panel')), may hold values from -6 to 6
- mesh_edges: int32 [2, 786432], P(None, ('region', 'panel')), may hold values from 0 to 1151, as said below
- boundary: int32 [65536], P(('region', 'panel')), may hold values from 0 to 1023, as said below
- contact_edges: int32 [2, 2097152], P(None, ('region', 'panel')), may hold values from 0 to 255, as said below
- contact_counts: int32 [256, 4], P(('region', 'panel')), may hold values from 256 to 2048, as said below
Outputs:
- new_latents: bfloat16 [262144, 128], P(('region', 'panel'))
- grad_latents: float32 [262144, 128], P(('region', 'panel'))
- grad_weights: float32 [9, 128, 128], replicated
The draws below stay inside these ranges and needn't reach their ends.
Inputs may be any that keep to these rules, and one draw needn't show every extreme that they name: `mesh_edges`: within a block, row 1 is a receiver row of the block (0 to 1023) and row 0 a row of the block's extended matrix within 64 of the receiver's row + 64. A block's boundary rows are distinct, the k-th lies in 4k to 4k + 3. `contact_edges`: row 0 is a boundary slot of the block, row 1 a boundary slot of the round's partner; columns of a run at or after the round's count are padding with arbitrary slots. `contact_counts`: in every round some block has all 2048 slots live.
All inputs are finite; a program needn't handle non-finite values.
Results may differ from the reference program's by a relative error of at most 0.0079.
Values may be sent and summed in bfloat16 or wider, within the bound.
No kernel may reach another device: no remote copies, remote signals or barrier semaphores. Data moves between devices by JAX's collectives and lax.ppermute only.
A program may use at most 64 MiB of HBM per device.

```python
import math
import jax
import jax.numpy as jnp
from jax import lax

D = 128
V_DEV = 1024
HB = 64
ROUNDS = 4
EDGE_DEV = 3072
CB = 256
CROWS = 2048
BLOCKS = 256
NODES = 262144
EDGES = 786432
CEDGES = 2097152
N_REGION = 32
N_PANEL = 8


def draw_mesh_edges(key, part):
    key = jax.random.fold_in(key, 11)
    blocks = EDGES // EDGE_DEV
    key_recv, key_step, key_sign = jax.random.split(key, 3)
    receivers = jax.random.randint(key_recv, (blocks, EDGE_DEV), 0, V_DEV)
    offsets = jax.random.randint(key_step, (blocks, EDGE_DEV), 1, HB + 1)
    sign_flip = jax.random.randint(key_sign, (blocks, EDGE_DEV), 0, 2) * 2 - 1
    senders = receivers + HB + sign_flip * offsets
    receivers = receivers.at[:, 0].set(V_DEV - 1).at[:, 1].set(0)
    senders = senders.at[:, 0].set(V_DEV - 1 + 2 * HB).at[:, 1].set(0)
    return jnp.stack([senders.reshape(-1), receivers.reshape(-1)]).astype(jnp.int32)


def draw_boundary(key, part):
    key = jax.random.fold_in(key, 12)
    blocks = NODES // V_DEV
    stride = V_DEV // CB
    offsets = jax.random.randint(key, (blocks, CB), 0, stride)
    offsets = offsets.at[:, 0].set(0).at[:, CB - 1].set(stride - 1)
    row_ids = jnp.arange(CB, dtype=jnp.int32)[None, :] * stride + offsets
    return row_ids.reshape(-1).astype(jnp.int32)


def draw_contact_edges(key, part):
    key = jax.random.fold_in(key, 13)
    blocks = CEDGES // (ROUNDS * CROWS)
    slot_ids = jax.random.randint(key, (2, blocks, ROUNDS * CROWS), 0, CB)
    slot_ids = slot_ids.at[0, :, 0].set(CB - 1).at[1, :, 0].set(0)
    slot_ids = slot_ids.at[0, :, 1].set(0).at[1, :, 1].set(CB - 1)
    return slot_ids.reshape(2, -1).astype(jnp.int32)


def draw_contact_counts(key, part):
    key = jax.random.fold_in(key, 14)
    key_base, key_heavy, key_chosen = jax.random.split(key, 3)
    base_counts = jax.random.randint(key_base, (BLOCKS, ROUNDS), CROWS // 8, CROWS // 2 + 1)
    heavy_rows = jax.random.randint(key_heavy, (BLOCKS, ROUNDS), 0, 8) == 0
    chosen = jax.random.randint(key_chosen, (ROUNDS,), 0, BLOCKS)
    full_rows = heavy_rows | (jnp.arange(BLOCKS, dtype=jnp.int32)[:, None] == chosen[None, :])
    return jnp.where(full_rows, CROWS, base_counts).astype(jnp.int32)


def level_of(rng, dims, cuts, low, largest):
    def one(dim, blocks):
        draws = jax.random.uniform(jax.random.fold_in(jax.random.fold_in(rng, 6), dim), (blocks,), jnp.float32, low / len(cuts), largest / len(cuts))
        return jnp.repeat(jnp.exp(draws), dims[dim] // blocks).reshape((-1,) + (1,) * (len(dims) - dim - 1))

    level = one(*cuts[0])
    for cut in cuts[1:]:
        level = level * one(*cut)
    return level


def centred(own_key, dims, deviation, most, cuts=(), kind=jnp.bfloat16):
    drawn = deviation * jax.random.normal(own_key, dims, jnp.float32)
    if cuts:
        drawn = drawn * level_of(own_key, dims, cuts, -0.22, 0.18)
    return jnp.clip(drawn, -most, most).astype(kind)


def setup_inputs(seed: int = 0) -> dict:
    splits = jax.random.split(jax.random.key(seed), 9)
    latents = centred(splits[0], (NODES, D), 1.0, 6.0, ((0, 256),))
    edge_feats = centred(splits[1], (EDGES, D), 1.0, 6.0, ((0, 256),))
    weights = centred(splits[2], (9, D, D), D ** -0.5, 0.5)
    cotangent = centred(splits[3], (NODES, D), 1.0, 6.0, ((0, 256),))
    mesh_edges = draw_mesh_edges(jax.random.fold_in(splits[8], 71), 0)
    boundary = draw_boundary(jax.random.fold_in(splits[8], 71), 0)
    contact_edges = draw_contact_edges(jax.random.fold_in(splits[8], 71), 0)
    contact_counts = draw_contact_counts(jax.random.fold_in(splits[8], 71), 0)
    return {"latents": latents, "edge_feats": edge_feats, "weights": weights, "cotangent": cotangent, "mesh_edges": mesh_edges, "boundary": boundary, "contact_edges": contact_edges, "contact_counts": contact_counts}


def swish_gradient(values):
    sigmoid = jax.nn.sigmoid(values)
    return sigmoid * (1.0 + values * (1.0 - sigmoid))

def product(left_side, right_side):
    return jnp.dot(left_side, right_side, preferred_element_type=jnp.float32)

def over_rows(left_side, right_side):
    return lax.dot_general(left_side, right_side, (((0,), (0,)), ((), ())), preferred_element_type=jnp.float32)

def times_transpose(left_side, right_side):
    return lax.dot_general(left_side, right_side, (((1,), (1,)), ((), ())), preferred_element_type=jnp.float32)

def segment_add(values, targets, segments):
    return jax.ops.segment_sum(values, targets, num_segments=segments)

def one_block(weights, pieces):
    node_block, extended, features, edge_pairs, cotangent, bound_rows, partners, contacts, partner_tally = pieces
    senders = edge_pairs[0]
    receivers = edge_pairs[1]
    send_rows = extended[senders]
    recv_rows = node_block[receivers]
    pre_mesh = product(send_rows, weights[0]) + product(recv_rows, weights[1]) + product(features, weights[2])
    msg_mesh = jax.nn.silu(pre_mesh).astype(jnp.bfloat16)
    agg_mesh = segment_add(msg_mesh.astype(jnp.float32), receivers, V_DEV).astype(jnp.bfloat16)
    bound_lat = node_block[bound_rows]
    slot_positions = jnp.arange(CROWS, dtype=jnp.int32)
    agg_bound = jnp.zeros((CB, D), jnp.float32)
    stored_rounds = []
    for round_lookup in range(ROUNDS):
        self_index = contacts[0, round_lookup]
        remote_index = contacts[1, round_lookup]
        active_flags = (slot_positions < partner_tally[round_lookup]).astype(jnp.float32)[:, None]
        self_rows = bound_lat[self_index]
        remote_rows = partners[round_lookup][remote_index]
        contact_preactivation = product(self_rows, weights[3]) + product(remote_rows, weights[4])
        contact_message = (jax.nn.silu(contact_preactivation) * active_flags).astype(jnp.bfloat16)
        agg_bound = agg_bound + segment_add(contact_message.astype(jnp.float32), self_index, CB)
        stored_rounds.append((self_index, remote_index, active_flags, self_rows, remote_rows, contact_preactivation))
    agg_contact = jnp.zeros((V_DEV, D), jnp.float32).at[bound_rows].set(agg_bound).astype(jnp.bfloat16)
    pre_node = product(node_block, weights[5]) + product(agg_mesh, weights[6]) + product(agg_contact, weights[7])
    hidden = jax.nn.silu(pre_node).astype(jnp.bfloat16)
    new_block = (node_block.astype(jnp.float32) + product(hidden, weights[8])).astype(jnp.bfloat16)
    d_node = (times_transpose(cotangent, weights[8]) * swish_gradient(pre_node)).astype(jnp.bfloat16)
    d_agg_mesh = times_transpose(d_node, weights[6]).astype(jnp.bfloat16)
    d_agg_contact = times_transpose(d_node, weights[7]).astype(jnp.bfloat16)
    grad_block = cotangent.astype(jnp.float32) + times_transpose(d_node, weights[5])
    d_mesh = (d_agg_mesh[receivers].astype(jnp.float32) * swish_gradient(pre_mesh)).astype(jnp.bfloat16)
    d_extended = segment_add(times_transpose(d_mesh, weights[0]), senders, V_DEV + 2 * HB)
    grad_block = grad_block + segment_add(times_transpose(d_mesh, weights[1]), receivers, V_DEV)
    grad_block = grad_block + d_extended[HB:HB + V_DEV]
    boundary_gradient = d_agg_contact[bound_rows]
    grad_own = jnp.zeros((CB, D), jnp.float32)
    grad_three = jnp.zeros((D, D), jnp.float32)
    grad_four = jnp.zeros((D, D), jnp.float32)
    far_grads = []
    for self_index, remote_index, active_flags, self_rows, remote_rows, contact_preactivation in stored_rounds:
        contact_gradient = (boundary_gradient[self_index].astype(jnp.float32) * swish_gradient(contact_preactivation) * active_flags).astype(jnp.bfloat16)
        grad_three = grad_three + over_rows(self_rows, contact_gradient)
        grad_four = grad_four + over_rows(remote_rows, contact_gradient)
        grad_own = grad_own + segment_add(times_transpose(contact_gradient, weights[3]), self_index, CB)
        far_grads.append(segment_add(times_transpose(contact_gradient, weights[4]), remote_index, CB))
    grad_block = grad_block.at[bound_rows].add(grad_own)
    grads = jnp.stack([over_rows(send_rows, d_mesh), over_rows(recv_rows, d_mesh), over_rows(features, d_mesh), grad_three, grad_four, over_rows(node_block, d_node), over_rows(agg_mesh, d_node), over_rows(agg_contact, d_node), over_rows(hidden, cotangent)])
    return (new_block, grad_block, d_extended[:HB], d_extended[HB + V_DEV:], jnp.stack(far_grads), grads)

def place_rows(grad_rows, row_ids, extra):
    return grad_rows.at[row_ids].add(extra)

def reference(latents, edge_feats, weights, cotangent, mesh_edges, boundary, contact_edges, contact_counts):
    blocks = N_REGION * N_PANEL
    node_grid = latents.reshape(N_REGION, N_PANEL, V_DEV, D)
    empty_rim = jnp.zeros((N_REGION, 1, HB, D), latents.dtype)
    lower_rims = jnp.concatenate([empty_rim, node_grid[:, :-1, V_DEV - HB:]], axis=1)
    upper_rims = jnp.concatenate([node_grid[:, 1:, :HB], empty_rim], axis=1)
    extended = jnp.concatenate([lower_rims, node_grid, upper_rims], axis=2)
    bound_rows = boundary.reshape(N_REGION, N_PANEL, CB)
    bound_lat = jnp.take_along_axis(node_grid, bound_rows[..., None], axis=2)
    regions = jnp.arange(N_REGION, dtype=jnp.int32)
    partners = jnp.stack([bound_lat[jnp.bitwise_xor(regions, 1 << round_lookup)] for round_lookup in range(ROUNDS)], axis=2)
    edge_pairs = mesh_edges.reshape(2, blocks, EDGE_DEV).transpose(1, 0, 2)
    contacts = contact_edges.reshape(2, blocks, ROUNDS, CROWS).transpose(1, 0, 2, 3)
    pieces = (node_grid.reshape(blocks, V_DEV, D), extended.reshape(blocks, V_DEV + 2 * HB, D), edge_feats.reshape(blocks, EDGE_DEV, D), edge_pairs, cotangent.reshape(blocks, V_DEV, D), boundary.reshape(blocks, CB), partners.reshape(blocks, ROUNDS, CB, D), contacts, contact_counts)

    def scan_step(grad_total, piece):
        outputs = one_block(weights, piece)
        return (grad_total + outputs[5], outputs[:5])
    grad_total, (new_blocks, grad_blocks, low_rims, high_rims, far_grads) = lax.scan(scan_step, jnp.zeros((9, D, D), jnp.float32), pieces)
    grad_grid = grad_blocks.reshape(N_REGION, N_PANEL, V_DEV, D)
    zero_rim = jnp.zeros((N_REGION, 1, HB, D), grad_grid.dtype)
    from_prev = jnp.concatenate([zero_rim, high_rims.reshape(N_REGION, N_PANEL, HB, D)[:, :-1]], axis=1)
    from_next = jnp.concatenate([low_rims.reshape(N_REGION, N_PANEL, HB, D)[:, 1:], zero_rim], axis=1)
    grad_grid = grad_grid.at[:, :, :HB].add(from_prev)
    grad_grid = grad_grid.at[:, :, V_DEV - HB:].add(from_next)
    far_grid = far_grads.reshape(N_REGION, N_PANEL, ROUNDS, CB, D)
    incoming = far_grid[jnp.bitwise_xor(regions, 1), :, 0]
    for round_lookup in range(1, ROUNDS):
        incoming = incoming + far_grid[jnp.bitwise_xor(regions, 1 << round_lookup), :, round_lookup]
    grad_flat = jax.vmap(place_rows)(grad_grid.reshape(blocks, V_DEV, D), boundary.reshape(blocks, CB), incoming.reshape(blocks, CB, D))
    grad_scale = 1.0 / math.sqrt(NODES)
    return (new_blocks.reshape(NODES, D), grad_flat.reshape(NODES, D), grad_total * grad_scale)
```

```python
import math

import jax
import jax.numpy as jnp
from jax import lax
from jax.sharding import PartitionSpec as P

HB = 64


def swapped(block, axis, bit):
    count = lax.axis_size(axis)
    route = []
    for low in range(count):
        high = low | 1 << bit
        if high != low and high < count:
            route += [(low, high), (high, low)]
    return lax.ppermute(block, axis, route)


def extended_2(array, sides, width):
    for axis, dim in sides:
        size, length = (lax.axis_size(axis), array.shape[dim])
        up = [(i, (i + 1) % size) for i in range(size - 1)]
        down = [(j, i) for i, j in up]
        last = lax.slice_in_dim(array, length - width, length, axis=dim)
        first = lax.slice_in_dim(array, 0, width, axis=dim)
        before = lax.ppermute(last, axis, up)
        after = lax.ppermute(first, axis, down)
        array = jnp.concatenate([before, array, after], axis=dim)
    return array


def shifted(array, axis, by):
    length = lax.axis_size(axis)
    pairs = [(i, i + by) for i in range(length) if 0 <= i + by < length]
    return lax.ppermute(array, axis, pairs)


def swish_gradient(values):
    sigmoid = jax.nn.sigmoid(values)
    return sigmoid * (1.0 + values * (1.0 - sigmoid))


def product(left_side, right_side):
    return jnp.dot(left_side, right_side, preferred_element_type=jnp.float32)


def over_rows(left_side, right_side):
    return lax.dot_general(
        left_side, right_side, (((0,), (0,)), ((), ())), preferred_element_type=jnp.float32
    )


def times_transpose(left_side, right_side):
    return lax.dot_general(
        left_side, right_side, (((1,), (1,)), ((), ())), preferred_element_type=jnp.float32
    )


def exact_transpose(left_side, weight_matrix):
    return lax.dot_general(
        left_side,
        weight_matrix.astype(jnp.float32),
        (((1,), (1,)), ((), ())),
        precision=lax.Precision.HIGHEST,
        preferred_element_type=jnp.float32,
    )


def exact_over_rows(left_side, right_side):
    return lax.dot_general(
        left_side.astype(jnp.float32),
        right_side,
        (((0,), (0,)), ((), ())),
        precision=lax.Precision.HIGHEST,
        preferred_element_type=jnp.float32,
    )


def one_hot_rows(row_ids, count):
    return (row_ids[:, None] == jnp.arange(count, dtype=jnp.int32)[None, :]).astype(jnp.bfloat16)


def each_block(adder, totals, active_count, total_rows):
    return adder(totals, 0, total_rows, active_count)


def sliced_rows(self_index, remote_index, leading_row, count_of_rows, active_count, slot_count):
    active_flags = (leading_row + jnp.arange(count_of_rows, dtype=jnp.int32) < active_count).astype(
        jnp.float32
    )[:, None]
    return (
        one_hot_rows(self_index, slot_count),
        one_hot_rows(remote_index, slot_count),
        active_flags,
    )


def contact_rows_of(bound_lat, far_lat, weights, self_table, remote_table):
    self_rows = product(self_table, bound_lat).astype(jnp.bfloat16)
    remote_rows = product(remote_table, far_lat).astype(jnp.bfloat16)
    contact_preactivation = product(self_rows, weights[3]) + product(remote_rows, weights[4])
    return (self_rows, remote_rows, contact_preactivation)


def forward_adder(bound_lat, far_lat, weights, self_index, remote_index):
    slot_count = bound_lat.shape[0]

    def adder(totals, leading_row, count_of_rows, active_count):
        self_table, remote_table, active_flags = sliced_rows(
            self_index, remote_index, leading_row, count_of_rows, active_count, slot_count
        )
        self_rows, remote_rows, contact_preactivation = contact_rows_of(
            bound_lat, far_lat, weights, self_table, remote_table
        )
        message_value = (jax.nn.silu(contact_preactivation) * active_flags).astype(jnp.bfloat16)
        return totals + over_rows(self_table, message_value)

    return adder


def backward_adder(bound_lat, far_lat, boundary_gradient, weights, self_index, remote_index):
    slot_count = bound_lat.shape[0]

    def adder(totals, leading_row, count_of_rows, active_count):
        self_table, remote_table, active_flags = sliced_rows(
            self_index, remote_index, leading_row, count_of_rows, active_count, slot_count
        )
        self_rows, remote_rows, contact_preactivation = contact_rows_of(
            bound_lat, far_lat, weights, self_table, remote_table
        )
        local_gradient = product(self_table, boundary_gradient)
        contact_gradient = (
            local_gradient * swish_gradient(contact_preactivation) * active_flags
        ).astype(jnp.bfloat16)
        grad_three, grad_four, sum_own, sum_far = totals
        return (
            grad_three + over_rows(self_rows, contact_gradient),
            grad_four + over_rows(remote_rows, contact_gradient),
            sum_own + over_rows(self_table, contact_gradient),
            over_rows(remote_table, contact_gradient),
        )

    return adder


def shards(
    latents, edge_feats, weights, cotangent, mesh_edges, boundary, contact_edges, contact_counts
):
    rows_dev = latents.shape[0]
    width = latents.shape[1]
    bound_count = boundary.shape[0]
    rounds = contact_counts.shape[1]
    round_rows = contact_edges.shape[1] // rounds
    live_counts = contact_counts[0]
    contacts = contact_edges.reshape(2, rounds, round_rows)
    senders = mesh_edges[0]
    receivers = mesh_edges[1]
    region_size = lax.axis_size("region")
    bound_table = one_hot_rows(boundary, rows_dev)
    bound_lat = product(bound_table, latents).astype(jnp.bfloat16)
    partners = [swapped(bound_lat, "region", round_lookup) for round_lookup in range(rounds)]
    extended = extended_2(latents, (("panel", 0),), HB)
    send_table = one_hot_rows(senders, rows_dev + 2 * HB)
    recv_table = one_hot_rows(receivers, rows_dev)
    send_rows = product(send_table, extended).astype(jnp.bfloat16)
    recv_rows = product(recv_table, latents).astype(jnp.bfloat16)
    pre_mesh = (
        product(send_rows, weights[0])
        + product(recv_rows, weights[1])
        + product(edge_feats, weights[2])
    )
    msg_mesh = jax.nn.silu(pre_mesh).astype(jnp.bfloat16)
    agg_mesh = over_rows(recv_table, msg_mesh).astype(jnp.bfloat16)
    agg_bound = jnp.zeros((bound_count, width), jnp.float32)
    for round_lookup in range(rounds):
        adder = forward_adder(
            bound_lat,
            partners[round_lookup],
            weights,
            contacts[0, round_lookup],
            contacts[1, round_lookup],
        )
        agg_bound = each_block(adder, agg_bound, live_counts[round_lookup], round_rows)
    agg_contact = over_rows(bound_table, agg_bound.astype(jnp.bfloat16)).astype(jnp.bfloat16)
    pre_node = (
        product(latents, weights[5])
        + product(agg_mesh, weights[6])
        + product(agg_contact, weights[7])
    )
    hidden = jax.nn.silu(pre_node).astype(jnp.bfloat16)
    new_rows = (latents.astype(jnp.float32) + product(hidden, weights[8])).astype(jnp.bfloat16)
    d_node = (times_transpose(cotangent, weights[8]) * swish_gradient(pre_node)).astype(
        jnp.bfloat16
    )
    d_agg_mesh = times_transpose(d_node, weights[6]).astype(jnp.bfloat16)
    d_agg_contact = times_transpose(d_node, weights[7]).astype(jnp.bfloat16)
    d_mesh = (product(recv_table, d_agg_mesh) * swish_gradient(pre_mesh)).astype(jnp.bfloat16)
    d_extended = exact_transpose(over_rows(send_table, d_mesh), weights[0])
    from_prev = shifted(d_extended[HB + rows_dev :].astype(jnp.bfloat16), "panel", 1).astype(
        jnp.float32
    )
    from_next = shifted(d_extended[:HB].astype(jnp.bfloat16), "panel", -1).astype(jnp.float32)
    grad_rows = cotangent.astype(jnp.float32) + times_transpose(d_node, weights[5])
    grad_rows = grad_rows + exact_transpose(over_rows(recv_table, d_mesh), weights[1])
    grad_rows = grad_rows + d_extended[HB : HB + rows_dev]
    boundary_gradient = product(bound_table, d_agg_contact).astype(jnp.bfloat16)
    grad_three = jnp.zeros((width, width), jnp.float32)
    grad_four = jnp.zeros((width, width), jnp.float32)
    sum_own = jnp.zeros((bound_count, width), jnp.float32)
    far_grads = []
    for round_lookup in range(rounds):
        adder = backward_adder(
            bound_lat,
            partners[round_lookup],
            boundary_gradient,
            weights,
            contacts[0, round_lookup],
            contacts[1, round_lookup],
        )
        totals = (grad_three, grad_four, sum_own, jnp.zeros((bound_count, width), jnp.float32))
        grad_three, grad_four, sum_own, sum_far = each_block(
            adder, totals, live_counts[round_lookup], round_rows
        )
        far_grads.append(exact_transpose(sum_far, weights[4]))
    grad_own = exact_transpose(sum_own, weights[3])
    incoming = jnp.zeros((bound_count, width), jnp.float32)
    for round_lookup in range(rounds):
        incoming = incoming + swapped(
            far_grads[round_lookup].astype(jnp.bfloat16), "region", round_lookup
        ).astype(jnp.float32)
    grad_rows = grad_rows.at[:HB].add(from_prev)
    grad_rows = grad_rows.at[rows_dev - HB :].add(from_next)
    grad_rows = grad_rows + exact_over_rows(bound_table, grad_own + incoming)
    grads = jnp.stack(
        [
            over_rows(send_rows, d_mesh),
            over_rows(recv_rows, d_mesh),
            over_rows(edge_feats, d_mesh),
            grad_three,
            grad_four,
            over_rows(latents, d_node),
            over_rows(agg_mesh, d_node),
            over_rows(agg_contact, d_node),
            over_rows(hidden, cotangent),
        ]
    )
    grad_scale = 1.0 / math.sqrt(rows_dev * region_size * lax.axis_size("panel"))
    summed = summed_everywhere((grads * grad_scale).reshape(-1, width)).reshape(grads.shape)
    return (new_rows, grad_rows, summed)


def exchanged(block, mask_x=0, mask_y=0, mask_z=0, mask_core=0):
    route = []
    for region in range(32):
        for panel in range(8):
            other_region = region ^ ((mask_x >> 1) << 4 | mask_z << 1 | mask_core)
            other_panel = panel ^ ((mask_x & 1) << 2 | mask_y)
            route.append((region * 8 + panel, other_region * 8 + other_panel))
    return lax.ppermute(block, ("region", "panel"), route)


def wide(block):
    return block.astype(jnp.float32)


def four_sum(block, name):
    one, two, three = [wide(exchanged(block, **{name: mask})) for mask in (1, 2, 3)]
    return ((wide(block) + one) + (two + three)).astype(jnp.bfloat16)


def summed_everywhere(grads):
    rows = grads.shape[0]
    half = rows // 2
    part = half // 4
    core = lax.axis_index("region") % 2
    row_y = lax.axis_index("panel") % 4
    block = grads.astype(jnp.bfloat16)
    kept = lax.dynamic_slice_in_dim(grads, core * half, half, 0)
    sent = lax.dynamic_slice_in_dim(block, (1 - core) * half, half, 0)
    block = (kept + wide(exchanged(sent, mask_core=1))).astype(jnp.bfloat16)
    pieces = [
        lax.dynamic_slice_in_dim(block, (row_y ^ mask) * part, part, 0) for mask in range(4)
    ]
    one, two, three = [
        wide(exchanged(pieces[mask], mask_y=mask)) for mask in (1, 2, 3)
    ]
    block = ((wide(pieces[0]) + one) + (two + three)).astype(jnp.bfloat16)
    block = four_sum(block, "mask_x")
    block = four_sum(block, "mask_z")
    block = (wide(block) + wide(exchanged(block, mask_z=4))).astype(jnp.bfloat16)
    found = [block] + [exchanged(block, mask_y=mask) for mask in (1, 2, 3)]
    odd, high = row_y % 2 == 1, row_y >= 2
    low_pair = [jnp.where(odd, found[1], found[0]), jnp.where(odd, found[0], found[1])]
    high_pair = [jnp.where(odd, found[3], found[2]), jnp.where(odd, found[2], found[3])]
    ordered = [jnp.where(high, b, a) for a, b in zip(low_pair, high_pair)]
    ordered += [jnp.where(high, a, b) for a, b in zip(low_pair, high_pair)]
    block = jnp.concatenate(ordered, axis=0)
    other = exchanged(block, mask_core=1)
    first = jnp.where(core == 1, other, block)
    second = jnp.where(core == 1, block, other)
    return wide(jnp.concatenate([first, second], axis=0))


def solution(mesh):
    placed = (
        P(("region", "panel"), None),
        P(("region", "panel"), None),
        P(),
        P(("region", "panel"), None),
        P(None, ("region", "panel")),
        P(("region", "panel")),
        P(None, ("region", "panel")),
        P(("region", "panel"), None),
    )
    return jax.shard_map(
        shards,
        mesh=mesh,
        in_specs=placed,
        out_specs=(P(("region", "panel"), None), P(("region", "panel"), None), P()),
        check_vma=False,
    )
```

```python
import functools
import math

import jax
import jax.numpy as jnp
from jax import lax
from jax.experimental import pallas as pl
from jax.experimental.pallas import tpu as pltpu
from jax.sharding import PartitionSpec as P

HB = 64
CHUNK = 512
BF = jnp.bfloat16
F32 = jnp.float32
VMEM_BYTES = 56 * 1024 * 1024


def nn(a, b):
    return lax.dot_general(a, b, (((1,), (0,)), ((), ())), preferred_element_type=F32)


def nt(a, b):
    return lax.dot_general(a, b, (((1,), (1,)), ((), ())), preferred_element_type=F32)


def tn(a, b):
    return lax.dot_general(a, b, (((0,), (0,)), ((), ())), preferred_element_type=F32)


def in_two(values):
    high = values.astype(BF)
    return high, (values - high.astype(F32)).astype(BF)


def wide_nt(a, b):
    high, low = in_two(a)
    return nt(high, b) + nt(low, b)


def wide_nn(a, b):
    high, low = in_two(b)
    return nn(a, high) + nn(a, low)


def identity():
    row = lax.broadcasted_iota(jnp.int32, (128, 128), 0)
    column = lax.broadcasted_iota(jnp.int32, (128, 128), 1)
    return (row == column).astype(BF)


def transposed(a):
    return nt(identity(), a).astype(BF)


def table(count, ids):
    rows = lax.broadcasted_iota(jnp.int32, (count, ids.shape[1]), 0)
    return (rows == ids).astype(BF)


def rim_table(rows_dev, ids):
    rows = lax.broadcasted_iota(jnp.int32, (2 * HB, ids.shape[1]), 0)
    rows = jnp.where(rows < HB, rows, rows + rows_dev)
    return (rows == ids).astype(BF)


def silu_parts(x):
    s = 0.5 * jnp.tanh(0.5 * x) + 0.5
    return x * s, s * (1.0 + x * (1.0 - s))


def columns(step):
    return pl.ds(pl.multiple_of(step * CHUNK, CHUNK), CHUNK)


def bound_kernel(lat_ref, bnd_ref, lat_t_ref, bound_t_ref):
    lat_t = transposed(lat_ref[...])
    lat_t_ref[...] = lat_t
    bound_t_ref[...] = nn(lat_t, table(lat_ref.shape[0], bnd_ref[...])).astype(BF)


def local_kernel(lat_t_ref, bound_t_ref, edges_ref, contacts_ref, rows_ref, own_ref):
    rows_dev = lat_t_ref.shape[1]

    @pl.loop(0, edges_ref.shape[1] // CHUNK)
    def _(step):
        at = columns(step)
        lat_t = lat_t_ref[...]
        rows_ref[:128, at] = nn(lat_t, table(rows_dev, edges_ref[0:1, at] - HB)).astype(BF)
        rows_ref[128:, at] = nn(lat_t, table(rows_dev, edges_ref[1:2, at])).astype(BF)

    @pl.loop(0, contacts_ref.shape[1] // CHUNK)
    def _(step):
        at = columns(step)
        bound_t = bound_t_ref[...]
        own_ref[:, at] = nn(bound_t, table(bound_t.shape[1], contacts_ref[0:1, at])).astype(BF)


def main_kernel(
    counts_ref,
    core_ref,
    lat_ref,
    lat_t_ref,
    rim_ref,
    far0_ref,
    far1_ref,
    far2_ref,
    far3_ref,
    rows_in_ref,
    own_ref,
    feats_ref,
    cot_ref,
    w_ref,
    edges_ref,
    contacts_ref,
    bnd_ref,
    new_ref,
    kept_ref,
    sent_ref,
    dm_ref,
    dc_ref,
    base_ref,
    agg_ref,
    aggb_ref,
    slope_m_ref,
    slope_c_ref,
    rows_ref,
    both_ref,
    gw_ref,
    wt_ref,
    aggc_ref,
    dagg_t_ref,
    daggc_t_ref,
    dbg_t_ref,
    *,
    scale,
):
    rows_dev = lat_ref.shape[0]
    bound_count = bnd_ref.shape[1]
    fars = (far0_ref, far1_ref, far2_ref, far3_ref)
    rounds = len(fars)
    round_rows = contacts_ref.shape[1] // rounds
    per_round = round_rows // CHUNK
    steps = edges_ref.shape[1] // CHUNK

    agg_ref[...] = jnp.zeros_like(agg_ref)
    aggb_ref[...] = jnp.zeros_like(aggb_ref)
    gw_ref[...] = jnp.zeros_like(gw_ref)
    wt_ref[0:128, 0:128] = transposed(w_ref[0])
    wt_ref[0:128, 128:256] = transposed(w_ref[1])
    wt_ref[128:256, 0:128] = transposed(w_ref[3])
    wt_ref[128:256, 128:256] = transposed(w_ref[4])
    w2_t = transposed(w_ref[2])
    rim_t = transposed(rim_ref[...])

    @pl.loop(0, steps)
    def _(step):
        at = columns(step)
        from_rim = nn(rim_t, rim_table(rows_dev, edges_ref[0:1, at]))
        rows_ref[:128, at] = (rows_in_ref[:128, at].astype(F32) + from_rim).astype(BF)
        rows_ref[128:, at] = rows_in_ref[128:, at]
        x = nn(wt_ref[0:128, :], rows_ref[:, at]) + nt(w2_t, feats_ref[at, :])
        message, slope = silu_parts(x)
        slope_m_ref[:, at] = slope
        agg_ref[...] += nt(table(rows_dev, edges_ref[1:2, at]), message.astype(BF))

    for r in range(rounds):
        far_ref = fars[r]
        count = counts_ref[0, r]

        @pl.loop(0, per_round)
        def _(part):
            @pl.when(part * CHUNK < count)
            def _():
                at = columns(r * per_round + part)
                place = lax.broadcasted_iota(jnp.int32, (1, CHUNK), 1) + part * CHUNK
                live = (place < count).astype(F32)
                both_ref[:128, at] = own_ref[:, at]
                both_ref[128:, at] = nn(
                    far_ref[...], table(bound_count, contacts_ref[1:2, at])
                ).astype(BF)
                x = nn(wt_ref[128:256, :], both_ref[:, at])
                message, slope = silu_parts(x)
                slope_c_ref[:, at] = slope * live
                aggb_ref[...] += nt(
                    table(bound_count, contacts_ref[0:1, at]), (message * live).astype(BF)
                )

    bound_table = table(rows_dev, bnd_ref[...])
    aggc_ref[...] = nn(bound_table, aggb_ref[...].astype(BF)).astype(BF)
    node = 256

    @pl.loop(0, rows_dev // node)
    def _(step):
        at = pl.ds(pl.multiple_of(step * node, node), node)
        lat = lat_ref[at, :]
        cot = cot_ref[at, :]
        agg = agg_ref[at, :].astype(BF)
        aggc = aggc_ref[at, :]
        x = nn(lat, w_ref[5]) + nn(agg, w_ref[6]) + nn(aggc, w_ref[7])
        message, slope = silu_parts(x)
        hidden = message.astype(BF)
        new_ref[at, :] = (lat.astype(F32) + nn(hidden, w_ref[8])).astype(BF)
        d_node = (nt(cot, w_ref[8]) * slope).astype(BF)
        base_ref[at, :] = cot.astype(F32) + nt(d_node, w_ref[5])
        dagg_t_ref[:, at] = nt(w_ref[6], d_node).astype(BF)
        daggc_t_ref[:, at] = nt(w_ref[7], d_node).astype(BF)
        gw_ref[640:768, :] += nn(lat_t_ref[:, at], d_node)
        gw_ref[768:896, :] += tn(agg, d_node)
        gw_ref[896:1024, :] += tn(aggc, d_node)
        gw_ref[1024:1152, :] += tn(hidden, cot)

    dbg_t_ref[...] = nn(daggc_t_ref[...], bound_table).astype(BF)

    @pl.loop(0, steps)
    def _(step):
        at = columns(step)
        gathered = nn(dagg_t_ref[...], table(rows_dev, edges_ref[1:2, at]))
        d = (gathered * slope_m_ref[:, at]).astype(BF)
        dm_ref[:, at] = d
        gw_ref[0:256, :] += nt(rows_ref[:, at], d)
        gw_ref[256:384, :] += nn(d, feats_ref[at, :])

    gw_ref[256:384, :] = gw_ref[256:384, :].T

    for r in range(rounds):
        count = counts_ref[0, r]

        @pl.loop(0, per_round)
        def _(part):
            @pl.when(part * CHUNK < count)
            def _():
                at = columns(r * per_round + part)
                gathered = nn(dbg_t_ref[...], table(bound_count, contacts_ref[0:1, at]))
                d = (gathered * slope_c_ref[:, at]).astype(BF)
                dc_ref[:, at] = d
                gw_ref[384:640, :] += nt(both_ref[:, at], d)

    half = gw_ref.shape[0] // 2
    core = core_ref[0]
    kept_ref[...] = gw_ref[pl.ds(pl.multiple_of(core * half, 64), half), :] * scale
    sent = gw_ref[pl.ds(pl.multiple_of((1 - core) * half, 64), half), :] * scale
    sent_ref[...] = sent.astype(BF)


def contact_back_kernel(
    counts_ref, w_ref, contacts_ref, dc_ref, far0_ref, far1_ref, far2_ref, far3_ref, own_ref, sum_ref
):
    outs = (far0_ref, far1_ref, far2_ref, far3_ref)
    bound_count = own_ref.shape[0]
    rounds = len(outs)
    per_round = contacts_ref.shape[1] // rounds // CHUNK
    own_ref[...] = jnp.zeros_like(own_ref)
    for r in range(rounds):
        count = counts_ref[0, r]
        sum_ref[...] = jnp.zeros_like(sum_ref)

        @pl.loop(0, per_round)
        def _(part):
            @pl.when(part * CHUNK < count)
            def _():
                at = columns(r * per_round + part)
                d = dc_ref[:, at]
                own_ref[...] += nt(table(bound_count, contacts_ref[0:1, at]), d)
                sum_ref[...] += nt(table(bound_count, contacts_ref[1:2, at]), d)

        outs[r][...] = wide_nt(sum_ref[...], w_ref[4]).astype(BF)
    own_ref[...] = wide_nt(own_ref[...], w_ref[3])


def mesh_back_kernel(
    w_ref, edges_ref, dm_ref, base_ref, grad_ref, low_ref, high_ref, send_ref, recv_ref
):
    rows_dev = base_ref.shape[0]
    send_ref[...] = jnp.zeros_like(send_ref)
    recv_ref[...] = jnp.zeros_like(recv_ref)

    @pl.loop(0, edges_ref.shape[1] // CHUNK)
    def _(step):
        at = columns(step)
        d = dm_ref[:, at]
        send_ref[...] += nt(table(rows_dev + 2 * HB, edges_ref[0:1, at]), d)
        recv_ref[...] += nt(table(rows_dev, edges_ref[1:2, at]), d)

    low_ref[...] = wide_nt(send_ref[:HB, :], w_ref[0]).astype(BF)
    high_ref[...] = wide_nt(send_ref[HB + rows_dev :, :], w_ref[0]).astype(BF)
    grad_ref[...] = (
        base_ref[...]
        + wide_nt(recv_ref[...], w_ref[1])
        + wide_nt(send_ref[HB : HB + rows_dev, :], w_ref[0])
    )


def last_kernel(
    part_ref, own_ref, in0_ref, in1_ref, in2_ref, in3_ref, prev_ref, next_ref, bnd_ref, out_ref
):
    rows_dev = part_ref.shape[0]
    total = own_ref[...]
    for ref in (in0_ref, in1_ref, in2_ref, in3_ref):
        total = total + ref[...].astype(F32)
    out_ref[...] = part_ref[...] + wide_nn(table(rows_dev, bnd_ref[...]), total)
    out_ref[:HB, :] += prev_ref[...].astype(F32)
    out_ref[rows_dev - HB :, :] += next_ref[...].astype(F32)


def call(kernel, outs, args, scratch=(), smem=0, flops=0):
    spec = pl.BlockSpec(memory_space=pltpu.VMEM)
    return pl.pallas_call(
        kernel,
        out_shape=[jax.ShapeDtypeStruct(shape, kind) for shape, kind in outs],
        in_specs=[pl.BlockSpec(memory_space=pltpu.SMEM)] * smem + [spec] * (len(args) - smem),
        out_specs=[spec] * len(outs),
        scratch_shapes=[pltpu.VMEM(shape, kind) for shape, kind in scratch],
        compiler_params=pltpu.CompilerParams(vmem_limit_bytes=VMEM_BYTES),
        cost_estimate=pl.CostEstimate(flops=flops, bytes_accessed=4000000, transcendentals=0),
    )(*args)


def exchanged(block, mask_x=0, mask_y=0, mask_z=0, mask_core=0):
    route = []
    for region in range(32):
        for panel in range(8):
            other_region = region ^ ((mask_x >> 1) << 4 | mask_z << 1 | mask_core)
            other_panel = panel ^ ((mask_x & 1) << 2 | mask_y)
            route.append((region * 8 + panel, other_region * 8 + other_panel))
    return lax.ppermute(block, ("region", "panel"), route)


def swapped(block, bit):
    size = lax.axis_size("region")
    return lax.ppermute(block, "region", [(i, i ^ (1 << bit)) for i in range(size)])


def shifted(array, by):
    length = lax.axis_size("panel")
    pairs = [(i, i + by) for i in range(length) if 0 <= i + by < length]
    return lax.ppermute(array, "panel", pairs)


def wide(block):
    return block.astype(F32)


def four_sum(block, name):
    one, two, three = [wide(exchanged(block, **{name: mask})) for mask in (1, 2, 3)]
    return ((wide(block) + one) + (two + three)).astype(BF)


def summed_everywhere(kept, sent, core, row_y):
    part = kept.shape[0] // 4
    block = (kept + wide(exchanged(sent, mask_core=1))).astype(BF)
    pieces = [
        lax.dynamic_slice_in_dim(block, (row_y ^ mask) * part, part, 0) for mask in range(4)
    ]
    one, two, three = [wide(exchanged(pieces[mask], mask_y=mask)) for mask in (1, 2, 3)]
    block = ((wide(pieces[0]) + one) + (two + three)).astype(BF)
    block = four_sum(block, "mask_x")
    block = four_sum(block, "mask_z")
    block = (wide(block) + wide(exchanged(block, mask_z=4))).astype(BF)
    found = [block] + [exchanged(block, mask_y=mask) for mask in (1, 2, 3)]
    odd, high = row_y % 2 == 1, row_y >= 2
    low_pair = [jnp.where(odd, found[1], found[0]), jnp.where(odd, found[0], found[1])]
    high_pair = [jnp.where(odd, found[3], found[2]), jnp.where(odd, found[2], found[3])]
    ordered = [jnp.where(high, b, a) for a, b in zip(low_pair, high_pair)]
    ordered += [jnp.where(high, a, b) for a, b in zip(low_pair, high_pair)]
    block = jnp.concatenate(ordered, axis=0)
    other = exchanged(block, mask_core=1)
    first = jnp.where(core == 1, other, block)
    second = jnp.where(core == 1, block, other)
    return wide(jnp.concatenate([first, second], axis=0))


def shards(
    latents, edge_feats, weights, cotangent, mesh_edges, boundary, contact_edges, contact_counts
):
    rows_dev, width = latents.shape
    bound_count = boundary.shape[0]
    rounds = contact_counts.shape[1]
    edge_count = mesh_edges.shape[1]
    contact_count = contact_edges.shape[1]
    bnd = boundary.reshape(1, bound_count)
    core = lax.axis_index("region") % 2
    row_y = lax.axis_index("panel") % 4
    scale = 1.0 / math.sqrt(rows_dev * lax.axis_size("region") * lax.axis_size("panel"))

    before = shifted(latents[rows_dev - HB :], 1)
    after = shifted(latents[:HB], -1)
    lat_t, bound_t = call(
        bound_kernel, [((width, rows_dev), BF), ((width, bound_count), BF)], [latents, bnd]
    )
    fars = [swapped(bound_t, r) for r in range(rounds)]
    rows, own_rows = call(
        local_kernel,
        [((2 * width, edge_count), BF), ((width, contact_count), BF)],
        [lat_t, bound_t, mesh_edges, contact_edges],
        flops=4 * 10**9,
    )
    rim = jnp.concatenate([before, after], axis=0)
    new_rows, kept, sent, d_mesh, d_contact, base = call(
        functools.partial(main_kernel, scale=scale),
        [
            ((rows_dev, width), BF),
            ((9 * width // 2, width), F32),
            ((9 * width // 2, width), BF),
            ((width, edge_count), BF),
            ((width, contact_count), BF),
            ((rows_dev, width), F32),
        ],
        [contact_counts, core.reshape(1), latents, lat_t, rim, *fars, rows, own_rows]
        + [edge_feats, cotangent, weights, mesh_edges, contact_edges, bnd],
        [
            ((rows_dev, width), F32),
            ((bound_count, width), F32),
            ((width, edge_count), F32),
            ((width, contact_count), F32),
            ((2 * width, edge_count), BF),
            ((2 * width, contact_count), BF),
            ((9 * width, width), F32),
            ((2 * width, 2 * width), BF),
            ((rows_dev, width), BF),
            ((width, rows_dev), BF),
            ((width, rows_dev), BF),
            ((width, bound_count), BF),
        ],
        smem=2,
        flops=8 * 10**9,
    )
    *far_grads, own_grad = call(
        contact_back_kernel,
        [((bound_count, width), BF)] * rounds + [((bound_count, width), F32)],
        [contact_counts, weights, contact_edges, d_contact],
        [((bound_count, width), F32)],
        smem=1,
        flops=10**9,
    )
    part, low, high = call(
        mesh_back_kernel,
        [((rows_dev, width), F32), ((HB, width), BF), ((HB, width), BF)],
        [weights, mesh_edges, d_mesh, base],
        [((rows_dev + 2 * HB, width), F32), ((rows_dev, width), F32)],
        flops=2 * 10**9,
    )
    incoming = [swapped(far_grads[r], r) for r in range(rounds)]
    from_prev = shifted(high, 1)
    from_next = shifted(low, -1)
    (grad_rows,) = call(
        last_kernel,
        [((rows_dev, width), F32)],
        [part, own_grad, *incoming, from_prev, from_next, bnd],
    )
    summed = summed_everywhere(kept, sent, core, row_y).reshape(9, width, width)
    return (new_rows, grad_rows, summed)


def solution(mesh):
    blocks = P(("region", "panel"), None)
    placed = (
        blocks,
        blocks,
        P(),
        blocks,
        P(None, ("region", "panel")),
        P(("region", "panel")),
        P(None, ("region", "panel")),
        blocks,
    )
    return jax.shard_map(
        shards, mesh=mesh, in_specs=placed, out_specs=(blocks, blocks, P()), check_vma=False
    )
```

```python
import functools
import math

import jax
import jax.numpy as jnp
from jax import lax
from jax.experimental import pallas as pl
from jax.experimental.pallas import tpu as pltpu
from jax.sharding import PartitionSpec as P

HB = 64
BF = jnp.bfloat16
F32 = jnp.float32
MESH_SPAN = 1536
NODE_SPAN = 512
MIB = 1024 * 1024


def nn(a, b):
    return lax.dot_general(a, b, (((1,), (0,)), ((), ())), preferred_element_type=F32)


def nt(a, b):
    return lax.dot_general(a, b, (((1,), (1,)), ((), ())), preferred_element_type=F32)


def tn(a, b):
    return lax.dot_general(a, b, (((0,), (0,)), ((), ())), preferred_element_type=F32)


def in_two(values):
    high = values.astype(BF)
    return high, (values - high.astype(F32)).astype(BF)


def wide_nt(a, b):
    high, low = in_two(a)
    return nt(high, b) + nt(low, b)


def wide_nn(a, b):
    high, low = in_two(b)
    return nn(a, high) + nn(a, low)


def identity():
    row = lax.broadcasted_iota(jnp.int32, (128, 128), 0)
    column = lax.broadcasted_iota(jnp.int32, (128, 128), 1)
    return (row == column).astype(BF)


def transposed(a):
    return nt(identity(), a).astype(BF)


def table(count, ids):
    rows = lax.broadcasted_iota(jnp.int32, (count, ids.shape[1]), 0)
    return (rows == ids).astype(BF)


def silu_parts(x):
    s = 0.5 * jnp.tanh(0.5 * x) + 0.5
    return x * s, s * (1.0 + x * (1.0 - s))


def spans(total, size):
    return [slice(first, first + size) for first in range(0, total, size)]


def bound_kernel(lat_ref, bnd_ref, lat_t_ref, bound_t_ref):
    lat_t = transposed(lat_ref[...])
    lat_t_ref[...] = lat_t
    bound_t_ref[...] = nn(lat_t, table(lat_ref.shape[0], bnd_ref[...])).astype(BF)


def mesh_kernel(
    lat_t_ref, before_ref, after_ref, feats_ref, w_ref, edges_ref,
    rows_ref, slope_ref, agg_ref, ext_t_ref, sum_ref,
):
    rows_dev = lat_t_ref.shape[1]
    rim = transposed(jnp.concatenate([before_ref[...], after_ref[...]], axis=0))
    ext_t_ref[:, :rows_dev] = lat_t_ref[...]
    ext_t_ref[:, rows_dev:] = rim
    w_t = jnp.concatenate([transposed(w_ref[0]), transposed(w_ref[1])], axis=1)
    w2_t = transposed(w_ref[2])
    for at in spans(edges_ref.shape[1], MESH_SPAN):
        ids = edges_ref[0:1, at] - HB
        ids = jnp.where(ids < 0, ids + rows_dev + HB, jnp.where(ids < rows_dev, ids, ids + HB))
        rows_ref[:128, at] = nn(ext_t_ref[...], table(rows_dev + 2 * HB, ids)).astype(BF)
        hits = table(rows_dev, edges_ref[1:2, at])
        rows_ref[128:, at] = nn(lat_t_ref[...], hits).astype(BF)
        x = nn(w_t, rows_ref[:, at]) + nt(w2_t, feats_ref[at, :])
        message, slope = silu_parts(x)
        slope_ref[:, at] = slope
        part = nt(hits, message.astype(BF))
        if at.start:
            part = part + sum_ref[...]
        sum_ref[...] = part
    agg_ref[...] = sum_ref[...].astype(BF)


def main_kernel(
    counts_ref, core_ref, lat_ref, lat_t_ref, bound_t_ref, far0_ref, far1_ref, far2_ref,
    far3_ref, rows_ref, slope_m_ref, agg_ref, feats_ref, cot_ref, w_ref, edges_ref,
    contacts_ref, bnd_ref,
    new_ref, kept_ref, sent_ref, dm_ref, dc_ref, dn_ref,
    aggb_ref, slope_c_ref, both_ref, gw_ref, aggc_ref, dagg_t_ref, daggc_t_ref,
    *, scale,
):
    rows_dev = lat_ref.shape[0]
    bound_count = bnd_ref.shape[1]
    fars = (far0_ref, far1_ref, far2_ref, far3_ref)
    rounds = len(fars)
    round_rows = contacts_ref.shape[1] // rounds
    w_t = jnp.concatenate([transposed(w_ref[3]), transposed(w_ref[4])], axis=1)

    for r, at in enumerate(spans(contacts_ref.shape[1], round_rows)):
        place = lax.broadcasted_iota(jnp.int32, (1, round_rows), 1)
        live = (place < counts_ref[0, r]).astype(F32)
        hits = table(bound_count, contacts_ref[0:1, at])
        both_ref[:128, at] = nn(bound_t_ref[...], hits).astype(BF)
        both_ref[128:, at] = nn(
            fars[r][...], table(bound_count, contacts_ref[1:2, at])
        ).astype(BF)
        message, slope = silu_parts(nn(w_t, both_ref[:, at]))
        slope_c_ref[:, at] = slope * live
        part = nt(hits, (message * live).astype(BF))
        if r:
            part = part + aggb_ref[...]
        aggb_ref[...] = part

    bound_table = table(rows_dev, bnd_ref[...])
    aggc_ref[...] = nn(bound_table, aggb_ref[...].astype(BF)).astype(BF)
    for at in spans(rows_dev, NODE_SPAN):
        lat = lat_ref[at, :]
        cot = cot_ref[at, :]
        agg = agg_ref[at, :]
        aggc = aggc_ref[at, :]
        x = nn(lat, w_ref[5]) + nn(agg, w_ref[6]) + nn(aggc, w_ref[7])
        message, slope = silu_parts(x)
        hidden = message.astype(BF)
        new_ref[at, :] = (lat.astype(F32) + nn(hidden, w_ref[8])).astype(BF)
        d_node = (nt(cot, w_ref[8]) * slope).astype(BF)
        dn_ref[at, :] = d_node
        dagg_t_ref[:, at] = nt(w_ref[6], d_node).astype(BF)
        daggc_t_ref[:, at] = nt(w_ref[7], d_node).astype(BF)
        parts = [
            nn(lat_t_ref[:, at], d_node), tn(agg, d_node), tn(aggc, d_node), tn(hidden, cot)
        ]
        for k, part in enumerate(parts):
            where = slice(640 + 128 * k, 768 + 128 * k)
            gw_ref[where, :] = part + gw_ref[where, :] if at.start else part

    for at in spans(edges_ref.shape[1], MESH_SPAN):
        gathered = nn(dagg_t_ref[...], table(rows_dev, edges_ref[1:2, at]))
        d = (gathered * slope_m_ref[:, at]).astype(BF)
        dm_ref[:, at] = d
        pair = nt(rows_ref[:, at], d)
        own = nn(d, feats_ref[at, :])
        gw_ref[0:256, :] = pair + gw_ref[0:256, :] if at.start else pair
        gw_ref[256:384, :] = own + gw_ref[256:384, :] if at.start else own

    gw_ref[256:384, :] = gw_ref[256:384, :].T
    dbg_t = nn(daggc_t_ref[...], bound_table).astype(BF)
    for r, at in enumerate(spans(contacts_ref.shape[1], round_rows)):
        gathered = nn(dbg_t, table(bound_count, contacts_ref[0:1, at]))
        d = (gathered * slope_c_ref[:, at]).astype(BF)
        dc_ref[:, at] = d
        pair = nt(both_ref[:, at], d)
        gw_ref[384:640, :] = pair + gw_ref[384:640, :] if r else pair

    half = gw_ref.shape[0] // 2
    core = core_ref[0]
    kept_ref[...] = gw_ref[pl.ds(pl.multiple_of(core * half, 64), half), :] * scale
    sent = gw_ref[pl.ds(pl.multiple_of((1 - core) * half, 64), half), :] * scale
    sent_ref[...] = sent.astype(BF)


def contact_back_kernel(
    w_ref, contacts_ref, dc_ref, far0_ref, far1_ref, far2_ref, far3_ref, own_ref
):
    outs = (far0_ref, far1_ref, far2_ref, far3_ref)
    bound_count = own_ref.shape[0]
    for r, at in enumerate(spans(contacts_ref.shape[1], contacts_ref.shape[1] // len(outs))):
        d = dc_ref[:, at]
        part = nt(table(bound_count, contacts_ref[0:1, at]), d)
        own_ref[...] = part + own_ref[...] if r else part
        far = nt(table(bound_count, contacts_ref[1:2, at]), d)
        outs[r][...] = wide_nt(far, w_ref[4]).astype(BF)
    own_ref[...] = wide_nt(own_ref[...], w_ref[3])


def mesh_back_kernel(
    w_ref, edges_ref, dm_ref, dn_ref, cot_ref, grad_ref, low_ref, high_ref, send_ref, recv_ref
):
    rows_dev = cot_ref.shape[0]
    for at in spans(edges_ref.shape[1], MESH_SPAN):
        d = dm_ref[:, at]
        send = nt(table(rows_dev + 2 * HB, edges_ref[0:1, at]), d)
        recv = nt(table(rows_dev, edges_ref[1:2, at]), d)
        send_ref[...] = send + send_ref[...] if at.start else send
        recv_ref[...] = recv + recv_ref[...] if at.start else recv
    low_ref[...] = wide_nt(send_ref[:HB, :], w_ref[0]).astype(BF)
    high_ref[...] = wide_nt(send_ref[HB + rows_dev :, :], w_ref[0]).astype(BF)
    grad_ref[...] = (
        cot_ref[...].astype(F32)
        + nt(dn_ref[...], w_ref[5])
        + wide_nt(recv_ref[...], w_ref[1])
        + wide_nt(send_ref[HB : HB + rows_dev, :], w_ref[0])
    )


def last_kernel(
    part_ref, own_ref, in0_ref, in1_ref, in2_ref, in3_ref, prev_ref, next_ref, bnd_ref, out_ref
):
    rows_dev = part_ref.shape[0]
    total = own_ref[...]
    for ref in (in0_ref, in1_ref, in2_ref, in3_ref):
        total = total + ref[...].astype(F32)
    out_ref[...] = part_ref[...] + wide_nn(table(rows_dev, bnd_ref[...]), total)
    out_ref[:HB, :] += prev_ref[...].astype(F32)
    out_ref[rows_dev - HB :, :] += next_ref[...].astype(F32)


def call(kernel, outs, args, scratch=(), smem=0, flops=0, mib=32):
    spec = pl.BlockSpec(memory_space=pltpu.VMEM)
    return pl.pallas_call(
        kernel,
        out_shape=[jax.ShapeDtypeStruct(shape, kind) for shape, kind in outs],
        in_specs=[pl.BlockSpec(memory_space=pltpu.SMEM)] * smem + [spec] * (len(args) - smem),
        out_specs=[spec] * len(outs),
        scratch_shapes=[pltpu.VMEM(shape, kind) for shape, kind in scratch],
        compiler_params=pltpu.CompilerParams(vmem_limit_bytes=mib * MIB),
        cost_estimate=pl.CostEstimate(flops=flops, bytes_accessed=4000000, transcendentals=0),
    )(*args)


def exchanged(block, mask_x=0, mask_y=0, mask_z=0, mask_core=0):
    route = []
    for region in range(32):
        for panel in range(8):
            other_region = region ^ ((mask_x >> 1) << 4 | mask_z << 1 | mask_core)
            other_panel = panel ^ ((mask_x & 1) << 2 | mask_y)
            route.append((region * 8 + panel, other_region * 8 + other_panel))
    return lax.ppermute(block, ("region", "panel"), route)


def swapped(block, bit):
    size = lax.axis_size("region")
    return lax.ppermute(block, "region", [(i, i ^ (1 << bit)) for i in range(size)])


def shifted(array, by):
    length = lax.axis_size("panel")
    pairs = [(i, i + by) for i in range(length) if 0 <= i + by < length]
    return lax.ppermute(array, "panel", pairs)


def wide(block):
    return block.astype(F32)


def four_sum(block, name):
    one, two, three = [wide(exchanged(block, **{name: mask})) for mask in (1, 2, 3)]
    return ((wide(block) + one) + (two + three)).astype(BF)


def summed_over_y(kept, other, row_y):
    part = kept.shape[0] // 4
    block = (kept + wide(other)).astype(BF)
    pieces = [
        lax.dynamic_slice_in_dim(block, (row_y ^ mask) * part, part, 0) for mask in range(4)
    ]
    return pieces


def ordered_by_y(found, row_y):
    odd, high = row_y % 2 == 1, row_y >= 2
    low_pair = [jnp.where(odd, found[1], found[0]), jnp.where(odd, found[0], found[1])]
    high_pair = [jnp.where(odd, found[3], found[2]), jnp.where(odd, found[2], found[3])]
    ordered = [jnp.where(high, b, a) for a, b in zip(low_pair, high_pair)]
    ordered += [jnp.where(high, a, b) for a, b in zip(low_pair, high_pair)]
    return jnp.concatenate(ordered, axis=0)


def tie(*arrays):
    return lax.optimization_barrier(arrays)


def shards(
    latents, edge_feats, weights, cotangent, mesh_edges, boundary, contact_edges, contact_counts
):
    rows_dev, width = latents.shape
    bound_count = boundary.shape[0]
    rounds = contact_counts.shape[1]
    edge_count = mesh_edges.shape[1]
    contact_count = contact_edges.shape[1]
    bnd = boundary.reshape(1, bound_count)
    core = lax.axis_index("region") % 2
    row_y = lax.axis_index("panel") % 4
    scale = 1.0 / math.sqrt(rows_dev * lax.axis_size("region") * lax.axis_size("panel"))

    before = shifted(latents[rows_dev - HB :], 1)
    after = shifted(latents[:HB], -1)
    lat_t, bound_t = call(
        bound_kernel, [((width, rows_dev), BF), ((width, bound_count), BF)], [latents, bnd], mib=8
    )
    fars = [swapped(bound_t, r) for r in range(rounds)]
    rows, slope, agg = call(
        mesh_kernel,
        [((2 * width, edge_count), BF), ((width, edge_count), F32), ((rows_dev, width), BF)],
        [lat_t, before, after, edge_feats, weights, mesh_edges],
        [((width, rows_dev + 2 * HB), BF), ((rows_dev, width), F32)],
        flops=6 * 10**9,
    )
    new_rows, kept, sent, d_mesh, d_contact, d_node = call(
        functools.partial(main_kernel, scale=scale),
        [
            ((rows_dev, width), BF),
            ((9 * width // 2, width), F32),
            ((9 * width // 2, width), BF),
            ((width, edge_count), BF),
            ((width, contact_count), BF),
            ((rows_dev, width), BF),
        ],
        [contact_counts, core.reshape(1), latents, lat_t, bound_t, *fars, rows, slope, agg]
        + [edge_feats, cotangent, weights, mesh_edges, contact_edges, bnd],
        [
            ((bound_count, width), F32),
            ((width, contact_count), F32),
            ((2 * width, contact_count), BF),
            ((9 * width, width), F32),
            ((rows_dev, width), BF),
            ((width, rows_dev), BF),
            ((width, rows_dev), BF),
        ],
        smem=2,
        flops=8 * 10**9,
        mib=40,
    )
    other = exchanged(sent, mask_core=1)
    other, d_contact = tie(other, d_contact)
    pieces = summed_over_y(kept, other, row_y)
    *far_grads, own_grad = call(
        contact_back_kernel,
        [((bound_count, width), BF)] * rounds + [((bound_count, width), F32)],
        [weights, contact_edges, d_contact],
        flops=2 * 10**9,
    )
    one, two, three = [wide(exchanged(pieces[mask], mask_y=mask)) for mask in (1, 2, 3)]
    block = ((wide(pieces[0]) + one) + (two + three)).astype(BF)
    block, d_mesh, *far_grads = tie(block, d_mesh, *far_grads)
    part, low, high = call(
        mesh_back_kernel,
        [((rows_dev, width), F32), ((HB, width), BF), ((HB, width), BF)],
        [weights, mesh_edges, d_mesh, d_node, cotangent],
        [((rows_dev + 2 * HB, width), F32), ((rows_dev, width), F32)],
        flops=3 * 10**9,
    )
    block = four_sum(block, "mask_x")
    block, low, high, *far_grads = tie(block, low, high, *far_grads)
    incoming = [swapped(far_grads[r], r) for r in range(rounds)]
    block = four_sum(block, "mask_z")
    block, *incoming = tie(block, *incoming)
    from_prev = shifted(high, 1)
    from_next = shifted(low, -1)
    block = (wide(block) + wide(exchanged(block, mask_z=4))).astype(BF)
    block, from_prev, from_next = tie(block, from_prev, from_next)
    (grad_rows,) = call(
        last_kernel,
        [((rows_dev, width), F32)],
        [part, own_grad, *incoming, from_prev, from_next, bnd],
        flops=10**8,
        mib=8,
    )
    found = [block] + [exchanged(block, mask_y=mask) for mask in (1, 2, 3)]
    block = ordered_by_y(found, row_y)
    other = exchanged(block, mask_core=1)
    first = jnp.where(core == 1, other, block)
    second = jnp.where(core == 1, block, other)
    summed = wide(jnp.concatenate([first, second], axis=0)).reshape(9, width, width)
    return (new_rows, grad_rows, summed)


def solution(mesh):
    blocks = P(("region", "panel"), None)
    placed = (
        blocks,
        blocks,
        P(),
        blocks,
        P(None, ("region", "panel")),
        P(("region", "panel")),
        P(None, ("region", "panel")),
        blocks,
    )
    return jax.shard_map(
        shards, mesh=mesh, in_specs=placed, out_specs=(blocks, blocks, P()), check_vma=False
    )
```

```python
import functools
import math

import jax
import jax.numpy as jnp
from jax import lax
from jax.experimental import pallas as pl
from jax.experimental.pallas import tpu as pltpu
from jax.sharding import PartitionSpec as P

HB = 64
BF = jnp.bfloat16
F32 = jnp.float32
MESH_SPAN = 1536
NODE_SPAN = 512
MIB = 1024 * 1024


def nn(a, b):
    return lax.dot_general(a, b, (((1,), (0,)), ((), ())), preferred_element_type=F32)


def nt(a, b):
    return lax.dot_general(a, b, (((1,), (1,)), ((), ())), preferred_element_type=F32)


def tn(a, b):
    return lax.dot_general(a, b, (((0,), (0,)), ((), ())), preferred_element_type=F32)


def in_two(values):
    high = values.astype(BF)
    return high, (values - high.astype(F32)).astype(BF)


def wide_nt(a, b):
    high, low = in_two(a)
    return nt(high, b) + nt(low, b)


def wide_nn(a, b):
    high, low = in_two(b)
    return nn(a, high) + nn(a, low)


def identity():
    row = lax.broadcasted_iota(jnp.int32, (128, 128), 0)
    column = lax.broadcasted_iota(jnp.int32, (128, 128), 1)
    return (row == column).astype(BF)


def transposed(a):
    return nt(identity(), a).astype(BF)


def table(count, ids):
    rows = lax.broadcasted_iota(jnp.int32, (count, ids.shape[1]), 0)
    return (rows == ids).astype(BF)


def silu_parts(x):
    s = 0.5 * jnp.tanh(0.5 * x) + 0.5
    return x * s, s * (1.0 + x * (1.0 - s))


def spans(total, size):
    return [slice(first, first + size) for first in range(0, total, size)]


def fetched(pairs, sems):
    copies = [pltpu.make_async_copy(a, b, sems.at[k]) for k, (a, b) in enumerate(pairs)]
    for copy in copies:
        copy.start()
    return copies


def bound_kernel(lat_hbm, bnd_hbm, low_ref, high_ref, lat_t_ref, bound_t_ref, lat, bnd, sems):
    for copy in fetched([(lat_hbm, lat), (bnd_hbm, bnd)], sems):
        copy.wait()
    rows_dev = lat.shape[0]
    low_ref[...] = lat[:HB, :]
    high_ref[...] = lat[rows_dev - HB :, :]
    lat_t = transposed(lat[...])
    lat_t_ref[...] = lat_t
    bound_t_ref[...] = nn(lat_t, table(rows_dev, bnd[...])).astype(BF)


def mesh_kernel(
    lat_t_ref, before_ref, after_ref, edges_hbm, w_hbm, feats_hbm,
    rows_ref, slope_ref, agg_ref, ext_t_ref, sum_ref, edges, w, feats, sems,
):
    rows_dev = lat_t_ref.shape[1]
    copies = fetched([(edges_hbm, edges), (w_hbm.at[0:3], w), (feats_hbm, feats)], sems)
    rim = transposed(jnp.concatenate([before_ref[...], after_ref[...]], axis=0))
    ext_t_ref[:, :rows_dev] = lat_t_ref[...]
    ext_t_ref[:, rows_dev:] = rim
    copies[0].wait()
    for at in spans(edges.shape[1], MESH_SPAN):
        ids = edges[0:1, at] - HB
        ids = jnp.where(ids < 0, ids + rows_dev + HB, jnp.where(ids < rows_dev, ids, ids + HB))
        rows_ref[:128, at] = nn(ext_t_ref[...], table(rows_dev + 2 * HB, ids)).astype(BF)
        hits = table(rows_dev, edges[1:2, at])
        rows_ref[128:, at] = nn(lat_t_ref[...], hits).astype(BF)
        if at.start == 0:
            copies[1].wait()
            copies[2].wait()
            w_t = jnp.concatenate([transposed(w[0]), transposed(w[1])], axis=1)
            w2_t = transposed(w[2])
        x = nn(w_t, rows_ref[:, at]) + nt(w2_t, feats[at, :])
        message, slope = silu_parts(x)
        slope_ref[:, at] = slope
        part = nt(hits, message.astype(BF))
        if at.start:
            part = part + sum_ref[...]
        sum_ref[...] = part
    agg_ref[...] = sum_ref[...].astype(BF)


def main_kernel(
    counts_ref, core_ref, lat_ref, lat_t_ref, bound_t_ref, far0_ref, far1_ref, far2_ref,
    far3_ref, rows_ref, slope_m_ref, agg_ref, feats_ref, cot_ref, w_ref, edges_ref,
    contacts_ref, bnd_ref,
    new_ref, kept_ref, sent_ref, dm_ref, dc_ref, dn_ref,
    aggb_ref, slope_c_ref, both_ref, gw_ref, aggc_ref, dagg_t_ref, daggc_t_ref,
    *, scale,
):
    rows_dev = lat_ref.shape[0]
    bound_count = bnd_ref.shape[1]
    fars = (far0_ref, far1_ref, far2_ref, far3_ref)
    rounds = len(fars)
    round_rows = contacts_ref.shape[1] // rounds
    w_t = jnp.concatenate([transposed(w_ref[3]), transposed(w_ref[4])], axis=1)

    for r, at in enumerate(spans(contacts_ref.shape[1], round_rows)):
        place = lax.broadcasted_iota(jnp.int32, (1, round_rows), 1)
        live = (place < counts_ref[0, r]).astype(F32)
        hits = table(bound_count, contacts_ref[0:1, at])
        both_ref[:128, at] = nn(bound_t_ref[...], hits).astype(BF)
        both_ref[128:, at] = nn(
            fars[r][...], table(bound_count, contacts_ref[1:2, at])
        ).astype(BF)
        message, slope = silu_parts(nn(w_t, both_ref[:, at]))
        slope_c_ref[:, at] = slope * live
        part = nt(hits, (message * live).astype(BF))
        if r:
            part = part + aggb_ref[...]
        aggb_ref[...] = part

    bound_table = table(rows_dev, bnd_ref[...])
    aggc_ref[...] = nn(bound_table, aggb_ref[...].astype(BF)).astype(BF)
    for at in spans(rows_dev, NODE_SPAN):
        lat = lat_ref[at, :]
        cot = cot_ref[at, :]
        agg = agg_ref[at, :]
        aggc = aggc_ref[at, :]
        x = nn(lat, w_ref[5]) + nn(agg, w_ref[6]) + nn(aggc, w_ref[7])
        message, slope = silu_parts(x)
        hidden = message.astype(BF)
        new_ref[at, :] = (lat.astype(F32) + nn(hidden, w_ref[8])).astype(BF)
        d_node = (nt(cot, w_ref[8]) * slope).astype(BF)
        dn_ref[at, :] = d_node
        dagg_t_ref[:, at] = nt(w_ref[6], d_node).astype(BF)
        daggc_t_ref[:, at] = nt(w_ref[7], d_node).astype(BF)
        parts = [
            nn(lat_t_ref[:, at], d_node), tn(agg, d_node), tn(aggc, d_node), tn(hidden, cot)
        ]
        for k, part in enumerate(parts):
            where = slice(640 + 128 * k, 768 + 128 * k)
            gw_ref[where, :] = part + gw_ref[where, :] if at.start else part

    for at in spans(edges_ref.shape[1], MESH_SPAN):
        gathered = nn(dagg_t_ref[...], table(rows_dev, edges_ref[1:2, at]))
        d = (gathered * slope_m_ref[:, at]).astype(BF)
        dm_ref[:, at] = d
        pair = nt(rows_ref[:, at], d)
        own = nn(d, feats_ref[at, :])
        gw_ref[0:256, :] = pair + gw_ref[0:256, :] if at.start else pair
        gw_ref[256:384, :] = own + gw_ref[256:384, :] if at.start else own

    gw_ref[256:384, :] = gw_ref[256:384, :].T
    dbg_t = nn(daggc_t_ref[...], bound_table).astype(BF)
    for r, at in enumerate(spans(contacts_ref.shape[1], round_rows)):
        gathered = nn(dbg_t, table(bound_count, contacts_ref[0:1, at]))
        d = (gathered * slope_c_ref[:, at]).astype(BF)
        dc_ref[:, at] = d
        pair = nt(both_ref[:, at], d)
        gw_ref[384:640, :] = pair + gw_ref[384:640, :] if r else pair

    half = gw_ref.shape[0] // 2
    core = core_ref[0]
    kept_ref[...] = gw_ref[pl.ds(pl.multiple_of(core * half, 64), half), :] * scale
    sent = gw_ref[pl.ds(pl.multiple_of((1 - core) * half, 64), half), :] * scale
    sent_ref[...] = sent.astype(BF)


def contact_back_kernel(
    w_ref, contacts_ref, dc_ref, far0_ref, far1_ref, far2_ref, far3_ref, own_ref
):
    outs = (far0_ref, far1_ref, far2_ref, far3_ref)
    bound_count = own_ref.shape[0]
    for r, at in enumerate(spans(contacts_ref.shape[1], contacts_ref.shape[1] // len(outs))):
        d = dc_ref[:, at]
        part = nt(table(bound_count, contacts_ref[0:1, at]), d)
        own_ref[...] = part + own_ref[...] if r else part
        far = nt(table(bound_count, contacts_ref[1:2, at]), d)
        outs[r][...] = wide_nt(far, w_ref[4]).astype(BF)
    own_ref[...] = wide_nt(own_ref[...], w_ref[3])


def send_back_kernel(w_ref, edges_ref, dm_ref, part_ref, low_ref, high_ref, send_ref):
    rows_dev = part_ref.shape[0]
    for at in spans(edges_ref.shape[1], MESH_SPAN):
        send = nt(table(rows_dev + 2 * HB, edges_ref[0:1, at]), dm_ref[:, at])
        send_ref[...] = send + send_ref[...] if at.start else send
    low_ref[...] = wide_nt(send_ref[:HB, :], w_ref[0]).astype(BF)
    high_ref[...] = wide_nt(send_ref[HB + rows_dev :, :], w_ref[0]).astype(BF)
    part_ref[...] = wide_nt(send_ref[HB : HB + rows_dev, :], w_ref[0])


def recv_back_kernel(w_ref, edges_ref, dm_ref, dn_ref, cot_ref, part_ref, grad_ref, recv_ref):
    rows_dev = cot_ref.shape[0]
    for at in spans(edges_ref.shape[1], MESH_SPAN):
        recv = nt(table(rows_dev, edges_ref[1:2, at]), dm_ref[:, at])
        recv_ref[...] = recv + recv_ref[...] if at.start else recv
    grad_ref[...] = (
        cot_ref[...].astype(F32)
        + nt(dn_ref[...], w_ref[5])
        + wide_nt(recv_ref[...], w_ref[1])
        + part_ref[...]
    )


def last_kernel(
    part_ref, own_ref, in0_ref, in1_ref, in2_ref, in3_ref, prev_ref, next_ref, bnd_ref, out_ref
):
    rows_dev = part_ref.shape[0]
    total = own_ref[...]
    for ref in (in0_ref, in1_ref, in2_ref, in3_ref):
        total = total + ref[...].astype(F32)
    out_ref[...] = part_ref[...] + wide_nn(table(rows_dev, bnd_ref[...]), total)
    out_ref[:HB, :] += prev_ref[...].astype(F32)
    out_ref[rows_dev - HB :, :] += next_ref[...].astype(F32)


def call(kernel, outs, args, scratch=(), smem=0, hbm=0, flops=0, mib=32):
    spec = pl.BlockSpec(memory_space=pltpu.VMEM)
    plain = len(args) - smem - hbm
    in_specs = [pl.BlockSpec(memory_space=pltpu.SMEM)] * smem + [spec] * plain
    in_specs += [pl.BlockSpec(memory_space=pltpu.HBM)] * hbm
    scratch_shapes = [pltpu.VMEM(shape, kind) for shape, kind in scratch]
    if hbm:
        scratch_shapes.append(pltpu.SemaphoreType.DMA((hbm,)))
    return pl.pallas_call(
        kernel,
        out_shape=[jax.ShapeDtypeStruct(shape, kind) for shape, kind in outs],
        in_specs=in_specs,
        out_specs=[spec] * len(outs),
        scratch_shapes=scratch_shapes,
        compiler_params=pltpu.CompilerParams(vmem_limit_bytes=mib * MIB),
        cost_estimate=pl.CostEstimate(flops=flops, bytes_accessed=4000000, transcendentals=0),
    )(*args)


def exchanged(block, mask_x=0, mask_y=0, mask_z=0, mask_core=0):
    route = []
    for region in range(32):
        for panel in range(8):
            other_region = region ^ ((mask_x >> 1) << 4 | mask_z << 1 | mask_core)
            other_panel = panel ^ ((mask_x & 1) << 2 | mask_y)
            route.append((region * 8 + panel, other_region * 8 + other_panel))
    return lax.ppermute(block, ("region", "panel"), route)


def swapped(block, bit):
    size = lax.axis_size("region")
    return lax.ppermute(block, "region", [(i, i ^ (1 << bit)) for i in range(size)])


def shifted(array, by):
    length = lax.axis_size("panel")
    pairs = [(i, i + by) for i in range(length) if 0 <= i + by < length]
    return lax.ppermute(array, "panel", pairs)


def wide(block):
    return block.astype(F32)


def half_of(block, which):
    size = block.shape[0] // 2
    return lax.dynamic_slice_in_dim(block, which * size, size, 0)


def joined(own, other, which):
    first = jnp.where(which == 0, own, other)
    second = jnp.where(which == 0, other, own)
    return jnp.concatenate([first, second], axis=0)


def tie(*arrays):
    return lax.optimization_barrier(arrays)


def shards(
    latents, edge_feats, weights, cotangent, mesh_edges, boundary, contact_edges, contact_counts
):
    rows_dev, width = latents.shape
    bound_count = boundary.shape[0]
    rounds = contact_counts.shape[1]
    edge_count = mesh_edges.shape[1]
    contact_count = contact_edges.shape[1]
    bnd = boundary.reshape(1, bound_count)
    core = lax.axis_index("region") % 2
    row_y = lax.axis_index("panel") % 4
    scale = 1.0 / math.sqrt(rows_dev * lax.axis_size("region") * lax.axis_size("panel"))

    low_rows, high_rows, lat_t, bound_t = call(
        bound_kernel,
        [((HB, width), BF), ((HB, width), BF), ((width, rows_dev), BF), ((width, bound_count), BF)],
        [latents, bnd],
        [((rows_dev, width), BF), ((1, bound_count), jnp.int32)],
        hbm=2,
        mib=8,
    )
    before = shifted(high_rows, 1)
    after = shifted(low_rows, -1)
    fars = [swapped(bound_t, r) for r in range(rounds)]
    rows, slope, agg = call(
        mesh_kernel,
        [((2 * width, edge_count), BF), ((width, edge_count), F32), ((rows_dev, width), BF)],
        [lat_t, before, after, mesh_edges, weights, edge_feats],
        [
            ((width, rows_dev + 2 * HB), BF),
            ((rows_dev, width), F32),
            ((2, edge_count), jnp.int32),
            ((3, width, width), BF),
            ((edge_count, width), BF),
        ],
        hbm=3,
        flops=6 * 10**9,
        mib=20,
    )
    new_rows, kept, sent, d_mesh, d_contact, d_node = call(
        functools.partial(main_kernel, scale=scale),
        [
            ((rows_dev, width), BF),
            ((9 * width // 2, width), F32),
            ((9 * width // 2, width), BF),
            ((width, edge_count), BF),
            ((width, contact_count), BF),
            ((rows_dev, width), BF),
        ],
        [contact_counts, core.reshape(1), latents, lat_t, bound_t, *fars, rows, slope, agg]
        + [edge_feats, cotangent, weights, mesh_edges, contact_edges, bnd],
        [
            ((bound_count, width), F32),
            ((width, contact_count), F32),
            ((2 * width, contact_count), BF),
            ((9 * width, width), F32),
            ((rows_dev, width), BF),
            ((width, rows_dev), BF),
            ((width, rows_dev), BF),
        ],
        smem=2,
        flops=8 * 10**9,
        mib=26,
    )
    other = exchanged(sent, mask_core=1)
    other, d_contact = tie(other, d_contact)
    block = kept + wide(other)
    half, quarter = (row_y ^ (row_y >> 1)) & 1, row_y >> 1
    other = exchanged(half_of(block, 1 - half).astype(BF), mask_y=1)
    *far_grads, own_grad = call(
        contact_back_kernel,
        [((bound_count, width), BF)] * rounds + [((bound_count, width), F32)],
        [weights, contact_edges, d_contact],
        flops=2 * 10**9,
        mib=16,
    )
    other, *far_grads = tie(other, *far_grads)
    block = half_of(block, half) + wide(other)
    other = exchanged(half_of(block, 1 - quarter).astype(BF), mask_y=3)
    in_zero = exchanged(far_grads[0], mask_core=1)
    other, in_zero, d_mesh = tie(other, in_zero, d_mesh)
    block = (half_of(block, quarter) + wide(other)).astype(BF)

    size = block.shape[0]
    other = exchanged(jnp.concatenate([block, far_grads[1]], axis=0), mask_z=1)
    part, low, high = call(
        send_back_kernel,
        [((rows_dev, width), F32), ((HB, width), BF), ((HB, width), BF)],
        [weights, mesh_edges, d_mesh],
        [((rows_dev + 2 * HB, width), F32)],
        flops=2 * 10**9,
        mib=16,
    )
    other, part, low, high = tie(other, part, low, high)
    in_one = other[size:]
    block = (wide(block) + wide(other[:size])).astype(BF)
    other = exchanged(jnp.concatenate([block, far_grads[2], far_grads[3]], axis=0), mask_z=2)
    (part,) = call(
        recv_back_kernel,
        [((rows_dev, width), F32)],
        [weights, mesh_edges, d_mesh, d_node, cotangent, part],
        [((rows_dev, width), F32)],
        flops=2 * 10**9,
        mib=16,
    )
    other, part = tie(other, part)
    in_two = other[size : size + bound_count]
    block = (wide(block) + wide(other[:size])).astype(BF)
    other = exchanged(jnp.concatenate([block, other[size + bound_count :]], axis=0), mask_z=6)
    in_three = other[size:]
    block = wide(block) + wide(other[:size])

    rim = wide(jnp.where(row_y == 0, low, high))
    other = exchanged(jnp.concatenate([block, rim], axis=0), mask_x=1)
    rim = other[size:].astype(BF)
    block = block + other[:size]
    block = (block + exchanged(block, mask_x=3)).astype(BF)
    rim = jnp.where(row_y == 1, high, jnp.where(row_y == 2, low, rim))
    other = exchanged(jnp.concatenate([block, rim], axis=0), mask_y=3)
    rim_three = other[size:]
    block = joined(block, other[:size], quarter)
    rim = jnp.where(row_y % 2 == 0, high, low)
    other = exchanged(jnp.concatenate([block, rim], axis=0), mask_y=1)
    rim_one = other[2 * size :]
    panel = lax.axis_index("panel")
    nothing = jnp.zeros_like(rim)
    from_prev = jnp.where(row_y % 2 == 0, rim_three, rim_one)
    from_prev = jnp.where(panel == 0, nothing, from_prev)
    from_next = jnp.where(row_y % 2 == 0, rim_one, rim_three)
    from_next = jnp.where(panel == lax.axis_size("panel") - 1, nothing, from_next)
    block = joined(block, other[: 2 * size], half)
    other = exchanged(block, mask_core=1)
    (grad_rows,) = call(
        last_kernel,
        [((rows_dev, width), F32)],
        [part, own_grad, in_zero, in_one, in_two, in_three, from_prev, from_next, bnd],
        flops=10**8,
        mib=8,
    )
    block = joined(block, other, core)
    return (new_rows, grad_rows, wide(block).reshape(9, width, width))


def solution(mesh):
    blocks = P(("region", "panel"), None)
    placed = (
        blocks,
        blocks,
        P(),
        blocks,
        P(None, ("region", "panel")),
        P(("region", "panel")),
        P(None, ("region", "panel")),
        blocks,
    )
    return jax.shard_map(
        shards, mesh=mesh, in_specs=placed, out_specs=(blocks, blocks, P()), check_vma=False
    )
```

```python
import functools
import math

import jax
import jax.numpy as jnp
from jax import lax
from jax.experimental import pallas as pl
from jax.experimental.pallas import tpu as pltpu
from jax.sharding import PartitionSpec as P

HB = 64
BF = jnp.bfloat16
F32 = jnp.float32
MESH_SPAN = 1536
NODE_SPAN = 512
MIB = 1024 * 1024


def nn(a, b):
    return lax.dot_general(a, b, (((1,), (0,)), ((), ())), preferred_element_type=F32)


def nt(a, b):
    return lax.dot_general(a, b, (((1,), (1,)), ((), ())), preferred_element_type=F32)


def tn(a, b):
    return lax.dot_general(a, b, (((0,), (0,)), ((), ())), preferred_element_type=F32)


def in_two(values):
    high = values.astype(BF)
    return high, (values - high.astype(F32)).astype(BF)


def wide_nt(a, b):
    high, low = in_two(a)
    return nt(high, b) + nt(low, b)


def wide_nn(a, b):
    high, low = in_two(b)
    return nn(a, high) + nn(a, low)


def identity():
    row = lax.broadcasted_iota(jnp.int32, (128, 128), 0)
    column = lax.broadcasted_iota(jnp.int32, (128, 128), 1)
    return (row == column).astype(BF)


def transposed(a):
    return nt(identity(), a).astype(BF)


def table(count, ids):
    rows = lax.broadcasted_iota(jnp.int32, (count, ids.shape[1]), 0)
    return (rows == ids).astype(BF)


def silu_parts(x):
    s = 0.5 * jnp.tanh(0.5 * x) + 0.5
    return x * s, s * (1.0 + x * (1.0 - s))


def spans(total, size):
    return [slice(first, first + size) for first in range(0, total, size)]


def fetched(pairs, sems):
    copies = [pltpu.make_async_copy(a, b, sems.at[k]) for k, (a, b) in enumerate(pairs)]
    for copy in copies:
        copy.start()
    return copies


def bound_kernel(lat_hbm, bnd_hbm, low_ref, high_ref, lat_t_ref, bound_t_ref, lat, bnd, sems):
    for copy in fetched([(lat_hbm, lat), (bnd_hbm, bnd)], sems):
        copy.wait()
    rows_dev = lat.shape[0]
    low_ref[...] = lat[:HB, :]
    high_ref[...] = lat[rows_dev - HB :, :]
    lat_t = transposed(lat[...])
    lat_t_ref[...] = lat_t
    bound_t_ref[...] = nn(lat_t, table(rows_dev, bnd[...])).astype(BF)


def mesh_kernel(
    lat_t_ref, before_ref, after_ref, edges_hbm, w_hbm, feats_hbm,
    rows_ref, slope_ref, agg_ref, ext_t_ref, sum_ref, edges, w, feats, sems,
):
    rows_dev = lat_t_ref.shape[1]
    copies = fetched([(edges_hbm, edges), (w_hbm.at[0:3], w), (feats_hbm, feats)], sems)
    rim = transposed(jnp.concatenate([before_ref[...], after_ref[...]], axis=0))
    ext_t_ref[:, :rows_dev] = lat_t_ref[...]
    ext_t_ref[:, rows_dev:] = rim
    copies[0].wait()
    for at in spans(edges.shape[1], MESH_SPAN):
        ids = edges[0:1, at] - HB
        ids = jnp.where(ids < 0, ids + rows_dev + HB, jnp.where(ids < rows_dev, ids, ids + HB))
        rows_ref[:128, at] = nn(ext_t_ref[...], table(rows_dev + 2 * HB, ids)).astype(BF)
        hits = table(rows_dev, edges[1:2, at])
        rows_ref[128:, at] = nn(lat_t_ref[...], hits).astype(BF)
        if at.start == 0:
            copies[1].wait()
            copies[2].wait()
            w_t = jnp.concatenate([transposed(w[0]), transposed(w[1])], axis=1)
            w2_t = transposed(w[2])
        x = nn(w_t, rows_ref[:, at]) + nt(w2_t, feats[at, :])
        message, slope = silu_parts(x)
        slope_ref[:, at] = slope
        part = nt(hits, message.astype(BF))
        if at.start:
            part = part + sum_ref[...]
        sum_ref[...] = part
    agg_ref[...] = sum_ref[...].astype(BF)


def main_kernel(
    counts_ref, core_ref, lat_ref, lat_t_ref, bound_t_ref, far0_ref, far1_ref, far2_ref,
    far3_ref, rows_ref, slope_m_ref, agg_ref, feats_ref, cot_ref, w_ref, edges_ref,
    contacts_ref, bnd_ref,
    new_ref, kept_ref, sent_ref, dm_ref, dc_ref, dn_ref,
    aggb_ref, slope_c_ref, both_ref, gw_ref, aggc_ref, dagg_t_ref, daggc_t_ref,
    *, scale,
):
    rows_dev = lat_ref.shape[0]
    bound_count = bnd_ref.shape[1]
    fars = (far0_ref, far1_ref, far2_ref, far3_ref)
    rounds = len(fars)
    round_rows = contacts_ref.shape[1] // rounds
    w_t = jnp.concatenate([transposed(w_ref[3]), transposed(w_ref[4])], axis=1)

    for r, at in enumerate(spans(contacts_ref.shape[1], round_rows)):
        place = lax.broadcasted_iota(jnp.int32, (1, round_rows), 1)
        live = (place < counts_ref[0, r]).astype(F32)
        hits = table(bound_count, contacts_ref[0:1, at])
        both_ref[:128, at] = nn(bound_t_ref[...], hits).astype(BF)
        both_ref[128:, at] = nn(
            fars[r][...], table(bound_count, contacts_ref[1:2, at])
        ).astype(BF)
        message, slope = silu_parts(nn(w_t, both_ref[:, at]))
        slope_c_ref[:, at] = slope * live
        part = nt(hits, (message * live).astype(BF))
        if r:
            part = part + aggb_ref[...]
        aggb_ref[...] = part

    bound_table = table(rows_dev, bnd_ref[...])
    aggc_ref[...] = nn(bound_table, aggb_ref[...].astype(BF)).astype(BF)
    for at in spans(rows_dev, NODE_SPAN):
        lat = lat_ref[at, :]
        cot = cot_ref[at, :]
        agg = agg_ref[at, :]
        aggc = aggc_ref[at, :]
        x = nn(lat, w_ref[5]) + nn(agg, w_ref[6]) + nn(aggc, w_ref[7])
        message, slope = silu_parts(x)
        hidden = message.astype(BF)
        new_ref[at, :] = (lat.astype(F32) + nn(hidden, w_ref[8])).astype(BF)
        d_node = (nt(cot, w_ref[8]) * slope).astype(BF)
        dn_ref[at, :] = d_node
        dagg_t_ref[:, at] = nt(w_ref[6], d_node).astype(BF)
        daggc_t_ref[:, at] = nt(w_ref[7], d_node).astype(BF)
        parts = [
            nn(lat_t_ref[:, at], d_node), tn(agg, d_node), tn(aggc, d_node), tn(hidden, cot)
        ]
        for k, part in enumerate(parts):
            where = slice(640 + 128 * k, 768 + 128 * k)
            gw_ref[where, :] = part + gw_ref[where, :] if at.start else part

    for at in spans(edges_ref.shape[1], MESH_SPAN):
        gathered = nn(dagg_t_ref[...], table(rows_dev, edges_ref[1:2, at]))
        d = (gathered * slope_m_ref[:, at]).astype(BF)
        dm_ref[:, at] = d
        pair = nt(rows_ref[:, at], d)
        own = nn(d, feats_ref[at, :])
        gw_ref[0:256, :] = pair + gw_ref[0:256, :] if at.start else pair
        gw_ref[256:384, :] = own + gw_ref[256:384, :] if at.start else own

    gw_ref[256:384, :] = gw_ref[256:384, :].T
    dbg_t = nn(daggc_t_ref[...], bound_table).astype(BF)
    for r, at in enumerate(spans(contacts_ref.shape[1], round_rows)):
        gathered = nn(dbg_t, table(bound_count, contacts_ref[0:1, at]))
        d = (gathered * slope_c_ref[:, at]).astype(BF)
        dc_ref[:, at] = d
        pair = nt(both_ref[:, at], d)
        gw_ref[384:640, :] = pair + gw_ref[384:640, :] if r else pair

    half = gw_ref.shape[0] // 2
    core = core_ref[0]
    kept_ref[...] = gw_ref[pl.ds(pl.multiple_of(core * half, 64), half), :] * scale
    sent = gw_ref[pl.ds(pl.multiple_of((1 - core) * half, 64), half), :] * scale
    sent_ref[...] = sent.astype(BF)


def contact_back_kernel(
    w_ref, contacts_ref, dc_ref, far0_ref, far1_ref, far2_ref, far3_ref, own_ref
):
    outs = (far0_ref, far1_ref, far2_ref, far3_ref)
    bound_count = own_ref.shape[0]
    for r, at in enumerate(spans(contacts_ref.shape[1], contacts_ref.shape[1] // len(outs))):
        d = dc_ref[:, at]
        part = nt(table(bound_count, contacts_ref[0:1, at]), d)
        own_ref[...] = part + own_ref[...] if r else part
        far = nt(table(bound_count, contacts_ref[1:2, at]), d)
        outs[r][...] = wide_nt(far, w_ref[4]).astype(BF)
    own_ref[...] = wide_nt(own_ref[...], w_ref[3])


def send_back_kernel(w_ref, edges_ref, dm_ref, part_ref, low_ref, high_ref, send_ref):
    rows_dev = part_ref.shape[0]
    for at in spans(edges_ref.shape[1], MESH_SPAN):
        send = nt(table(rows_dev + 2 * HB, edges_ref[0:1, at]), dm_ref[:, at])
        send_ref[...] = send + send_ref[...] if at.start else send
    low_ref[...] = wide_nt(send_ref[:HB, :], w_ref[0]).astype(BF)
    high_ref[...] = wide_nt(send_ref[HB + rows_dev :, :], w_ref[0]).astype(BF)
    part_ref[...] = wide_nt(send_ref[HB : HB + rows_dev, :], w_ref[0])


def recv_back_kernel(w_ref, edges_ref, dm_ref, dn_ref, cot_ref, part_ref, grad_ref, recv_ref):
    rows_dev = cot_ref.shape[0]
    for at in spans(edges_ref.shape[1], MESH_SPAN):
        recv = nt(table(rows_dev, edges_ref[1:2, at]), dm_ref[:, at])
        recv_ref[...] = recv + recv_ref[...] if at.start else recv
    grad_ref[...] = (
        cot_ref[...].astype(F32)
        + nt(dn_ref[...], w_ref[5])
        + wide_nt(recv_ref[...], w_ref[1])
        + part_ref[...]
    )


def last_kernel(
    part_ref, own_ref, in0_ref, in1_ref, in2_ref, in3_ref, prev_ref, next_ref, bnd_ref, out_ref
):
    rows_dev = part_ref.shape[0]
    total = own_ref[...]
    for ref in (in0_ref, in1_ref, in2_ref, in3_ref):
        total = total + ref[...].astype(F32)
    out_ref[...] = part_ref[...] + wide_nn(table(rows_dev, bnd_ref[...]), total)
    out_ref[:HB, :] += prev_ref[...].astype(F32)
    out_ref[rows_dev - HB :, :] += next_ref[...].astype(F32)


def call(kernel, outs, args, scratch=(), smem=0, hbm=0, flops=0, mib=32):
    spec = pl.BlockSpec(memory_space=pltpu.VMEM)
    plain = len(args) - smem - hbm
    in_specs = [pl.BlockSpec(memory_space=pltpu.SMEM)] * smem + [spec] * plain
    in_specs += [pl.BlockSpec(memory_space=pltpu.HBM)] * hbm
    scratch_shapes = [pltpu.VMEM(shape, kind) for shape, kind in scratch]
    if hbm:
        scratch_shapes.append(pltpu.SemaphoreType.DMA((hbm,)))
    return pl.pallas_call(
        kernel,
        out_shape=[jax.ShapeDtypeStruct(shape, kind) for shape, kind in outs],
        in_specs=in_specs,
        out_specs=[spec] * len(outs),
        scratch_shapes=scratch_shapes,
        compiler_params=pltpu.CompilerParams(vmem_limit_bytes=mib * MIB),
        cost_estimate=pl.CostEstimate(flops=flops, bytes_accessed=4000000, transcendentals=0),
    )(*args)


def exchanged(block, mask_x=0, mask_y=0, mask_z=0, mask_core=0):
    route = []
    for region in range(32):
        for panel in range(8):
            other_region = region ^ ((mask_x >> 1) << 4 | mask_z << 1 | mask_core)
            other_panel = panel ^ ((mask_x & 1) << 2 | mask_y)
            route.append((region * 8 + panel, other_region * 8 + other_panel))
    return lax.ppermute(block, ("region", "panel"), route)


def swapped(block, bit):
    size = lax.axis_size("region")
    return lax.ppermute(block, "region", [(i, i ^ (1 << bit)) for i in range(size)])


def shifted(array, by):
    length = lax.axis_size("panel")
    pairs = [(i, i + by) for i in range(length) if 0 <= i + by < length]
    return lax.ppermute(array, "panel", pairs)


def wide(block):
    return block.astype(F32)


def ordered_by_y(found, row_y):
    odd, high = row_y % 2 == 1, row_y >= 2
    low_pair = [jnp.where(odd, found[1], found[0]), jnp.where(odd, found[0], found[1])]
    high_pair = [jnp.where(odd, found[3], found[2]), jnp.where(odd, found[2], found[3])]
    ordered = [jnp.where(high, b, a) for a, b in zip(low_pair, high_pair)]
    ordered += [jnp.where(high, a, b) for a, b in zip(low_pair, high_pair)]
    return jnp.concatenate(ordered, axis=0)


def joined(own, other, which):
    first = jnp.where(which == 0, own, other)
    second = jnp.where(which == 0, other, own)
    return jnp.concatenate([first, second], axis=0)


def tie(*arrays):
    return lax.optimization_barrier(arrays)


def shards(
    latents, edge_feats, weights, cotangent, mesh_edges, boundary, contact_edges, contact_counts
):
    rows_dev, width = latents.shape
    bound_count = boundary.shape[0]
    rounds = contact_counts.shape[1]
    edge_count = mesh_edges.shape[1]
    contact_count = contact_edges.shape[1]
    bnd = boundary.reshape(1, bound_count)
    core = lax.axis_index("region") % 2
    row_y = lax.axis_index("panel") % 4
    scale = 1.0 / math.sqrt(rows_dev * lax.axis_size("region") * lax.axis_size("panel"))

    low_rows, high_rows, lat_t, bound_t = call(
        bound_kernel,
        [((HB, width), BF), ((HB, width), BF), ((width, rows_dev), BF), ((width, bound_count), BF)],
        [latents, bnd],
        [((rows_dev, width), BF), ((1, bound_count), jnp.int32)],
        hbm=2,
        mib=8,
    )
    far_two = exchanged(bound_t, mask_z=2)
    before = shifted(high_rows, 1)
    after = shifted(low_rows, -1)
    far_one = exchanged(bound_t, mask_z=1)
    far_zero = exchanged(bound_t, mask_core=1)
    far_two, before, after = tie(far_two, before, after)
    far_three = exchanged(far_two, mask_z=6)
    fars = [far_zero, far_one, far_two, far_three]
    rows, slope, agg = call(
        mesh_kernel,
        [((2 * width, edge_count), BF), ((width, edge_count), F32), ((rows_dev, width), BF)],
        [lat_t, before, after, mesh_edges, weights, edge_feats],
        [
            ((width, rows_dev + 2 * HB), BF),
            ((rows_dev, width), F32),
            ((2, edge_count), jnp.int32),
            ((3, width, width), BF),
            ((edge_count, width), BF),
        ],
        hbm=3,
        flops=6 * 10**9,
        mib=20,
    )
    new_rows, kept, sent, d_mesh, d_contact, d_node = call(
        functools.partial(main_kernel, scale=scale),
        [
            ((rows_dev, width), BF),
            ((9 * width // 2, width), F32),
            ((9 * width // 2, width), BF),
            ((width, edge_count), BF),
            ((width, contact_count), BF),
            ((rows_dev, width), BF),
        ],
        [contact_counts, core.reshape(1), latents, lat_t, bound_t, *fars, rows, slope, agg]
        + [edge_feats, cotangent, weights, mesh_edges, contact_edges, bnd],
        [
            ((bound_count, width), F32),
            ((width, contact_count), F32),
            ((2 * width, contact_count), BF),
            ((9 * width, width), F32),
            ((rows_dev, width), BF),
            ((width, rows_dev), BF),
            ((width, rows_dev), BF),
        ],
        smem=2,
        flops=8 * 10**9,
        mib=26,
    )
    other = exchanged(sent, mask_core=1)
    *far_grads, own_grad = call(
        contact_back_kernel,
        [((bound_count, width), BF)] * rounds + [((bound_count, width), F32)],
        [weights, contact_edges, d_contact],
        flops=2 * 10**9,
        mib=16,
    )
    other, *far_grads = tie(other, *far_grads)
    block = kept + wide(other)
    size = block.shape[0] // 4
    pieces = [
        lax.dynamic_slice_in_dim(block, (row_y ^ mask) * size, size, 0) for mask in range(4)
    ]
    one, two, three = [exchanged(pieces[mask].astype(BF), mask_y=mask) for mask in (1, 2, 3)]
    in_one = exchanged(far_grads[1], mask_z=1)
    pair = exchanged(jnp.concatenate(far_grads[2:], axis=0), mask_z=2)
    one, two, three, d_mesh = tie(one, two, three, d_mesh)
    block = ((pieces[0] + wide(one)) + (wide(two) + wide(three))).astype(BF)

    one, two, three = [exchanged(block, mask_x=mask) for mask in (1, 2, 3)]
    part, low, high = call(
        send_back_kernel,
        [((rows_dev, width), F32), ((HB, width), BF), ((HB, width), BF)],
        [weights, mesh_edges, d_mesh],
        [((rows_dev + 2 * HB, width), F32)],
        flops=2 * 10**9,
        mib=16,
    )
    one, two, three, part, low, high, in_one, pair = tie(
        one, two, three, part, low, high, in_one, pair
    )
    block = ((wide(block) + wide(one)) + (wide(two) + wide(three))).astype(BF)

    other = exchanged(block, mask_z=1)
    from_prev = shifted(high, 1)
    from_next = shifted(low, -1)
    other, part = tie(other, part)
    block = (wide(block) + wide(other)).astype(BF)
    other = exchanged(block, mask_z=2)
    (part,) = call(
        recv_back_kernel,
        [((rows_dev, width), F32)],
        [weights, mesh_edges, d_mesh, d_node, cotangent, part],
        [((rows_dev, width), F32)],
        flops=2 * 10**9,
        mib=16,
    )
    other, part, from_prev, from_next, pair = tie(other, part, from_prev, from_next, pair)
    block = (wide(block) + wide(other)).astype(BF)
    other = exchanged(block, mask_z=6)
    in_zero = exchanged(far_grads[0], mask_core=1)
    in_two = pair[:bound_count]
    in_three = exchanged(pair[bound_count:], mask_z=6)
    other, in_zero = tie(other, in_zero)
    block = (wide(block) + wide(other)).astype(BF)

    found = [exchanged(block, mask_y=mask) for mask in (1, 2, 3)]
    *found, in_three = tie(*found, in_three)
    block = ordered_by_y([block] + found, row_y)
    other = exchanged(block, mask_core=1)
    (grad_rows,) = call(
        last_kernel,
        [((rows_dev, width), F32)],
        [part, own_grad, in_zero, in_one, in_two, in_three, from_prev, from_next, bnd],
        flops=10**8,
        mib=8,
    )
    block = joined(block, other, core)
    return (new_rows, grad_rows, wide(block).reshape(9, width, width))


def solution(mesh):
    blocks = P(("region", "panel"), None)
    placed = (
        blocks,
        blocks,
        P(),
        blocks,
        P(None, ("region", "panel")),
        P(("region", "panel")),
        P(None, ("region", "panel")),
        blocks,
    )
    return jax.shard_map(
        shards, mesh=mesh, in_specs=placed, out_specs=(blocks, blocks, P()), check_vma=False
    )
```

```python
import functools
import math

import jax
import jax.numpy as jnp
from jax import lax
from jax.experimental import pallas as pl
from jax.experimental.pallas import tpu as pltpu
from jax.sharding import PartitionSpec as P

HB = 64
BF = jnp.bfloat16
F32 = jnp.float32
MESH_SPAN = 1536
NODE_SPAN = 512
MIB = 1024 * 1024


def nn(a, b):
    return lax.dot_general(a, b, (((1,), (0,)), ((), ())), preferred_element_type=F32)


def nt(a, b):
    return lax.dot_general(a, b, (((1,), (1,)), ((), ())), preferred_element_type=F32)


def tn(a, b):
    return lax.dot_general(a, b, (((0,), (0,)), ((), ())), preferred_element_type=F32)


def in_two(values):
    high = values.astype(BF)
    return high, (values - high.astype(F32)).astype(BF)


def wide_nt(a, b):
    high, low = in_two(a)
    return nt(high, b) + nt(low, b)


def wide_nn(a, b):
    high, low = in_two(b)
    return nn(a, high) + nn(a, low)


def identity():
    row = lax.broadcasted_iota(jnp.int32, (128, 128), 0)
    column = lax.broadcasted_iota(jnp.int32, (128, 128), 1)
    return (row == column).astype(BF)


def transposed(a):
    return nt(identity(), a).astype(BF)


def table(count, ids):
    rows = lax.broadcasted_iota(jnp.int32, (count, ids.shape[1]), 0)
    return (rows == ids).astype(BF)


def silu_parts(x):
    s = 0.5 * jnp.tanh(0.5 * x) + 0.5
    return x * s, s * (1.0 + x * (1.0 - s))


def spans(total, size):
    return [slice(first, first + size) for first in range(0, total, size)]


def fetched(pairs, sems):
    copies = [pltpu.make_async_copy(a, b, sems.at[k]) for k, (a, b) in enumerate(pairs)]
    for copy in copies:
        copy.start()
    return copies


def bound_kernel(lat_hbm, bnd_hbm, low_ref, high_ref, lat_t_ref, bound_t_ref, lat, bnd, sems):
    for copy in fetched([(lat_hbm, lat), (bnd_hbm, bnd)], sems):
        copy.wait()
    rows_dev = lat.shape[0]
    low_ref[...] = lat[:HB, :]
    high_ref[...] = lat[rows_dev - HB :, :]
    lat_t = transposed(lat[...])
    lat_t_ref[...] = lat_t
    bound_t_ref[...] = nn(lat_t, table(rows_dev, bnd[...])).astype(BF)


def gather_kernel(lat_t_ref, edges_ref, send_ref, recv_ref):
    rows_dev = lat_t_ref.shape[1]
    for at in spans(edges_ref.shape[1], MESH_SPAN):
        send_ref[:, at] = nn(lat_t_ref[...], table(rows_dev, edges_ref[0:1, at] - HB)).astype(BF)
        recv_ref[:, at] = nn(lat_t_ref[...], table(rows_dev, edges_ref[1:2, at])).astype(BF)


def mesh_kernel(
    before_ref, after_ref, own_ref, recv_ref, edges_ref, w_ref, feats_ref,
    send_ref, slope_ref, agg_ref, sum_ref,
):
    rows_dev = agg_ref.shape[0]
    rim_t = transposed(jnp.concatenate([before_ref[...], after_ref[...]], axis=0))
    w0_t, w1_t, w2_t = transposed(w_ref[0]), transposed(w_ref[1]), transposed(w_ref[2])
    for at in spans(edges_ref.shape[1], MESH_SPAN):
        ids = edges_ref[0:1, at]
        ids = jnp.where(ids < HB, ids, jnp.where(ids < HB + rows_dev, -1, ids - rows_dev))
        rim_rows = nn(rim_t, table(2 * HB, ids))
        send_ref[:, at] = (own_ref[:, at].astype(F32) + rim_rows).astype(BF)
        x = nn(w0_t, send_ref[:, at]) + nn(w1_t, recv_ref[:, at]) + nt(w2_t, feats_ref[at, :])
        message, slope = silu_parts(x)
        slope_ref[:, at] = slope
        part = nt(table(rows_dev, edges_ref[1:2, at]), message.astype(BF))
        if at.start:
            part = part + sum_ref[...]
        sum_ref[...] = part
    agg_ref[...] = sum_ref[...].astype(BF)


def main_kernel(
    counts_ref, core_ref, lat_ref, lat_t_ref, bound_t_ref, far0_ref, far1_ref, far2_ref,
    far3_ref, send_ref, recv_ref, slope_m_ref, agg_ref, feats_ref, cot_ref, w_ref, edges_ref,
    contacts_ref, bnd_ref,
    new_ref, kept_ref, sent_ref, dm_ref, dc_ref, dn_ref,
    aggb_ref, slope_c_ref, both_ref, gw_ref, aggc_ref, dagg_t_ref, daggc_t_ref,
    *, scale,
):
    rows_dev = lat_ref.shape[0]
    bound_count = bnd_ref.shape[1]
    fars = (far0_ref, far1_ref, far2_ref, far3_ref)
    rounds = len(fars)
    round_rows = contacts_ref.shape[1] // rounds
    w_t = jnp.concatenate([transposed(w_ref[3]), transposed(w_ref[4])], axis=1)

    for r, at in enumerate(spans(contacts_ref.shape[1], round_rows)):
        place = lax.broadcasted_iota(jnp.int32, (1, round_rows), 1)
        live = (place < counts_ref[0, r]).astype(F32)
        hits = table(bound_count, contacts_ref[0:1, at])
        both_ref[:128, at] = nn(bound_t_ref[...], hits).astype(BF)
        both_ref[128:, at] = nn(
            fars[r][...], table(bound_count, contacts_ref[1:2, at])
        ).astype(BF)
        message, slope = silu_parts(nn(w_t, both_ref[:, at]))
        slope_c_ref[:, at] = slope * live
        part = nt(hits, (message * live).astype(BF))
        if r:
            part = part + aggb_ref[...]
        aggb_ref[...] = part

    bound_table = table(rows_dev, bnd_ref[...])
    aggc_ref[...] = nn(bound_table, aggb_ref[...].astype(BF)).astype(BF)
    for at in spans(rows_dev, NODE_SPAN):
        lat = lat_ref[at, :]
        cot = cot_ref[at, :]
        agg = agg_ref[at, :]
        aggc = aggc_ref[at, :]
        x = nn(lat, w_ref[5]) + nn(agg, w_ref[6]) + nn(aggc, w_ref[7])
        message, slope = silu_parts(x)
        hidden = message.astype(BF)
        new_ref[at, :] = (lat.astype(F32) + nn(hidden, w_ref[8])).astype(BF)
        d_node = (nt(cot, w_ref[8]) * slope).astype(BF)
        dn_ref[at, :] = d_node
        dagg_t_ref[:, at] = nt(w_ref[6], d_node).astype(BF)
        daggc_t_ref[:, at] = nt(w_ref[7], d_node).astype(BF)
        parts = [
            nn(lat_t_ref[:, at], d_node), tn(agg, d_node), tn(aggc, d_node), tn(hidden, cot)
        ]
        for k, part in enumerate(parts):
            where = slice(640 + 128 * k, 768 + 128 * k)
            gw_ref[where, :] = part + gw_ref[where, :] if at.start else part

    for at in spans(edges_ref.shape[1], MESH_SPAN):
        gathered = nn(dagg_t_ref[...], table(rows_dev, edges_ref[1:2, at]))
        d = (gathered * slope_m_ref[:, at]).astype(BF)
        dm_ref[:, at] = d
        parts = [nt(send_ref[:, at], d), nt(recv_ref[:, at], d), nn(d, feats_ref[at, :])]
        for k, part in enumerate(parts):
            where = slice(128 * k, 128 * k + 128)
            gw_ref[where, :] = part + gw_ref[where, :] if at.start else part

    gw_ref[256:384, :] = gw_ref[256:384, :].T
    dbg_t = nn(daggc_t_ref[...], bound_table).astype(BF)
    for r, at in enumerate(spans(contacts_ref.shape[1], round_rows)):
        gathered = nn(dbg_t, table(bound_count, contacts_ref[0:1, at]))
        d = (gathered * slope_c_ref[:, at]).astype(BF)
        dc_ref[:, at] = d
        pair = nt(both_ref[:, at], d)
        gw_ref[384:640, :] = pair + gw_ref[384:640, :] if r else pair

    half = gw_ref.shape[0] // 2
    core = core_ref[0]
    kept_ref[...] = gw_ref[pl.ds(pl.multiple_of(core * half, 64), half), :] * scale
    sent = gw_ref[pl.ds(pl.multiple_of((1 - core) * half, 64), half), :] * scale
    sent_ref[...] = sent.astype(BF)


def contact_back_kernel(
    w_ref, contacts_ref, dc_ref, far0_ref, far1_ref, far2_ref, far3_ref, own_ref
):
    outs = (far0_ref, far1_ref, far2_ref, far3_ref)
    bound_count = own_ref.shape[0]
    for r, at in enumerate(spans(contacts_ref.shape[1], contacts_ref.shape[1] // len(outs))):
        d = dc_ref[:, at]
        part = nt(table(bound_count, contacts_ref[0:1, at]), d)
        own_ref[...] = part + own_ref[...] if r else part
        far = nt(table(bound_count, contacts_ref[1:2, at]), d)
        outs[r][...] = wide_nt(far, w_ref[4]).astype(BF)
    own_ref[...] = wide_nt(own_ref[...], w_ref[3])


def send_back_kernel(w_ref, edges_ref, dm_ref, part_ref, low_ref, high_ref, send_ref):
    rows_dev = part_ref.shape[0]
    for at in spans(edges_ref.shape[1], MESH_SPAN):
        send = nt(table(rows_dev + 2 * HB, edges_ref[0:1, at]), dm_ref[:, at])
        send_ref[...] = send + send_ref[...] if at.start else send
    low_ref[...] = wide_nt(send_ref[:HB, :], w_ref[0]).astype(BF)
    high_ref[...] = wide_nt(send_ref[HB + rows_dev :, :], w_ref[0]).astype(BF)
    part_ref[...] = wide_nt(send_ref[HB : HB + rows_dev, :], w_ref[0])


def recv_back_kernel(w_ref, edges_ref, dm_ref, dn_ref, cot_ref, part_ref, grad_ref, recv_ref):
    rows_dev = cot_ref.shape[0]
    for at in spans(edges_ref.shape[1], MESH_SPAN):
        recv = nt(table(rows_dev, edges_ref[1:2, at]), dm_ref[:, at])
        recv_ref[...] = recv + recv_ref[...] if at.start else recv
    grad_ref[...] = (
        cot_ref[...].astype(F32)
        + nt(dn_ref[...], w_ref[5])
        + wide_nt(recv_ref[...], w_ref[1])
        + part_ref[...]
    )


def last_kernel(
    part_ref, own_ref, in0_ref, in1_ref, in2_ref, in3_ref, prev_ref, next_ref, bnd_ref, out_ref
):
    rows_dev = part_ref.shape[0]
    total = own_ref[...]
    for ref in (in0_ref, in1_ref, in2_ref, in3_ref):
        total = total + ref[...].astype(F32)
    out_ref[...] = part_ref[...] + wide_nn(table(rows_dev, bnd_ref[...]), total)
    out_ref[:HB, :] += prev_ref[...].astype(F32)
    out_ref[rows_dev - HB :, :] += next_ref[...].astype(F32)


def call(kernel, outs, args, scratch=(), smem=0, hbm=0, flops=0, mib=32):
    spec = pl.BlockSpec(memory_space=pltpu.VMEM)
    plain = len(args) - smem - hbm
    in_specs = [pl.BlockSpec(memory_space=pltpu.SMEM)] * smem + [spec] * plain
    in_specs += [pl.BlockSpec(memory_space=pltpu.HBM)] * hbm
    scratch_shapes = [pltpu.VMEM(shape, kind) for shape, kind in scratch]
    if hbm:
        scratch_shapes.append(pltpu.SemaphoreType.DMA((hbm,)))
    return pl.pallas_call(
        kernel,
        out_shape=[jax.ShapeDtypeStruct(shape, kind) for shape, kind in outs],
        in_specs=in_specs,
        out_specs=[spec] * len(outs),
        scratch_shapes=scratch_shapes,
        compiler_params=pltpu.CompilerParams(vmem_limit_bytes=mib * MIB),
        cost_estimate=pl.CostEstimate(flops=flops, bytes_accessed=4000000, transcendentals=0),
    )(*args)


def exchanged(block, mask_x=0, mask_y=0, mask_z=0, mask_core=0):
    route = []
    for region in range(32):
        for panel in range(8):
            other_region = region ^ ((mask_x >> 1) << 4 | mask_z << 1 | mask_core)
            other_panel = panel ^ ((mask_x & 1) << 2 | mask_y)
            route.append((region * 8 + panel, other_region * 8 + other_panel))
    return lax.ppermute(block, ("region", "panel"), route)


def swapped(block, bit):
    size = lax.axis_size("region")
    return lax.ppermute(block, "region", [(i, i ^ (1 << bit)) for i in range(size)])


def shifted(array, by):
    length = lax.axis_size("panel")
    pairs = [(i, i + by) for i in range(length) if 0 <= i + by < length]
    return lax.ppermute(array, "panel", pairs)


def wide(block):
    return block.astype(F32)


def ordered_by_y(found, row_y):
    odd, high = row_y % 2 == 1, row_y >= 2
    low_pair = [jnp.where(odd, found[1], found[0]), jnp.where(odd, found[0], found[1])]
    high_pair = [jnp.where(odd, found[3], found[2]), jnp.where(odd, found[2], found[3])]
    ordered = [jnp.where(high, b, a) for a, b in zip(low_pair, high_pair)]
    ordered += [jnp.where(high, a, b) for a, b in zip(low_pair, high_pair)]
    return jnp.concatenate(ordered, axis=0)


def joined(own, other, which):
    first = jnp.where(which == 0, own, other)
    second = jnp.where(which == 0, other, own)
    return jnp.concatenate([first, second], axis=0)


def tie(*arrays):
    return lax.optimization_barrier(arrays)


def shards(
    latents, edge_feats, weights, cotangent, mesh_edges, boundary, contact_edges, contact_counts
):
    rows_dev, width = latents.shape
    bound_count = boundary.shape[0]
    rounds = contact_counts.shape[1]
    edge_count = mesh_edges.shape[1]
    contact_count = contact_edges.shape[1]
    bnd = boundary.reshape(1, bound_count)
    core = lax.axis_index("region") % 2
    row_y = lax.axis_index("panel") % 4
    scale = 1.0 / math.sqrt(rows_dev * lax.axis_size("region") * lax.axis_size("panel"))

    low_rows, high_rows, lat_t, bound_t = call(
        bound_kernel,
        [((HB, width), BF), ((HB, width), BF), ((width, rows_dev), BF), ((width, bound_count), BF)],
        [latents, bnd],
        [((rows_dev, width), BF), ((1, bound_count), jnp.int32)],
        hbm=2,
        flops=10**10,
        mib=8,
    )
    before = shifted(high_rows, 1)
    after = shifted(low_rows, -1)
    fars = [exchanged(bound_t, mask_core=1)]
    fars += [exchanged(bound_t, mask_z=mask) for mask in (1, 2, 4)]
    own_rows, recv_rows = call(
        gather_kernel,
        [((width, edge_count), BF), ((width, edge_count), BF)],
        [lat_t, mesh_edges],
        flops=4 * 10**9,
        mib=16,
    )
    before, after, own_rows = tie(before, after, own_rows)
    send_rows, slope, agg = call(
        mesh_kernel,
        [((width, edge_count), BF), ((width, edge_count), F32), ((rows_dev, width), BF)],
        [before, after, own_rows, recv_rows, mesh_edges, weights, edge_feats],
        [((rows_dev, width), F32)],
        flops=3 * 10**9,
        mib=16,
    )
    new_rows, kept, sent, d_mesh, d_contact, d_node = call(
        functools.partial(main_kernel, scale=scale),
        [
            ((rows_dev, width), BF),
            ((9 * width // 2, width), F32),
            ((9 * width // 2, width), BF),
            ((width, edge_count), BF),
            ((width, contact_count), BF),
            ((rows_dev, width), BF),
        ],
        [contact_counts, core.reshape(1), latents, lat_t, bound_t, *fars, send_rows, recv_rows, slope, agg]
        + [edge_feats, cotangent, weights, mesh_edges, contact_edges, bnd],
        [
            ((bound_count, width), F32),
            ((width, contact_count), F32),
            ((2 * width, contact_count), BF),
            ((9 * width, width), F32),
            ((rows_dev, width), BF),
            ((width, rows_dev), BF),
            ((width, rows_dev), BF),
        ],
        smem=2,
        flops=8 * 10**9,
        mib=26,
    )
    other = exchanged(sent, mask_core=1)
    *far_grads, own_grad = call(
        contact_back_kernel,
        [((bound_count, width), BF)] * rounds + [((bound_count, width), F32)],
        [weights, contact_edges, d_contact],
        flops=2 * 10**9,
        mib=16,
    )
    other, *far_grads = tie(other, *far_grads)
    block = kept + wide(other)
    size = block.shape[0] // 4
    pieces = [
        lax.dynamic_slice_in_dim(block, (row_y ^ mask) * size, size, 0) for mask in range(4)
    ]
    one, two, three = [exchanged(pieces[mask].astype(BF), mask_y=mask) for mask in (1, 2, 3)]
    in_one = exchanged(far_grads[1], mask_z=1)
    pair = exchanged(jnp.concatenate(far_grads[2:], axis=0), mask_z=2)
    one, two, three, d_mesh = tie(one, two, three, d_mesh)
    block = ((pieces[0] + wide(one)) + (wide(two) + wide(three))).astype(BF)

    one, two, three = [exchanged(block, mask_x=mask) for mask in (1, 2, 3)]
    part, low, high = call(
        send_back_kernel,
        [((rows_dev, width), F32), ((HB, width), BF), ((HB, width), BF)],
        [weights, mesh_edges, d_mesh],
        [((rows_dev + 2 * HB, width), F32)],
        flops=2 * 10**9,
        mib=16,
    )
    one, two, three, part, low, high, in_one, pair = tie(
        one, two, three, part, low, high, in_one, pair
    )
    block = ((wide(block) + wide(one)) + (wide(two) + wide(three))).astype(BF)

    other = exchanged(block, mask_z=1)
    in_zero = exchanged(far_grads[0], mask_core=1)
    other, in_zero, part = tie(other, in_zero, part)
    block = (wide(block) + wide(other)).astype(BF)
    other = exchanged(block, mask_z=2)
    (part,) = call(
        recv_back_kernel,
        [((rows_dev, width), F32)],
        [weights, mesh_edges, d_mesh, d_node, cotangent, part],
        [((rows_dev, width), F32)],
        flops=2 * 10**9,
        mib=16,
    )
    other, part, pair, low, high = tie(other, part, pair, low, high)
    block = (wide(block) + wide(other)).astype(BF)
    in_two = pair[:bound_count]
    other = exchanged(jnp.concatenate([block, pair[bound_count:]], axis=0), mask_z=6)
    from_prev = shifted(high, 1)
    from_next = shifted(low, -1)
    other, from_prev, from_next = tie(other, from_prev, from_next)
    in_three = other[size:]
    block = (wide(block) + wide(other[:size])).astype(BF)

    found = [exchanged(block, mask_y=mask) for mask in (1, 2, 3)]
    found = tie(*found)
    block = ordered_by_y([block, *found], row_y)
    other = exchanged(block, mask_core=1)
    (grad_rows,) = call(
        last_kernel,
        [((rows_dev, width), F32)],
        [part, own_grad, in_zero, in_one, in_two, in_three, from_prev, from_next, bnd],
        flops=10**8,
        mib=8,
    )
    block = joined(block, other, core)
    return (new_rows, grad_rows, wide(block).reshape(9, width, width))


def solution(mesh):
    blocks = P(("region", "panel"), None)
    placed = (
        blocks,
        blocks,
        P(),
        blocks,
        P(None, ("region", "panel")),
        P(("region", "panel")),
        P(None, ("region", "panel")),
        blocks,
    )
    return jax.shard_map(
        shards, mesh=mesh, in_specs=placed, out_specs=(blocks, blocks, P()), check_vma=False
    )
```

```python
import functools
import math

import jax
import jax.numpy as jnp
from jax import lax
from jax.experimental import pallas as pl
from jax.experimental.pallas import tpu as pltpu
from jax.sharding import PartitionSpec as P

HB = 64
BF = jnp.bfloat16
F32 = jnp.float32
MESH_SPAN = 1536
NODE_SPAN = 512
MIB = 1024 * 1024


def nn(a, b):
    return lax.dot_general(a, b, (((1,), (0,)), ((), ())), preferred_element_type=F32)


def nt(a, b):
    return lax.dot_general(a, b, (((1,), (1,)), ((), ())), preferred_element_type=F32)


def tn(a, b):
    return lax.dot_general(a, b, (((0,), (0,)), ((), ())), preferred_element_type=F32)


def in_two(values):
    high = values.astype(BF)
    return high, (values - high.astype(F32)).astype(BF)


def wide_nt(a, b):
    high, low = in_two(a)
    return nt(high, b) + nt(low, b)


def wide_nn(a, b):
    high, low = in_two(b)
    return nn(a, high) + nn(a, low)


def identity():
    row = lax.broadcasted_iota(jnp.int32, (128, 128), 0)
    column = lax.broadcasted_iota(jnp.int32, (128, 128), 1)
    return (row == column).astype(BF)


def transposed(a):
    return nt(identity(), a).astype(BF)


def table(count, ids):
    rows = lax.broadcasted_iota(jnp.int32, (count, ids.shape[1]), 0)
    return (rows == ids).astype(BF)


def silu_parts(x):
    s = 0.5 * jnp.tanh(0.5 * x) + 0.5
    return x * s, s * (1.0 + x * (1.0 - s))


def spans(total, size):
    return [slice(first, first + size) for first in range(0, total, size)]


def fetched(pairs, sems):
    copies = [pltpu.make_async_copy(a, b, sems.at[k]) for k, (a, b) in enumerate(pairs)]
    for copy in copies:
        copy.start()
    return copies


def bound_kernel(lat_hbm, bnd_hbm, low_ref, high_ref, lat_t_ref, bound_t_ref, lat, bnd, sems):
    for copy in fetched([(lat_hbm, lat), (bnd_hbm, bnd)], sems):
        copy.wait()
    rows_dev = lat.shape[0]
    low_ref[...] = lat[:HB, :]
    high_ref[...] = lat[rows_dev - HB :, :]
    lat_t = transposed(lat[...])
    lat_t_ref[...] = lat_t
    bound_t_ref[...] = nn(lat_t, table(rows_dev, bnd[...])).astype(BF)


def gather_kernel(lat_t_ref, edges_ref, send_ref, recv_ref):
    rows_dev = lat_t_ref.shape[1]
    for at in spans(edges_ref.shape[1], MESH_SPAN):
        send_ref[:, at] = nn(lat_t_ref[...], table(rows_dev, edges_ref[0:1, at] - HB)).astype(BF)
        recv_ref[:, at] = nn(lat_t_ref[...], table(rows_dev, edges_ref[1:2, at])).astype(BF)


def mesh_kernel(
    before_ref, after_ref, own_ref, recv_ref, edges_ref, w_ref, feats_ref,
    send_ref, slope_ref, agg_ref, sum_ref,
):
    rows_dev = agg_ref.shape[0]
    rim_t = transposed(jnp.concatenate([before_ref[...], after_ref[...]], axis=0))
    w0_t, w1_t, w2_t = transposed(w_ref[0]), transposed(w_ref[1]), transposed(w_ref[2])
    for at in spans(edges_ref.shape[1], MESH_SPAN):
        ids = edges_ref[0:1, at]
        ids = jnp.where(ids < HB, ids, jnp.where(ids < HB + rows_dev, -1, ids - rows_dev))
        rim_rows = nn(rim_t, table(2 * HB, ids))
        send_ref[:, at] = (own_ref[:, at].astype(F32) + rim_rows).astype(BF)
        x = nn(w0_t, send_ref[:, at]) + nn(w1_t, recv_ref[:, at]) + nt(w2_t, feats_ref[at, :])
        message, slope = silu_parts(x)
        slope_ref[:, at] = slope
        part = nt(table(rows_dev, edges_ref[1:2, at]), message.astype(BF))
        if at.start:
            part = part + sum_ref[...]
        sum_ref[...] = part
    agg_ref[...] = sum_ref[...].astype(BF)


def main_kernel(
    counts_ref, core_ref, lat_ref, lat_t_ref, bound_t_ref, far0_ref, far1_ref, far2_ref,
    far3_ref, send_ref, recv_ref, slope_m_ref, agg_ref, feats_ref, cot_ref, w_ref, edges_ref,
    contacts_ref, bnd_ref,
    new_ref, kept_ref, sent_ref, dm_ref, dc_ref, dn_ref,
    aggb_ref, slope_c_ref, both_ref, gw_ref, aggc_ref, dagg_t_ref, daggc_t_ref,
    *, scale,
):
    rows_dev = lat_ref.shape[0]
    bound_count = bnd_ref.shape[1]
    fars = (far0_ref, far1_ref, far2_ref, far3_ref)
    rounds = len(fars)
    round_rows = contacts_ref.shape[1] // rounds
    w_t = jnp.concatenate([transposed(w_ref[3]), transposed(w_ref[4])], axis=1)

    for r, at in enumerate(spans(contacts_ref.shape[1], round_rows)):
        place = lax.broadcasted_iota(jnp.int32, (1, round_rows), 1)
        live = (place < counts_ref[0, r]).astype(F32)
        hits = table(bound_count, contacts_ref[0:1, at])
        both_ref[:128, at] = nn(bound_t_ref[...], hits).astype(BF)
        both_ref[128:, at] = nn(
            fars[r][...], table(bound_count, contacts_ref[1:2, at])
        ).astype(BF)
        message, slope = silu_parts(nn(w_t, both_ref[:, at]))
        slope_c_ref[:, at] = slope * live
        part = nt(hits, (message * live).astype(BF))
        if r:
            part = part + aggb_ref[...]
        aggb_ref[...] = part

    bound_table = table(rows_dev, bnd_ref[...])
    aggc_ref[...] = nn(bound_table, aggb_ref[...].astype(BF)).astype(BF)
    for at in spans(rows_dev, NODE_SPAN):
        lat = lat_ref[at, :]
        cot = cot_ref[at, :]
        agg = agg_ref[at, :]
        aggc = aggc_ref[at, :]
        x = nn(lat, w_ref[5]) + nn(agg, w_ref[6]) + nn(aggc, w_ref[7])
        message, slope = silu_parts(x)
        hidden = message.astype(BF)
        new_ref[at, :] = (lat.astype(F32) + nn(hidden, w_ref[8])).astype(BF)
        d_node = (nt(cot, w_ref[8]) * slope).astype(BF)
        dn_ref[at, :] = d_node
        dagg_t_ref[:, at] = nt(w_ref[6], d_node).astype(BF)
        daggc_t_ref[:, at] = nt(w_ref[7], d_node).astype(BF)
        parts = [
            nn(lat_t_ref[:, at], d_node), tn(agg, d_node), tn(aggc, d_node), tn(hidden, cot)
        ]
        for k, part in enumerate(parts):
            where = slice(640 + 128 * k, 768 + 128 * k)
            gw_ref[where, :] = part + gw_ref[where, :] if at.start else part

    for at in spans(edges_ref.shape[1], MESH_SPAN):
        gathered = nn(dagg_t_ref[...], table(rows_dev, edges_ref[1:2, at]))
        d = (gathered * slope_m_ref[:, at]).astype(BF)
        dm_ref[:, at] = d
        parts = [nt(send_ref[:, at], d), nt(recv_ref[:, at], d), nn(d, feats_ref[at, :])]
        for k, part in enumerate(parts):
            where = slice(128 * k, 128 * k + 128)
            gw_ref[where, :] = part + gw_ref[where, :] if at.start else part

    gw_ref[256:384, :] = gw_ref[256:384, :].T
    dbg_t = nn(daggc_t_ref[...], bound_table).astype(BF)
    for r, at in enumerate(spans(contacts_ref.shape[1], round_rows)):
        gathered = nn(dbg_t, table(bound_count, contacts_ref[0:1, at]))
        d = (gathered * slope_c_ref[:, at]).astype(BF)
        dc_ref[:, at] = d
        pair = nt(both_ref[:, at], d)
        gw_ref[384:640, :] = pair + gw_ref[384:640, :] if r else pair

    half = gw_ref.shape[0] // 2
    core = core_ref[0]
    kept_ref[...] = gw_ref[pl.ds(pl.multiple_of(core * half, 64), half), :] * scale
    sent = gw_ref[pl.ds(pl.multiple_of((1 - core) * half, 64), half), :] * scale
    sent_ref[...] = sent.astype(BF)


def contact_back_kernel(
    w_ref, contacts_ref, dc_ref, far0_ref, far1_ref, far2_ref, far3_ref, own_ref
):
    outs = (far0_ref, far1_ref, far2_ref, far3_ref)
    bound_count = own_ref.shape[0]
    for r, at in enumerate(spans(contacts_ref.shape[1], contacts_ref.shape[1] // len(outs))):
        d = dc_ref[:, at]
        part = nt(table(bound_count, contacts_ref[0:1, at]), d)
        own_ref[...] = part + own_ref[...] if r else part
        far = nt(table(bound_count, contacts_ref[1:2, at]), d)
        outs[r][...] = wide_nt(far, w_ref[4]).astype(BF)
    own_ref[...] = wide_nt(own_ref[...], w_ref[3])


def send_back_kernel(w_ref, edges_ref, dm_ref, part_ref, low_ref, high_ref, send_ref):
    rows_dev = part_ref.shape[0]
    for at in spans(edges_ref.shape[1], MESH_SPAN):
        send = nt(table(rows_dev + 2 * HB, edges_ref[0:1, at]), dm_ref[:, at])
        send_ref[...] = send + send_ref[...] if at.start else send
    low_ref[...] = wide_nt(send_ref[:HB, :], w_ref[0]).astype(BF)
    high_ref[...] = wide_nt(send_ref[HB + rows_dev :, :], w_ref[0]).astype(BF)
    part_ref[...] = wide_nt(send_ref[HB : HB + rows_dev, :], w_ref[0])


def recv_back_kernel(w_ref, edges_ref, dm_ref, dn_ref, cot_ref, part_ref, grad_ref, recv_ref):
    rows_dev = cot_ref.shape[0]
    for at in spans(edges_ref.shape[1], MESH_SPAN):
        recv = nt(table(rows_dev, edges_ref[1:2, at]), dm_ref[:, at])
        recv_ref[...] = recv + recv_ref[...] if at.start else recv
    grad_ref[...] = (
        cot_ref[...].astype(F32)
        + nt(dn_ref[...], w_ref[5])
        + wide_nt(recv_ref[...], w_ref[1])
        + part_ref[...]
    )


def last_kernel(
    part_ref, own_ref, in0_ref, in1_ref, in2_ref, in3_ref, prev_ref, next_ref, bnd_ref, out_ref
):
    rows_dev = part_ref.shape[0]
    total = own_ref[...]
    for ref in (in0_ref, in1_ref, in2_ref, in3_ref):
        total = total + ref[...].astype(F32)
    out_ref[...] = part_ref[...] + wide_nn(table(rows_dev, bnd_ref[...]), total)
    out_ref[:HB, :] += prev_ref[...].astype(F32)
    out_ref[rows_dev - HB :, :] += next_ref[...].astype(F32)


def call(kernel, outs, args, scratch=(), smem=0, hbm=0, flops=0, mib=32):
    spec = pl.BlockSpec(memory_space=pltpu.VMEM)
    plain = len(args) - smem - hbm
    in_specs = [pl.BlockSpec(memory_space=pltpu.SMEM)] * smem + [spec] * plain
    in_specs += [pl.BlockSpec(memory_space=pltpu.HBM)] * hbm
    scratch_shapes = [pltpu.VMEM(shape, kind) for shape, kind in scratch]
    if hbm:
        scratch_shapes.append(pltpu.SemaphoreType.DMA((hbm,)))
    return pl.pallas_call(
        kernel,
        out_shape=[jax.ShapeDtypeStruct(shape, kind) for shape, kind in outs],
        in_specs=in_specs,
        out_specs=[spec] * len(outs),
        scratch_shapes=scratch_shapes,
        compiler_params=pltpu.CompilerParams(vmem_limit_bytes=mib * MIB),
        cost_estimate=pl.CostEstimate(flops=flops, bytes_accessed=4000000, transcendentals=0),
    )(*args)


def exchanged(block, mask_x=0, mask_y=0, mask_z=0, mask_core=0):
    route = []
    for region in range(32):
        for panel in range(8):
            other_region = region ^ ((mask_x >> 1) << 4 | mask_z << 1 | mask_core)
            other_panel = panel ^ ((mask_x & 1) << 2 | mask_y)
            route.append((region * 8 + panel, other_region * 8 + other_panel))
    return lax.ppermute(block, ("region", "panel"), route)


def swapped(block, bit):
    size = lax.axis_size("region")
    return lax.ppermute(block, "region", [(i, i ^ (1 << bit)) for i in range(size)])


def shifted(array, by):
    length = lax.axis_size("panel")
    pairs = [(i, i + by) for i in range(length) if 0 <= i + by < length]
    return lax.ppermute(array, "panel", pairs)


def wide(block):
    return block.astype(F32)


def ordered_by_y(found, row_y):
    odd, high = row_y % 2 == 1, row_y >= 2
    low_pair = [jnp.where(odd, found[1], found[0]), jnp.where(odd, found[0], found[1])]
    high_pair = [jnp.where(odd, found[3], found[2]), jnp.where(odd, found[2], found[3])]
    ordered = [jnp.where(high, b, a) for a, b in zip(low_pair, high_pair)]
    ordered += [jnp.where(high, a, b) for a, b in zip(low_pair, high_pair)]
    return jnp.concatenate(ordered, axis=0)


def joined(own, other, which):
    first = jnp.where(which == 0, own, other)
    second = jnp.where(which == 0, other, own)
    return jnp.concatenate([first, second], axis=0)


def tie(*arrays):
    return lax.optimization_barrier(arrays)


def shards(
    latents, edge_feats, weights, cotangent, mesh_edges, boundary, contact_edges, contact_counts
):
    rows_dev, width = latents.shape
    bound_count = boundary.shape[0]
    rounds = contact_counts.shape[1]
    edge_count = mesh_edges.shape[1]
    contact_count = contact_edges.shape[1]
    bnd = boundary.reshape(1, bound_count)
    core = lax.axis_index("region") % 2
    row_y = lax.axis_index("panel") % 4
    scale = 1.0 / math.sqrt(rows_dev * lax.axis_size("region") * lax.axis_size("panel"))

    low_rows, high_rows, lat_t, bound_t = call(
        bound_kernel,
        [((HB, width), BF), ((HB, width), BF), ((width, rows_dev), BF), ((width, bound_count), BF)],
        [latents, bnd],
        [((rows_dev, width), BF), ((1, bound_count), jnp.int32)],
        hbm=2,
        flops=10**10,
        mib=8,
    )
    before = shifted(high_rows, 1)
    after = shifted(low_rows, -1)
    fars = [exchanged(bound_t, mask_core=1)]
    fars += [exchanged(bound_t, mask_z=mask) for mask in (1, 2, 4)]
    own_rows, recv_rows = call(
        gather_kernel,
        [((width, edge_count), BF), ((width, edge_count), BF)],
        [lat_t, mesh_edges],
        flops=4 * 10**9,
        mib=16,
    )
    before, after, own_rows = tie(before, after, own_rows)
    send_rows, slope, agg = call(
        mesh_kernel,
        [((width, edge_count), BF), ((width, edge_count), F32), ((rows_dev, width), BF)],
        [before, after, own_rows, recv_rows, mesh_edges, weights, edge_feats],
        [((rows_dev, width), F32)],
        flops=3 * 10**9,
        mib=16,
    )
    new_rows, kept, sent, d_mesh, d_contact, d_node = call(
        functools.partial(main_kernel, scale=scale),
        [
            ((rows_dev, width), BF),
            ((9 * width // 2, width), F32),
            ((9 * width // 2, width), BF),
            ((width, edge_count), BF),
            ((width, contact_count), BF),
            ((rows_dev, width), BF),
        ],
        [contact_counts, core.reshape(1), latents, lat_t, bound_t, *fars, send_rows, recv_rows, slope, agg]
        + [edge_feats, cotangent, weights, mesh_edges, contact_edges, bnd],
        [
            ((bound_count, width), F32),
            ((width, contact_count), F32),
            ((2 * width, contact_count), BF),
            ((9 * width, width), F32),
            ((rows_dev, width), BF),
            ((width, rows_dev), BF),
            ((width, rows_dev), BF),
        ],
        smem=2,
        flops=8 * 10**9,
        mib=26,
    )
    other = exchanged(sent, mask_core=1)
    part, low, high = call(
        send_back_kernel,
        [((rows_dev, width), F32), ((HB, width), BF), ((HB, width), BF)],
        [weights, mesh_edges, d_mesh],
        [((rows_dev + 2 * HB, width), F32)],
        flops=2 * 10**9,
        mib=16,
    )
    other, part, low, high, d_contact = tie(other, part, low, high, d_contact)
    block = kept + wide(other)
    size = block.shape[0] // 4
    pieces = [
        lax.dynamic_slice_in_dim(block, (row_y ^ mask) * size, size, 0) for mask in range(4)
    ]
    found = [exchanged(pieces[mask].astype(BF), mask_y=mask) for mask in (1, 2, 3)]
    *far_grads, own_grad = call(
        contact_back_kernel,
        [((bound_count, width), BF)] * rounds + [((bound_count, width), F32)],
        [weights, contact_edges, d_contact],
        flops=2 * 10**9,
        mib=16,
    )
    one, two, three, *far_grads = tie(*found, *far_grads)
    block = ((pieces[0] + wide(one)) + (wide(two) + wide(three))).astype(BF)

    rim = jnp.where(row_y == 0, low, high)
    one = exchanged(jnp.concatenate([block, rim], axis=0), mask_x=1)
    two, three = [exchanged(block, mask_x=mask) for mask in (2, 3)]
    in_one = exchanged(far_grads[1], mask_z=1)
    pair = exchanged(jnp.concatenate(far_grads[2:], axis=0), mask_z=2)
    one, two, three, part = tie(one, two, three, part)
    rim = one[size:]
    block = ((wide(block) + wide(one[:size])) + (wide(two) + wide(three))).astype(BF)

    other = exchanged(block, mask_z=1)
    (part,) = call(
        recv_back_kernel,
        [((rows_dev, width), F32)],
        [weights, mesh_edges, d_mesh, d_node, cotangent, part],
        [((rows_dev, width), F32)],
        flops=2 * 10**9,
        mib=16,
    )
    other, part, in_one = tie(other, part, in_one)
    block = (wide(block) + wide(other)).astype(BF)
    other = exchanged(block, mask_z=2)
    in_zero = exchanged(far_grads[0], mask_core=1)
    other, in_zero, pair = tie(other, in_zero, pair)
    block = (wide(block) + wide(other)).astype(BF)
    in_two = pair[:bound_count]
    other = exchanged(jnp.concatenate([block, pair[bound_count:]], axis=0), mask_z=6)
    in_three = other[size:]
    block = (wide(block) + wide(other[:size])).astype(BF)

    rim = jnp.where(row_y == 1, high, jnp.where(row_y == 2, low, rim))
    three = exchanged(jnp.concatenate([block, rim], axis=0), mask_y=3)
    rim = jnp.where(row_y % 2 == 0, high, low)
    one = exchanged(jnp.concatenate([block, rim], axis=0), mask_y=1)
    two = exchanged(block, mask_y=2)
    one, two, three = tie(one, two, three)
    panel = lax.axis_index("panel")
    nothing = jnp.zeros_like(rim)
    from_prev = jnp.where(row_y % 2 == 0, three[size:], one[size:])
    from_prev = jnp.where(panel == 0, nothing, from_prev)
    from_next = jnp.where(row_y % 2 == 0, one[size:], three[size:])
    from_next = jnp.where(panel == lax.axis_size("panel") - 1, nothing, from_next)
    block = ordered_by_y([block, one[:size], two, three[:size]], row_y)
    other = exchanged(block, mask_core=1)
    (grad_rows,) = call(
        last_kernel,
        [((rows_dev, width), F32)],
        [part, own_grad, in_zero, in_one, in_two, in_three, from_prev, from_next, bnd],
        flops=10**8,
        mib=8,
    )
    block = joined(block, other, core)
    return (new_rows, grad_rows, wide(block).reshape(9, width, width))


def solution(mesh):
    blocks = P(("region", "panel"), None)
    placed = (
        blocks,
        blocks,
        P(),
        blocks,
        P(None, ("region", "panel")),
        P(("region", "panel")),
        P(None, ("region", "panel")),
        blocks,
    )
    return jax.shard_map(
        shards, mesh=mesh, in_specs=placed, out_specs=(blocks, blocks, P()), check_vma=False
    )
```

```python
import functools
import math

import jax
import jax.numpy as jnp
from jax import lax
from jax.experimental import pallas as pl
from jax.experimental.pallas import tpu as pltpu
from jax.sharding import PartitionSpec as P

HB = 64
BF = jnp.bfloat16
F32 = jnp.float32
MESH_SPAN = 1536
NODE_SPAN = 512
MIB = 1024 * 1024


def nn(a, b):
    return lax.dot_general(a, b, (((1,), (0,)), ((), ())), preferred_element_type=F32)


def nt(a, b):
    return lax.dot_general(a, b, (((1,), (1,)), ((), ())), preferred_element_type=F32)


def tn(a, b):
    return lax.dot_general(a, b, (((0,), (0,)), ((), ())), preferred_element_type=F32)


def in_two(values):
    high = values.astype(BF)
    return high, (values - high.astype(F32)).astype(BF)


def wide_nt(a, b):
    high, low = in_two(a)
    return nt(high, b) + nt(low, b)


def wide_nn(a, b):
    high, low = in_two(b)
    return nn(a, high) + nn(a, low)


def identity():
    row = lax.broadcasted_iota(jnp.int32, (128, 128), 0)
    column = lax.broadcasted_iota(jnp.int32, (128, 128), 1)
    return (row == column).astype(BF)


def transposed(a):
    return nt(identity(), a).astype(BF)


def table(count, ids):
    rows = lax.broadcasted_iota(jnp.int32, (count, ids.shape[1]), 0)
    return (rows == ids).astype(BF)


def silu_parts(x):
    s = 0.5 * jnp.tanh(0.5 * x) + 0.5
    return x * s, s * (1.0 + x * (1.0 - s))


def spans(total, size):
    return [slice(first, first + size) for first in range(0, total, size)]


def fetched(pairs, sems):
    copies = [pltpu.make_async_copy(a, b, sems.at[k]) for k, (a, b) in enumerate(pairs)]
    for copy in copies:
        copy.start()
    return copies


def bound_kernel(lat_hbm, bnd_hbm, low_ref, high_ref, lat_t_ref, bound_t_ref, lat, bnd, sems):
    for copy in fetched([(lat_hbm, lat), (bnd_hbm, bnd)], sems):
        copy.wait()
    rows_dev = lat.shape[0]
    low_ref[...] = lat[:HB, :]
    high_ref[...] = lat[rows_dev - HB :, :]
    lat_t = transposed(lat[...])
    lat_t_ref[...] = lat_t
    bound_t_ref[...] = nn(lat_t, table(rows_dev, bnd[...])).astype(BF)


def gather_kernel(lat_t_ref, edges_ref, send_ref, recv_ref):
    rows_dev = lat_t_ref.shape[1]
    for at in spans(edges_ref.shape[1], MESH_SPAN):
        send_ref[:, at] = nn(lat_t_ref[...], table(rows_dev, edges_ref[0:1, at] - HB)).astype(BF)
        recv_ref[:, at] = nn(lat_t_ref[...], table(rows_dev, edges_ref[1:2, at])).astype(BF)


def mesh_kernel(
    before_ref, after_ref, own_ref, recv_ref, edges_ref, w_ref, feats_ref,
    send_ref, slope_ref, agg_ref, sum_ref,
):
    rows_dev = agg_ref.shape[0]
    rim_t = transposed(jnp.concatenate([before_ref[...], after_ref[...]], axis=0))
    w0_t, w1_t, w2_t = transposed(w_ref[0]), transposed(w_ref[1]), transposed(w_ref[2])
    for at in spans(edges_ref.shape[1], MESH_SPAN):
        ids = edges_ref[0:1, at]
        ids = jnp.where(ids < HB, ids, jnp.where(ids < HB + rows_dev, -1, ids - rows_dev))
        rim_rows = nn(rim_t, table(2 * HB, ids))
        send_ref[:, at] = (own_ref[:, at].astype(F32) + rim_rows).astype(BF)
        x = nn(w0_t, send_ref[:, at]) + nn(w1_t, recv_ref[:, at]) + nt(w2_t, feats_ref[at, :])
        message, slope = silu_parts(x)
        slope_ref[:, at] = slope
        part = nt(table(rows_dev, edges_ref[1:2, at]), message.astype(BF))
        if at.start:
            part = part + sum_ref[...]
        sum_ref[...] = part
    agg_ref[...] = sum_ref[...].astype(BF)


def contact_round(count, bound_t, far_t, w_t, self_ids, far_ids, both_ref, slope_ref, at):
    slots = bound_t.shape[1]
    place = lax.broadcasted_iota(jnp.int32, self_ids.shape, 1)
    live = (place < count).astype(F32)
    hits = table(slots, self_ids)
    both_ref[:128, at] = nn(bound_t, hits).astype(BF)
    both_ref[128:, at] = nn(far_t, table(slots, far_ids)).astype(BF)
    message, slope = silu_parts(nn(w_t, both_ref[:, at]))
    slope_ref[:, at] = slope * live
    return nt(hits, (message * live).astype(BF))


def contact_kernel(
    counts_ref, bound_t_ref, far0_ref, far1_ref, far2_ref, w_ref, contacts_ref,
    both_ref, slope_ref, sum_ref,
):
    fars = (far0_ref, far1_ref, far2_ref)
    w_t = jnp.concatenate([transposed(w_ref[3]), transposed(w_ref[4])], axis=1)
    round_rows = both_ref.shape[1] // len(fars)
    for r, at in enumerate(spans(both_ref.shape[1], round_rows)):
        part = contact_round(
            counts_ref[0, r], bound_t_ref[...], fars[r][...], w_t,
            contacts_ref[0:1, at], contacts_ref[1:2, at], both_ref, slope_ref, at,
        )
        sum_ref[...] = part + sum_ref[...] if r else part


def main_kernel(
    counts_ref, core_ref, lat_ref, lat_t_ref, bound_t_ref, far3_ref, both_ref, slope_c_ref,
    aggb_ref, send_ref, recv_ref, slope_m_ref, agg_ref, feats_ref, cot_ref, w_ref, edges_ref,
    contacts_ref, bnd_ref,
    new_ref, kept_ref, sent_ref, dm_ref, dc_ref, dn_ref,
    slope_l_ref, both_l_ref, gw_ref, aggc_ref, dagg_t_ref, daggc_t_ref,
    *, scale,
):
    rows_dev = lat_ref.shape[0]
    bound_count = bnd_ref.shape[1]
    round_rows = both_l_ref.shape[1]
    last = contacts_ref.shape[1] // round_rows - 1
    w_t = jnp.concatenate([transposed(w_ref[3]), transposed(w_ref[4])], axis=1)
    at = slice(last * round_rows, (last + 1) * round_rows)
    aggb = aggb_ref[...] + contact_round(
        counts_ref[0, last], bound_t_ref[...], far3_ref[...], w_t,
        contacts_ref[0:1, at], contacts_ref[1:2, at], both_l_ref, slope_l_ref, slice(None),
    )

    bound_table = table(rows_dev, bnd_ref[...])
    aggc_ref[...] = nn(bound_table, aggb.astype(BF)).astype(BF)
    for at in spans(rows_dev, NODE_SPAN):
        lat = lat_ref[at, :]
        cot = cot_ref[at, :]
        agg = agg_ref[at, :]
        aggc = aggc_ref[at, :]
        x = nn(lat, w_ref[5]) + nn(agg, w_ref[6]) + nn(aggc, w_ref[7])
        message, slope = silu_parts(x)
        hidden = message.astype(BF)
        new_ref[at, :] = (lat.astype(F32) + nn(hidden, w_ref[8])).astype(BF)
        d_node = (nt(cot, w_ref[8]) * slope).astype(BF)
        dn_ref[at, :] = d_node
        dagg_t_ref[:, at] = nt(w_ref[6], d_node).astype(BF)
        daggc_t_ref[:, at] = nt(w_ref[7], d_node).astype(BF)
        parts = [
            nn(lat_t_ref[:, at], d_node), tn(agg, d_node), tn(aggc, d_node), tn(hidden, cot)
        ]
        for k, part in enumerate(parts):
            where = slice(640 + 128 * k, 768 + 128 * k)
            gw_ref[where, :] = part + gw_ref[where, :] if at.start else part

    for at in spans(edges_ref.shape[1], MESH_SPAN):
        gathered = nn(dagg_t_ref[...], table(rows_dev, edges_ref[1:2, at]))
        d = (gathered * slope_m_ref[:, at]).astype(BF)
        dm_ref[:, at] = d
        parts = [nt(send_ref[:, at], d), nt(recv_ref[:, at], d), nn(d, feats_ref[at, :])]
        for k, part in enumerate(parts):
            where = slice(128 * k, 128 * k + 128)
            gw_ref[where, :] = part + gw_ref[where, :] if at.start else part

    gw_ref[256:384, :] = gw_ref[256:384, :].T
    dbg_t = nn(daggc_t_ref[...], bound_table).astype(BF)
    for r, at in enumerate(spans(contacts_ref.shape[1], round_rows)):
        gathered = nn(dbg_t, table(bound_count, contacts_ref[0:1, at]))
        slope = slope_l_ref[...] if r == last else slope_c_ref[:, at]
        both = both_l_ref[...] if r == last else both_ref[:, at]
        d = (gathered * slope).astype(BF)
        dc_ref[:, at] = d
        pair = nt(both, d)
        gw_ref[384:640, :] = pair + gw_ref[384:640, :] if r else pair

    half = gw_ref.shape[0] // 2
    core = core_ref[0]
    kept_ref[...] = gw_ref[pl.ds(pl.multiple_of(core * half, 64), half), :] * scale
    sent = gw_ref[pl.ds(pl.multiple_of((1 - core) * half, 64), half), :] * scale
    sent_ref[...] = sent.astype(BF)


def contact_back_kernel(
    w_ref, contacts_ref, dc_ref, far0_ref, far1_ref, far2_ref, far3_ref, own_ref
):
    outs = (far0_ref, far1_ref, far2_ref, far3_ref)
    bound_count = own_ref.shape[0]
    for r, at in enumerate(spans(contacts_ref.shape[1], contacts_ref.shape[1] // len(outs))):
        d = dc_ref[:, at]
        part = nt(table(bound_count, contacts_ref[0:1, at]), d)
        own_ref[...] = part + own_ref[...] if r else part
        far = nt(table(bound_count, contacts_ref[1:2, at]), d)
        outs[r][...] = wide_nt(far, w_ref[4]).astype(BF)
    own_ref[...] = wide_nt(own_ref[...], w_ref[3])


def send_back_kernel(w_ref, edges_ref, dm_ref, part_ref, low_ref, high_ref, send_ref):
    rows_dev = part_ref.shape[0]
    for at in spans(edges_ref.shape[1], MESH_SPAN):
        send = nt(table(rows_dev + 2 * HB, edges_ref[0:1, at]), dm_ref[:, at])
        send_ref[...] = send + send_ref[...] if at.start else send
    low_ref[...] = wide_nt(send_ref[:HB, :], w_ref[0]).astype(BF)
    high_ref[...] = wide_nt(send_ref[HB + rows_dev :, :], w_ref[0]).astype(BF)
    part_ref[...] = wide_nt(send_ref[HB : HB + rows_dev, :], w_ref[0])


def recv_back_kernel(w_ref, edges_ref, dm_ref, dn_ref, cot_ref, part_ref, grad_ref, recv_ref):
    rows_dev = cot_ref.shape[0]
    for at in spans(edges_ref.shape[1], MESH_SPAN):
        recv = nt(table(rows_dev, edges_ref[1:2, at]), dm_ref[:, at])
        recv_ref[...] = recv + recv_ref[...] if at.start else recv
    grad_ref[...] = (
        cot_ref[...].astype(F32)
        + nt(dn_ref[...], w_ref[5])
        + wide_nt(recv_ref[...], w_ref[1])
        + part_ref[...]
    )


def last_kernel(
    part_ref, own_ref, in0_ref, in1_ref, in2_ref, in3_ref, prev_ref, next_ref, bnd_ref, out_ref
):
    rows_dev = part_ref.shape[0]
    total = own_ref[...]
    for ref in (in0_ref, in1_ref, in2_ref, in3_ref):
        total = total + ref[...].astype(F32)
    out_ref[...] = part_ref[...] + wide_nn(table(rows_dev, bnd_ref[...]), total)
    out_ref[:HB, :] += prev_ref[...].astype(F32)
    out_ref[rows_dev - HB :, :] += next_ref[...].astype(F32)


def call(kernel, outs, args, scratch=(), smem=0, hbm=0, flops=0, mib=32):
    spec = pl.BlockSpec(memory_space=pltpu.VMEM)
    plain = len(args) - smem - hbm
    in_specs = [pl.BlockSpec(memory_space=pltpu.SMEM)] * smem + [spec] * plain
    in_specs += [pl.BlockSpec(memory_space=pltpu.HBM)] * hbm
    scratch_shapes = [pltpu.VMEM(shape, kind) for shape, kind in scratch]
    if hbm:
        scratch_shapes.append(pltpu.SemaphoreType.DMA((hbm,)))
    return pl.pallas_call(
        kernel,
        out_shape=[jax.ShapeDtypeStruct(shape, kind) for shape, kind in outs],
        in_specs=in_specs,
        out_specs=[spec] * len(outs),
        scratch_shapes=scratch_shapes,
        compiler_params=pltpu.CompilerParams(vmem_limit_bytes=mib * MIB),
        cost_estimate=pl.CostEstimate(flops=flops, bytes_accessed=4000000, transcendentals=0),
    )(*args)


def exchanged(block, mask_x=0, mask_y=0, mask_z=0, mask_core=0):
    route = []
    for region in range(32):
        for panel in range(8):
            other_region = region ^ ((mask_x >> 1) << 4 | mask_z << 1 | mask_core)
            other_panel = panel ^ ((mask_x & 1) << 2 | mask_y)
            route.append((region * 8 + panel, other_region * 8 + other_panel))
    return lax.ppermute(block, ("region", "panel"), route)


def swapped(block, bit):
    size = lax.axis_size("region")
    return lax.ppermute(block, "region", [(i, i ^ (1 << bit)) for i in range(size)])


def shifted(array, by):
    length = lax.axis_size("panel")
    pairs = [(i, i + by) for i in range(length) if 0 <= i + by < length]
    return lax.ppermute(array, "panel", pairs)


def wide(block):
    return block.astype(F32)


def ordered_by_y(found, row_y):
    odd, high = row_y % 2 == 1, row_y >= 2
    low_pair = [jnp.where(odd, found[1], found[0]), jnp.where(odd, found[0], found[1])]
    high_pair = [jnp.where(odd, found[3], found[2]), jnp.where(odd, found[2], found[3])]
    ordered = [jnp.where(high, b, a) for a, b in zip(low_pair, high_pair)]
    ordered += [jnp.where(high, a, b) for a, b in zip(low_pair, high_pair)]
    return jnp.concatenate(ordered, axis=0)


def joined(own, other, which):
    first = jnp.where(which == 0, own, other)
    second = jnp.where(which == 0, other, own)
    return jnp.concatenate([first, second], axis=0)


def tie(*arrays):
    return lax.optimization_barrier(arrays)


def shards(
    latents, edge_feats, weights, cotangent, mesh_edges, boundary, contact_edges, contact_counts
):
    rows_dev, width = latents.shape
    bound_count = boundary.shape[0]
    rounds = contact_counts.shape[1]
    edge_count = mesh_edges.shape[1]
    contact_count = contact_edges.shape[1]
    bnd = boundary.reshape(1, bound_count)
    core = lax.axis_index("region") % 2
    row_y = lax.axis_index("panel") % 4
    scale = 1.0 / math.sqrt(rows_dev * lax.axis_size("region") * lax.axis_size("panel"))

    low_rows, high_rows, lat_t, bound_t = call(
        bound_kernel,
        [((HB, width), BF), ((HB, width), BF), ((width, rows_dev), BF), ((width, bound_count), BF)],
        [latents, bnd],
        [((rows_dev, width), BF), ((1, bound_count), jnp.int32)],
        hbm=2,
        flops=10**10,
        mib=8,
    )
    before = shifted(high_rows, 1)
    after = shifted(low_rows, -1)
    fars = [exchanged(bound_t, mask_core=1)]
    fars += [exchanged(bound_t, mask_z=mask) for mask in (1, 2, 4)]
    own_rows, recv_rows = call(
        gather_kernel,
        [((width, edge_count), BF), ((width, edge_count), BF)],
        [lat_t, mesh_edges],
        flops=4 * 10**9,
        mib=16,
    )
    before, after, own_rows = tie(before, after, own_rows)
    send_rows, slope, agg = call(
        mesh_kernel,
        [((width, edge_count), BF), ((width, edge_count), F32), ((rows_dev, width), BF)],
        [before, after, own_rows, recv_rows, mesh_edges, weights, edge_feats],
        [((rows_dev, width), F32)],
        flops=3 * 10**9,
        mib=16,
    )
    first = (rounds - 1) * contact_count // rounds
    both, slope_c, aggb = call(
        contact_kernel,
        [((2 * width, first), BF), ((width, first), F32), ((bound_count, width), F32)],
        [contact_counts, bound_t, *fars[:3], weights, contact_edges],
        smem=1,
        flops=3 * 10**9,
        mib=16,
    )
    fars[3], both = tie(fars[3], both)
    new_rows, kept, sent, d_mesh, d_contact, d_node = call(
        functools.partial(main_kernel, scale=scale),
        [
            ((rows_dev, width), BF),
            ((9 * width // 2, width), F32),
            ((9 * width // 2, width), BF),
            ((width, edge_count), BF),
            ((width, contact_count), BF),
            ((rows_dev, width), BF),
        ],
        [contact_counts, core.reshape(1), latents, lat_t, bound_t, fars[3], both, slope_c, aggb]
        + [send_rows, recv_rows, slope, agg]
        + [edge_feats, cotangent, weights, mesh_edges, contact_edges, bnd],
        [
            ((width, contact_count // rounds), F32),
            ((2 * width, contact_count // rounds), BF),
            ((9 * width, width), F32),
            ((rows_dev, width), BF),
            ((width, rows_dev), BF),
            ((width, rows_dev), BF),
        ],
        smem=2,
        flops=6 * 10**9,
        mib=20,
    )
    other = exchanged(sent, mask_core=1)
    part, low, high = call(
        send_back_kernel,
        [((rows_dev, width), F32), ((HB, width), BF), ((HB, width), BF)],
        [weights, mesh_edges, d_mesh],
        [((rows_dev + 2 * HB, width), F32)],
        flops=2 * 10**9,
        mib=16,
    )
    other, part, low, high, d_contact = tie(other, part, low, high, d_contact)
    block = kept + wide(other)
    size = block.shape[0] // 4
    pieces = [
        lax.dynamic_slice_in_dim(block, (row_y ^ mask) * size, size, 0) for mask in range(4)
    ]
    found = [exchanged(pieces[mask].astype(BF), mask_y=mask) for mask in (1, 2, 3)]
    *far_grads, own_grad = call(
        contact_back_kernel,
        [((bound_count, width), BF)] * rounds + [((bound_count, width), F32)],
        [weights, contact_edges, d_contact],
        flops=2 * 10**9,
        mib=16,
    )
    one, two, three, *far_grads = tie(*found, *far_grads)
    block = ((pieces[0] + wide(one)) + (wide(two) + wide(three))).astype(BF)

    rim = jnp.where(row_y == 0, low, high)
    one = exchanged(jnp.concatenate([block, rim], axis=0), mask_x=1)
    two, three = [exchanged(block, mask_x=mask) for mask in (2, 3)]
    in_one = exchanged(far_grads[1], mask_z=1)
    pair = exchanged(jnp.concatenate(far_grads[2:], axis=0), mask_z=2)
    one, two, three, part = tie(one, two, three, part)
    rim = one[size:]
    block = ((wide(block) + wide(one[:size])) + (wide(two) + wide(three))).astype(BF)

    other = exchanged(block, mask_z=1)
    (part,) = call(
        recv_back_kernel,
        [((rows_dev, width), F32)],
        [weights, mesh_edges, d_mesh, d_node, cotangent, part],
        [((rows_dev, width), F32)],
        flops=2 * 10**9,
        mib=16,
    )
    other, part, in_one = tie(other, part, in_one)
    block = (wide(block) + wide(other)).astype(BF)
    other = exchanged(block, mask_z=2)
    in_zero = exchanged(far_grads[0], mask_core=1)
    other, in_zero, pair = tie(other, in_zero, pair)
    block = (wide(block) + wide(other)).astype(BF)
    in_two = pair[:bound_count]
    other = exchanged(jnp.concatenate([block, pair[bound_count:]], axis=0), mask_z=6)
    in_three = other[size:]
    block = (wide(block) + wide(other[:size])).astype(BF)

    rim = jnp.where(row_y == 1, high, jnp.where(row_y == 2, low, rim))
    three = exchanged(jnp.concatenate([block, rim], axis=0), mask_y=3)
    rim = jnp.where(row_y % 2 == 0, high, low)
    one = exchanged(jnp.concatenate([block, rim], axis=0), mask_y=1)
    two = exchanged(block, mask_y=2)
    one, two, three = tie(one, two, three)
    panel = lax.axis_index("panel")
    nothing = jnp.zeros_like(rim)
    from_prev = jnp.where(row_y % 2 == 0, three[size:], one[size:])
    from_prev = jnp.where(panel == 0, nothing, from_prev)
    from_next = jnp.where(row_y % 2 == 0, one[size:], three[size:])
    from_next = jnp.where(panel == lax.axis_size("panel") - 1, nothing, from_next)
    block = ordered_by_y([block, one[:size], two, three[:size]], row_y)
    other = exchanged(block, mask_core=1)
    (grad_rows,) = call(
        last_kernel,
        [((rows_dev, width), F32)],
        [part, own_grad, in_zero, in_one, in_two, in_three, from_prev, from_next, bnd],
        flops=10**8,
        mib=8,
    )
    block = joined(wide(block), wide(other), core)
    return (new_rows, grad_rows, block.reshape(9, width, width))


def solution(mesh):
    blocks = P(("region", "panel"), None)
    placed = (
        blocks,
        blocks,
        P(),
        blocks,
        P(None, ("region", "panel")),
        P(("region", "panel")),
        P(None, ("region", "panel")),
        blocks,
    )
    return jax.shard_map(
        shards, mesh=mesh, in_specs=placed, out_specs=(blocks, blocks, P()), check_vma=False
    )
```

```python
import functools
import math

import jax
import jax.numpy as jnp
from jax import lax
from jax.experimental import pallas as pl
from jax.experimental.pallas import tpu as pltpu
from jax.sharding import PartitionSpec as P

HB = 64
BF = jnp.bfloat16
F32 = jnp.float32
MESH_SPAN = 1536
NODE_SPAN = 512
MIB = 1024 * 1024


def nn(a, b):
    return lax.dot_general(a, b, (((1,), (0,)), ((), ())), preferred_element_type=F32)


def nt(a, b):
    return lax.dot_general(a, b, (((1,), (1,)), ((), ())), preferred_element_type=F32)


def tn(a, b):
    return lax.dot_general(a, b, (((0,), (0,)), ((), ())), preferred_element_type=F32)


def in_two(values):
    high = values.astype(BF)
    return high, (values - high.astype(F32)).astype(BF)


def wide_nt(a, b):
    high, low = in_two(a)
    return nt(high, b) + nt(low, b)


def wide_nn(a, b):
    high, low = in_two(b)
    return nn(a, high) + nn(a, low)


def identity():
    row = lax.broadcasted_iota(jnp.int32, (128, 128), 0)
    column = lax.broadcasted_iota(jnp.int32, (128, 128), 1)
    return (row == column).astype(BF)


def transposed(a):
    return nt(identity(), a).astype(BF)


def table(count, ids):
    rows = lax.broadcasted_iota(jnp.int32, (count, ids.shape[1]), 0)
    return (rows == ids).astype(BF)


def silu_parts(x):
    s = 0.5 * jnp.tanh(0.5 * x) + 0.5
    return x * s, s * (1.0 + x * (1.0 - s))


def spans(total, size):
    return [slice(first, first + size) for first in range(0, total, size)]


def fetched(pairs, sems):
    copies = [pltpu.make_async_copy(a, b, sems.at[k]) for k, (a, b) in enumerate(pairs)]
    for copy in copies:
        copy.start()
    return copies


def bound_kernel(lat_hbm, bnd_hbm, low_ref, high_ref, lat_t_ref, bound_t_ref, lat, bnd, sems):
    for copy in fetched([(lat_hbm, lat), (bnd_hbm, bnd)], sems):
        copy.wait()
    rows_dev = lat.shape[0]
    low_ref[...] = lat[:HB, :]
    high_ref[...] = lat[rows_dev - HB :, :]
    lat_t = transposed(lat[...])
    lat_t_ref[...] = lat_t
    bound_t_ref[...] = nn(lat_t, table(rows_dev, bnd[...])).astype(BF)


def gather_kernel(lat_t_ref, edges_ref, send_ref, recv_ref):
    rows_dev = lat_t_ref.shape[1]
    for at in spans(edges_ref.shape[1], MESH_SPAN):
        send_ref[:, at] = nn(lat_t_ref[...], table(rows_dev, edges_ref[0:1, at] - HB)).astype(BF)
        recv_ref[:, at] = nn(lat_t_ref[...], table(rows_dev, edges_ref[1:2, at])).astype(BF)


def mesh_kernel(
    before_ref, after_ref, own_ref, recv_ref, edges_ref, w_ref, feats_ref,
    send_ref, slope_ref, agg_ref, sum_ref,
):
    rows_dev = agg_ref.shape[0]
    rim_t = transposed(jnp.concatenate([before_ref[...], after_ref[...]], axis=0))
    w0_t, w1_t, w2_t = transposed(w_ref[0]), transposed(w_ref[1]), transposed(w_ref[2])
    for at in spans(edges_ref.shape[1], MESH_SPAN):
        ids = edges_ref[0:1, at]
        ids = jnp.where(ids < HB, ids, jnp.where(ids < HB + rows_dev, -1, ids - rows_dev))
        rim_rows = nn(rim_t, table(2 * HB, ids))
        send_ref[:, at] = (own_ref[:, at].astype(F32) + rim_rows).astype(BF)
        x = nn(w0_t, send_ref[:, at]) + nn(w1_t, recv_ref[:, at]) + nt(w2_t, feats_ref[at, :])
        message, slope = silu_parts(x)
        slope_ref[:, at] = slope
        part = nt(table(rows_dev, edges_ref[1:2, at]), message.astype(BF))
        if at.start:
            part = part + sum_ref[...]
        sum_ref[...] = part
    agg_ref[...] = sum_ref[...].astype(BF)


def contact_round(count, bound_t, far_t, w_t, self_ids, far_ids, both_ref, slope_ref, at):
    slots = bound_t.shape[1]
    place = lax.broadcasted_iota(jnp.int32, self_ids.shape, 1)
    live = (place < count).astype(F32)
    hits = table(slots, self_ids)
    both_ref[:128, at] = nn(bound_t, hits).astype(BF)
    both_ref[128:, at] = nn(far_t, table(slots, far_ids)).astype(BF)
    message, slope = silu_parts(nn(w_t, both_ref[:, at]))
    slope_ref[:, at] = slope * live
    return nt(hits, (message * live).astype(BF))


def contact_kernel(
    counts_ref, bound_t_ref, far0_ref, far1_ref, far2_ref, w_ref, contacts_ref,
    both_ref, slope_ref, sum_ref,
):
    fars = (far0_ref, far1_ref, far2_ref)
    w_t = jnp.concatenate([transposed(w_ref[3]), transposed(w_ref[4])], axis=1)
    round_rows = both_ref.shape[1] // len(fars)
    for r, at in enumerate(spans(both_ref.shape[1], round_rows)):
        part = contact_round(
            counts_ref[0, r], bound_t_ref[...], fars[r][...], w_t,
            contacts_ref[0:1, at], contacts_ref[1:2, at], both_ref, slope_ref, at,
        )
        sum_ref[...] = part + sum_ref[...] if r else part


def main_kernel(
    counts_ref, core_ref, lat_ref, lat_t_ref, bound_t_ref, far3_ref, both_ref, slope_c_ref,
    aggb_ref, send_ref, recv_ref, slope_m_ref, agg_ref, feats_ref, cot_ref, w_ref, edges_ref,
    contacts_ref, bnd_ref,
    new_ref, kept_ref, sent_ref, dm_ref, dc_ref, dn_ref,
    slope_l_ref, both_l_ref, gw_ref, aggc_ref, dagg_t_ref, daggc_t_ref,
    *, scale,
):
    rows_dev = lat_ref.shape[0]
    bound_count = bnd_ref.shape[1]
    round_rows = both_l_ref.shape[1]
    last = contacts_ref.shape[1] // round_rows - 1
    w_t = jnp.concatenate([transposed(w_ref[3]), transposed(w_ref[4])], axis=1)
    at = slice(last * round_rows, (last + 1) * round_rows)
    aggb = aggb_ref[...] + contact_round(
        counts_ref[0, last], bound_t_ref[...], far3_ref[...], w_t,
        contacts_ref[0:1, at], contacts_ref[1:2, at], both_l_ref, slope_l_ref, slice(None),
    )

    bound_table = table(rows_dev, bnd_ref[...])
    aggc_ref[...] = nn(bound_table, aggb.astype(BF)).astype(BF)
    for at in spans(rows_dev, NODE_SPAN):
        lat = lat_ref[at, :]
        cot = cot_ref[at, :]
        agg = agg_ref[at, :]
        aggc = aggc_ref[at, :]
        x = nn(lat, w_ref[5]) + nn(agg, w_ref[6]) + nn(aggc, w_ref[7])
        message, slope = silu_parts(x)
        hidden = message.astype(BF)
        new_ref[at, :] = (lat.astype(F32) + nn(hidden, w_ref[8])).astype(BF)
        d_node = (nt(cot, w_ref[8]) * slope).astype(BF)
        dn_ref[at, :] = d_node
        dagg_t_ref[:, at] = nt(w_ref[6], d_node).astype(BF)
        daggc_t_ref[:, at] = nt(w_ref[7], d_node).astype(BF)
        parts = [
            nn(lat_t_ref[:, at], d_node), tn(agg, d_node), tn(aggc, d_node), tn(hidden, cot)
        ]
        for k, part in enumerate(parts):
            where = slice(640 + 128 * k, 768 + 128 * k)
            gw_ref[where, :] = part + gw_ref[where, :] if at.start else part

    for at in spans(edges_ref.shape[1], MESH_SPAN):
        gathered = nn(dagg_t_ref[...], table(rows_dev, edges_ref[1:2, at]))
        d = (gathered * slope_m_ref[:, at]).astype(BF)
        dm_ref[:, at] = d
        parts = [nt(send_ref[:, at], d), nt(recv_ref[:, at], d), nn(d, feats_ref[at, :])]
        for k, part in enumerate(parts):
            where = slice(128 * k, 128 * k + 128)
            gw_ref[where, :] = part + gw_ref[where, :] if at.start else part

    gw_ref[256:384, :] = gw_ref[256:384, :].T
    dbg_t = nn(daggc_t_ref[...], bound_table).astype(BF)
    for r, at in enumerate(spans(contacts_ref.shape[1], round_rows)):
        gathered = nn(dbg_t, table(bound_count, contacts_ref[0:1, at]))
        slope = slope_l_ref[...] if r == last else slope_c_ref[:, at]
        both = both_l_ref[...] if r == last else both_ref[:, at]
        d = (gathered * slope).astype(BF)
        dc_ref[:, at] = d
        pair = nt(both, d)
        gw_ref[384:640, :] = pair + gw_ref[384:640, :] if r else pair

    half = gw_ref.shape[0] // 2
    core = core_ref[0]
    kept_ref[...] = gw_ref[pl.ds(pl.multiple_of(core * half, 64), half), :] * scale
    sent = gw_ref[pl.ds(pl.multiple_of((1 - core) * half, 64), half), :] * scale
    sent_ref[...] = sent.astype(BF)


def contact_back_kernel(
    w_ref, contacts_ref, dc_ref, far0_ref, far1_ref, far2_ref, far3_ref, own_ref
):
    outs = (far0_ref, far1_ref, far2_ref, far3_ref)
    bound_count = own_ref.shape[0]
    for r, at in enumerate(spans(contacts_ref.shape[1], contacts_ref.shape[1] // len(outs))):
        d = dc_ref[:, at]
        part = nt(table(bound_count, contacts_ref[0:1, at]), d)
        own_ref[...] = part + own_ref[...] if r else part
        far = nt(table(bound_count, contacts_ref[1:2, at]), d)
        outs[r][...] = wide_nt(far, w_ref[4]).astype(BF)
    own_ref[...] = wide_nt(own_ref[...], w_ref[3])


def send_back_kernel(w_ref, edges_ref, dm_ref, part_ref, low_ref, high_ref, send_ref):
    rows_dev = part_ref.shape[0]
    for at in spans(edges_ref.shape[1], MESH_SPAN):
        send = nt(table(rows_dev + 2 * HB, edges_ref[0:1, at]), dm_ref[:, at])
        send_ref[...] = send + send_ref[...] if at.start else send
    low_ref[...] = wide_nt(send_ref[:HB, :], w_ref[0]).astype(BF)
    high_ref[...] = wide_nt(send_ref[HB + rows_dev :, :], w_ref[0]).astype(BF)
    part_ref[...] = wide_nt(send_ref[HB : HB + rows_dev, :], w_ref[0])


def recv_back_kernel(w_ref, edges_ref, dm_ref, dn_ref, cot_ref, part_ref, grad_ref, recv_ref):
    rows_dev = cot_ref.shape[0]
    for at in spans(edges_ref.shape[1], MESH_SPAN):
        recv = nt(table(rows_dev, edges_ref[1:2, at]), dm_ref[:, at])
        recv_ref[...] = recv + recv_ref[...] if at.start else recv
    grad_ref[...] = (
        cot_ref[...].astype(F32)
        + nt(dn_ref[...], w_ref[5])
        + wide_nt(recv_ref[...], w_ref[1])
        + part_ref[...]
    )


def last_kernel(
    part_ref, own_ref, in0_ref, in1_ref, in2_ref, in3_ref, prev_ref, next_ref, bnd_ref, out_ref
):
    rows_dev = part_ref.shape[0]
    total = own_ref[...]
    for ref in (in0_ref, in1_ref, in2_ref, in3_ref):
        total = total + ref[...].astype(F32)
    out_ref[...] = part_ref[...] + wide_nn(table(rows_dev, bnd_ref[...]), total)
    out_ref[:HB, :] += prev_ref[...].astype(F32)
    out_ref[rows_dev - HB :, :] += next_ref[...].astype(F32)


def call(kernel, outs, args, scratch=(), smem=0, hbm=0, flops=0, mib=32):
    spec = pl.BlockSpec(memory_space=pltpu.VMEM)
    plain = len(args) - smem - hbm
    in_specs = [pl.BlockSpec(memory_space=pltpu.SMEM)] * smem + [spec] * plain
    in_specs += [pl.BlockSpec(memory_space=pltpu.HBM)] * hbm
    scratch_shapes = [pltpu.VMEM(shape, kind) for shape, kind in scratch]
    if hbm:
        scratch_shapes.append(pltpu.SemaphoreType.DMA((hbm,)))
    return pl.pallas_call(
        kernel,
        out_shape=[jax.ShapeDtypeStruct(shape, kind) for shape, kind in outs],
        in_specs=in_specs,
        out_specs=[spec] * len(outs),
        scratch_shapes=scratch_shapes,
        compiler_params=pltpu.CompilerParams(vmem_limit_bytes=mib * MIB),
        cost_estimate=pl.CostEstimate(flops=flops, bytes_accessed=4000000, transcendentals=0),
    )(*args)


def exchanged(block, mask_x=0, mask_y=0, mask_z=0, mask_core=0):
    route = []
    for region in range(32):
        for panel in range(8):
            other_region = region ^ ((mask_x >> 1) << 4 | mask_z << 1 | mask_core)
            other_panel = panel ^ ((mask_x & 1) << 2 | mask_y)
            route.append((region * 8 + panel, other_region * 8 + other_panel))
    return lax.ppermute(block, ("region", "panel"), route)


def swapped(block, bit):
    size = lax.axis_size("region")
    return lax.ppermute(block, "region", [(i, i ^ (1 << bit)) for i in range(size)])


def shifted(array, by):
    length = lax.axis_size("panel")
    pairs = [(i, i + by) for i in range(length) if 0 <= i + by < length]
    return lax.ppermute(array, "panel", pairs)


def wide(block):
    return block.astype(F32)


def ordered_by_y(found, row_y):
    odd, high = row_y % 2 == 1, row_y >= 2
    low_pair = [jnp.where(odd, found[1], found[0]), jnp.where(odd, found[0], found[1])]
    high_pair = [jnp.where(odd, found[3], found[2]), jnp.where(odd, found[2], found[3])]
    ordered = [jnp.where(high, b, a) for a, b in zip(low_pair, high_pair)]
    ordered += [jnp.where(high, a, b) for a, b in zip(low_pair, high_pair)]
    return jnp.concatenate(ordered, axis=0)


def joined(own, other, which):
    first = jnp.where(which == 0, own, other)
    second = jnp.where(which == 0, other, own)
    return jnp.concatenate([first, second], axis=0)


def tie(*arrays):
    return lax.optimization_barrier(arrays)


def shards(
    latents, edge_feats, weights, cotangent, mesh_edges, boundary, contact_edges, contact_counts
):
    rows_dev, width = latents.shape
    bound_count = boundary.shape[0]
    rounds = contact_counts.shape[1]
    edge_count = mesh_edges.shape[1]
    contact_count = contact_edges.shape[1]
    bnd = boundary.reshape(1, bound_count)
    core = lax.axis_index("region") % 2
    row_y = lax.axis_index("panel") % 4
    scale = 1.0 / math.sqrt(rows_dev * lax.axis_size("region") * lax.axis_size("panel"))

    low_rows, high_rows, lat_t, bound_t = call(
        bound_kernel,
        [((HB, width), BF), ((HB, width), BF), ((width, rows_dev), BF), ((width, bound_count), BF)],
        [latents, bnd],
        [((rows_dev, width), BF), ((1, bound_count), jnp.int32)],
        hbm=2,
        flops=10**10,
        mib=8,
    )
    before = shifted(high_rows, 1)
    after = shifted(low_rows, -1)
    fars = [exchanged(bound_t, mask_core=1)]
    fars += [exchanged(bound_t, mask_z=mask) for mask in (1, 2, 4)]
    own_rows, recv_rows = call(
        gather_kernel,
        [((width, edge_count), BF), ((width, edge_count), BF)],
        [lat_t, mesh_edges],
        flops=4 * 10**9,
        mib=16,
    )
    before, after, own_rows = tie(before, after, own_rows)
    send_rows, slope, agg = call(
        mesh_kernel,
        [((width, edge_count), BF), ((width, edge_count), F32), ((rows_dev, width), BF)],
        [before, after, own_rows, recv_rows, mesh_edges, weights, edge_feats],
        [((rows_dev, width), F32)],
        flops=3 * 10**9,
        mib=16,
    )
    first = (rounds - 1) * contact_count // rounds
    both, slope_c, aggb = call(
        contact_kernel,
        [((2 * width, first), BF), ((width, first), F32), ((bound_count, width), F32)],
        [contact_counts, bound_t, *fars[:3], weights, contact_edges],
        smem=1,
        flops=3 * 10**9,
        mib=16,
    )
    fars[3], both = tie(fars[3], both)
    new_rows, kept, sent, d_mesh, d_contact, d_node = call(
        functools.partial(main_kernel, scale=scale),
        [
            ((rows_dev, width), BF),
            ((9 * width // 2, width), F32),
            ((9 * width // 2, width), BF),
            ((width, edge_count), BF),
            ((width, contact_count), BF),
            ((rows_dev, width), BF),
        ],
        [contact_counts, core.reshape(1), latents, lat_t, bound_t, fars[3], both, slope_c, aggb]
        + [send_rows, recv_rows, slope, agg]
        + [edge_feats, cotangent, weights, mesh_edges, contact_edges, bnd],
        [
            ((width, contact_count // rounds), F32),
            ((2 * width, contact_count // rounds), BF),
            ((9 * width, width), F32),
            ((rows_dev, width), BF),
            ((width, rows_dev), BF),
            ((width, rows_dev), BF),
        ],
        smem=2,
        flops=6 * 10**9,
        mib=20,
    )
    other = exchanged(sent, mask_core=1)
    *far_grads, own_grad = call(
        contact_back_kernel,
        [((bound_count, width), BF)] * rounds + [((bound_count, width), F32)],
        [weights, contact_edges, d_contact],
        flops=2 * 10**9,
        mib=16,
    )
    other, *far_grads = tie(other, *far_grads)
    block = kept + wide(other)
    size = block.shape[0] // 4
    pieces = [
        lax.dynamic_slice_in_dim(block, (row_y ^ mask) * size, size, 0) for mask in range(4)
    ]
    found = [exchanged(pieces[mask].astype(BF), mask_y=mask) for mask in (1, 2, 3)]
    pair = exchanged(jnp.concatenate(far_grads[2:], axis=0), mask_z=2)
    in_one = exchanged(far_grads[1], mask_z=1)
    one, two, three, d_mesh = tie(*found, d_mesh)
    block = ((pieces[0] + wide(one)) + (wide(two) + wide(three))).astype(BF)

    other = exchanged(block, mask_z=1)
    part, low, high = call(
        send_back_kernel,
        [((rows_dev, width), F32), ((HB, width), BF), ((HB, width), BF)],
        [weights, mesh_edges, d_mesh],
        [((rows_dev + 2 * HB, width), F32)],
        flops=2 * 10**9,
        mib=16,
    )
    other, part, low, high, in_one = tie(other, part, low, high, in_one)
    block = (wide(block) + wide(other)).astype(BF)
    other = exchanged(block, mask_z=2)
    (part,) = call(
        recv_back_kernel,
        [((rows_dev, width), F32)],
        [weights, mesh_edges, d_mesh, d_node, cotangent, part],
        [((rows_dev, width), F32)],
        flops=2 * 10**9,
        mib=16,
    )
    other, part, pair = tie(other, part, pair)
    block = (wide(block) + wide(other)).astype(BF)
    other = exchanged(block, mask_z=6)
    in_two = pair[:bound_count]
    in_three = exchanged(pair[bound_count:], mask_z=6)
    in_zero = exchanged(far_grads[0], mask_core=1)
    other, in_zero = tie(other, in_zero)
    block = (wide(block) + wide(other)).astype(BF)

    rim = jnp.where(row_y == 0, low, high)
    one = exchanged(jnp.concatenate([block, rim], axis=0), mask_x=1)
    two, three = [exchanged(block, mask_x=mask) for mask in (2, 3)]
    one, two, three, in_three = tie(one, two, three, in_three)
    rim = one[size:]
    block = ((wide(block) + wide(one[:size])) + (wide(two) + wide(three))).astype(BF)

    rim = jnp.where(row_y == 1, high, jnp.where(row_y == 2, low, rim))
    three = exchanged(jnp.concatenate([block, rim], axis=0), mask_y=3)
    rim = jnp.where(row_y % 2 == 0, high, low)
    one = exchanged(jnp.concatenate([block, rim], axis=0), mask_y=1)
    two = exchanged(block, mask_y=2)
    one, two, three = tie(one, two, three)
    panel = lax.axis_index("panel")
    nothing = jnp.zeros_like(rim)
    from_prev = jnp.where(row_y % 2 == 0, three[size:], one[size:])
    from_prev = jnp.where(panel == 0, nothing, from_prev)
    from_next = jnp.where(row_y % 2 == 0, one[size:], three[size:])
    from_next = jnp.where(panel == lax.axis_size("panel") - 1, nothing, from_next)
    block = ordered_by_y([block, one[:size], two, three[:size]], row_y)
    other = exchanged(block, mask_core=1)
    (grad_rows,) = call(
        last_kernel,
        [((rows_dev, width), F32)],
        [part, own_grad, in_zero, in_one, in_two, in_three, from_prev, from_next, bnd],
        flops=10**8,
        mib=8,
    )
    block = joined(wide(block), wide(other), core)
    return (new_rows, grad_rows, block.reshape(9, width, width))


def solution(mesh):
    blocks = P(("region", "panel"), None)
    placed = (
        blocks,
        blocks,
        P(),
        blocks,
        P(None, ("region", "panel")),
        P(("region", "panel")),
        P(None, ("region", "panel")),
        blocks,
    )
    return jax.shard_map(
        shards, mesh=mesh, in_specs=placed, out_specs=(blocks, blocks, P()), check_vma=False
    )
```

```python
import functools
import math

import jax
import jax.numpy as jnp
from jax import lax
from jax.experimental import pallas as pl
from jax.experimental.pallas import tpu as pltpu
from jax.sharding import PartitionSpec as P

HB = 64
BF = jnp.bfloat16
F32 = jnp.float32
MESH_SPAN = 1536
NODE_SPAN = 512
MIB = 1024 * 1024


def nn(a, b):
    return lax.dot_general(a, b, (((1,), (0,)), ((), ())), preferred_element_type=F32)


def nt(a, b):
    return lax.dot_general(a, b, (((1,), (1,)), ((), ())), preferred_element_type=F32)


def tn(a, b):
    return lax.dot_general(a, b, (((0,), (0,)), ((), ())), preferred_element_type=F32)


def in_two(values):
    high = values.astype(BF)
    return high, (values - high.astype(F32)).astype(BF)


def wide_nt(a, b):
    high, low = in_two(a)
    return nt(high, b) + nt(low, b)


def wide_nn(a, b):
    high, low = in_two(b)
    return nn(a, high) + nn(a, low)


def identity():
    row = lax.broadcasted_iota(jnp.int32, (128, 128), 0)
    column = lax.broadcasted_iota(jnp.int32, (128, 128), 1)
    return (row == column).astype(BF)


def transposed(a):
    return nt(identity(), a).astype(BF)


def table(count, ids):
    rows = lax.broadcasted_iota(jnp.int32, (count, ids.shape[1]), 0)
    return (rows == ids).astype(BF)


def silu_parts(x):
    s = 0.5 * jnp.tanh(0.5 * x) + 0.5
    return x * s, s * (1.0 + x * (1.0 - s))


def spans(total, size):
    return [slice(first, first + size) for first in range(0, total, size)]


def fetched(pairs, sems):
    copies = [pltpu.make_async_copy(a, b, sems.at[k]) for k, (a, b) in enumerate(pairs)]
    for copy in copies:
        copy.start()
    return copies


def bound_kernel(lat_hbm, bnd_hbm, low_ref, high_ref, lat_t_ref, bound_t_ref, lat, bnd, sems):
    for copy in fetched([(lat_hbm, lat), (bnd_hbm, bnd)], sems):
        copy.wait()
    rows_dev = lat.shape[0]
    low_ref[...] = lat[:HB, :]
    high_ref[...] = lat[rows_dev - HB :, :]
    lat_t = transposed(lat[...])
    lat_t_ref[...] = lat_t
    bound_t_ref[...] = nn(lat_t, table(rows_dev, bnd[...])).astype(BF)


def gather_kernel(lat_t_ref, edges_ref, send_ref, recv_ref):
    rows_dev = lat_t_ref.shape[1]
    for at in spans(edges_ref.shape[1], MESH_SPAN):
        send_ref[:, at] = nn(lat_t_ref[...], table(rows_dev, edges_ref[0:1, at] - HB)).astype(BF)
        recv_ref[:, at] = nn(lat_t_ref[...], table(rows_dev, edges_ref[1:2, at])).astype(BF)


def mesh_kernel(
    before_ref, after_ref, own_ref, recv_ref, edges_ref, w_ref, feats_ref,
    send_ref, slope_ref, agg_ref, sum_ref,
):
    rows_dev = agg_ref.shape[0]
    rim_t = transposed(jnp.concatenate([before_ref[...], after_ref[...]], axis=0))
    w0_t, w1_t, w2_t = transposed(w_ref[0]), transposed(w_ref[1]), transposed(w_ref[2])
    for at in spans(edges_ref.shape[1], MESH_SPAN):
        ids = edges_ref[0:1, at]
        ids = jnp.where(ids < HB, ids, jnp.where(ids < HB + rows_dev, -1, ids - rows_dev))
        rim_rows = nn(rim_t, table(2 * HB, ids))
        send_ref[:, at] = (own_ref[:, at].astype(F32) + rim_rows).astype(BF)
        x = nn(w0_t, send_ref[:, at]) + nn(w1_t, recv_ref[:, at]) + nt(w2_t, feats_ref[at, :])
        message, slope = silu_parts(x)
        slope_ref[:, at] = slope
        part = nt(table(rows_dev, edges_ref[1:2, at]), message.astype(BF))
        if at.start:
            part = part + sum_ref[...]
        sum_ref[...] = part
    agg_ref[...] = sum_ref[...].astype(BF)


def contact_round(count, bound_t, far_t, w_t, self_ids, far_ids, both_ref, slope_ref, at):
    slots = bound_t.shape[1]
    place = lax.broadcasted_iota(jnp.int32, self_ids.shape, 1)
    live = (place < count).astype(F32)
    hits = table(slots, self_ids)
    both_ref[:128, at] = nn(bound_t, hits).astype(BF)
    both_ref[128:, at] = nn(far_t, table(slots, far_ids)).astype(BF)
    message, slope = silu_parts(nn(w_t, both_ref[:, at]))
    slope_ref[:, at] = slope * live
    return nt(hits, (message * live).astype(BF))


def contact_kernel(
    counts_ref, bound_t_ref, far0_ref, far1_ref, far2_ref, w_ref, contacts_ref,
    both_ref, slope_ref, sum_ref,
):
    fars = (far0_ref, far1_ref, far2_ref)
    w_t = jnp.concatenate([transposed(w_ref[3]), transposed(w_ref[4])], axis=1)
    round_rows = both_ref.shape[1] // len(fars)
    for r, at in enumerate(spans(both_ref.shape[1], round_rows)):
        part = contact_round(
            counts_ref[0, r], bound_t_ref[...], fars[r][...], w_t,
            contacts_ref[0:1, at], contacts_ref[1:2, at], both_ref, slope_ref, at,
        )
        sum_ref[...] = part + sum_ref[...] if r else part


def main_kernel(
    counts_ref, lat_ref, lat_t_ref, bound_t_ref, far3_ref, both_ref, slope_c_ref,
    aggb_ref, send_ref, recv_ref, slope_m_ref, agg_ref, feats_ref, cot_ref, w_ref, edges_ref,
    contacts_ref, bnd_ref,
    new_ref, kept_ref, sent_ref, dm_ref, dc_ref, dn_ref,
    slope_l_ref, both_l_ref, gw_ref, aggc_ref, dagg_t_ref, daggc_t_ref,
    *, scale,
):
    rows_dev = lat_ref.shape[0]
    bound_count = bnd_ref.shape[1]
    round_rows = both_l_ref.shape[1]
    last = contacts_ref.shape[1] // round_rows - 1
    w_t = jnp.concatenate([transposed(w_ref[3]), transposed(w_ref[4])], axis=1)
    at = slice(last * round_rows, (last + 1) * round_rows)
    aggb = aggb_ref[...] + contact_round(
        counts_ref[0, last], bound_t_ref[...], far3_ref[...], w_t,
        contacts_ref[0:1, at], contacts_ref[1:2, at], both_l_ref, slope_l_ref, slice(None),
    )

    bound_table = table(rows_dev, bnd_ref[...])
    aggc_ref[...] = nn(bound_table, aggb.astype(BF)).astype(BF)
    for at in spans(rows_dev, NODE_SPAN):
        lat = lat_ref[at, :]
        cot = cot_ref[at, :]
        agg = agg_ref[at, :]
        aggc = aggc_ref[at, :]
        x = nn(lat, w_ref[5]) + nn(agg, w_ref[6]) + nn(aggc, w_ref[7])
        message, slope = silu_parts(x)
        hidden = message.astype(BF)
        new_ref[at, :] = (lat.astype(F32) + nn(hidden, w_ref[8])).astype(BF)
        d_node = (nt(cot, w_ref[8]) * slope).astype(BF)
        dn_ref[at, :] = d_node
        dagg_t_ref[:, at] = nt(w_ref[6], d_node).astype(BF)
        daggc_t_ref[:, at] = nt(w_ref[7], d_node).astype(BF)
        parts = [
            nn(lat_t_ref[:, at], d_node), tn(agg, d_node), tn(aggc, d_node), tn(hidden, cot)
        ]
        for k, part in enumerate(parts):
            where = slice(640 + 128 * k, 768 + 128 * k)
            gw_ref[where, :] = part + gw_ref[where, :] if at.start else part

    for at in spans(edges_ref.shape[1], MESH_SPAN):
        gathered = nn(dagg_t_ref[...], table(rows_dev, edges_ref[1:2, at]))
        d = (gathered * slope_m_ref[:, at]).astype(BF)
        dm_ref[:, at] = d
        parts = [nt(send_ref[:, at], d), nt(recv_ref[:, at], d), nn(d, feats_ref[at, :])]
        for k, part in enumerate(parts):
            where = slice(128 * k, 128 * k + 128)
            gw_ref[where, :] = part + gw_ref[where, :] if at.start else part

    gw_ref[256:384, :] = gw_ref[256:384, :].T
    dbg_t = nn(daggc_t_ref[...], bound_table).astype(BF)
    for r, at in enumerate(spans(contacts_ref.shape[1], round_rows)):
        gathered = nn(dbg_t, table(bound_count, contacts_ref[0:1, at]))
        slope = slope_l_ref[...] if r == last else slope_c_ref[:, at]
        both = both_l_ref[...] if r == last else both_ref[:, at]
        d = (gathered * slope).astype(BF)
        dc_ref[:, at] = d
        pair = nt(both, d)
        gw_ref[384:640, :] = pair + gw_ref[384:640, :] if r else pair

    total = gw_ref[...] * scale
    kept_ref[...] = total
    sent_ref[...] = total.astype(BF)


def contact_back_kernel(
    w_ref, contacts_ref, dc_ref, far0_ref, far1_ref, far2_ref, far3_ref, own_ref
):
    outs = (far0_ref, far1_ref, far2_ref, far3_ref)
    bound_count = own_ref.shape[0]
    for r, at in enumerate(spans(contacts_ref.shape[1], contacts_ref.shape[1] // len(outs))):
        d = dc_ref[:, at]
        part = nt(table(bound_count, contacts_ref[0:1, at]), d)
        own_ref[...] = part + own_ref[...] if r else part
        far = nt(table(bound_count, contacts_ref[1:2, at]), d)
        outs[r][...] = wide_nt(far, w_ref[4]).astype(BF)
    own_ref[...] = wide_nt(own_ref[...], w_ref[3])


def send_back_kernel(w_ref, edges_ref, dm_ref, part_ref, low_ref, high_ref, send_ref):
    rows_dev = part_ref.shape[0]
    for at in spans(edges_ref.shape[1], MESH_SPAN):
        send = nt(table(rows_dev + 2 * HB, edges_ref[0:1, at]), dm_ref[:, at])
        send_ref[...] = send + send_ref[...] if at.start else send
    low_ref[...] = wide_nt(send_ref[:HB, :], w_ref[0]).astype(BF)
    high_ref[...] = wide_nt(send_ref[HB + rows_dev :, :], w_ref[0]).astype(BF)
    part_ref[...] = wide_nt(send_ref[HB : HB + rows_dev, :], w_ref[0])


def recv_back_kernel(w_ref, edges_ref, dm_ref, dn_ref, cot_ref, part_ref, grad_ref, recv_ref):
    rows_dev = cot_ref.shape[0]
    for at in spans(edges_ref.shape[1], MESH_SPAN):
        recv = nt(table(rows_dev, edges_ref[1:2, at]), dm_ref[:, at])
        recv_ref[...] = recv + recv_ref[...] if at.start else recv
    grad_ref[...] = (
        cot_ref[...].astype(F32)
        + nt(dn_ref[...], w_ref[5])
        + wide_nt(recv_ref[...], w_ref[1])
        + part_ref[...]
    )


def last_kernel(
    part_ref, own_ref, in0_ref, in1_ref, in2_ref, in3_ref, prev_ref, next_ref, bnd_ref, out_ref
):
    rows_dev = part_ref.shape[0]
    total = own_ref[...]
    for ref in (in0_ref, in1_ref, in2_ref, in3_ref):
        total = total + ref[...].astype(F32)
    out_ref[...] = part_ref[...] + wide_nn(table(rows_dev, bnd_ref[...]), total)
    out_ref[:HB, :] += prev_ref[...].astype(F32)
    out_ref[rows_dev - HB :, :] += next_ref[...].astype(F32)


def call(kernel, outs, args, scratch=(), smem=0, hbm=0, flops=0, mib=32):
    spec = pl.BlockSpec(memory_space=pltpu.VMEM)
    plain = len(args) - smem - hbm
    in_specs = [pl.BlockSpec(memory_space=pltpu.SMEM)] * smem + [spec] * plain
    in_specs += [pl.BlockSpec(memory_space=pltpu.HBM)] * hbm
    scratch_shapes = [pltpu.VMEM(shape, kind) for shape, kind in scratch]
    if hbm:
        scratch_shapes.append(pltpu.SemaphoreType.DMA((hbm,)))
    return pl.pallas_call(
        kernel,
        out_shape=[jax.ShapeDtypeStruct(shape, kind) for shape, kind in outs],
        in_specs=in_specs,
        out_specs=[spec] * len(outs),
        scratch_shapes=scratch_shapes,
        compiler_params=pltpu.CompilerParams(vmem_limit_bytes=mib * MIB),
        cost_estimate=pl.CostEstimate(flops=flops, bytes_accessed=4000000, transcendentals=0),
    )(*args)


def exchanged(block, mask_x=0, mask_y=0, mask_z=0, mask_core=0, only_core=None):
    route = []
    for region in range(32):
        if only_core is not None and region % 2 != only_core:
            continue
        for panel in range(8):
            other_region = region ^ ((mask_x >> 1) << 4 | mask_z << 1 | mask_core)
            other_panel = panel ^ ((mask_x & 1) << 2 | mask_y)
            route.append((region * 8 + panel, other_region * 8 + other_panel))
    return lax.ppermute(block, ("region", "panel"), route)


def shifted(array, by):
    length = lax.axis_size("panel")
    pairs = [(i, i + by) for i in range(length) if 0 <= i + by < length]
    return lax.ppermute(array, "panel", pairs)


def wide(block):
    return block.astype(F32)


def ordered_by_y(found, row_y):
    odd, high = row_y % 2 == 1, row_y >= 2
    low_pair = [jnp.where(odd, found[1], found[0]), jnp.where(odd, found[0], found[1])]
    high_pair = [jnp.where(odd, found[3], found[2]), jnp.where(odd, found[2], found[3])]
    ordered = [jnp.where(high, b, a) for a, b in zip(low_pair, high_pair)]
    ordered += [jnp.where(high, a, b) for a, b in zip(low_pair, high_pair)]
    return jnp.concatenate(ordered, axis=0)


def tie(*arrays):
    return lax.optimization_barrier(arrays)


def shards(
    latents, edge_feats, weights, cotangent, mesh_edges, boundary, contact_edges, contact_counts
):
    rows_dev, width = latents.shape
    bound_count = boundary.shape[0]
    rounds = contact_counts.shape[1]
    edge_count = mesh_edges.shape[1]
    contact_count = contact_edges.shape[1]
    bnd = boundary.reshape(1, bound_count)
    core = lax.axis_index("region") % 2
    row_y = lax.axis_index("panel") % 4
    scale = 1.0 / math.sqrt(rows_dev * lax.axis_size("region") * lax.axis_size("panel"))

    low_rows, high_rows, lat_t, bound_t = call(
        bound_kernel,
        [((HB, width), BF), ((HB, width), BF), ((width, rows_dev), BF), ((width, bound_count), BF)],
        [latents, bnd],
        [((rows_dev, width), BF), ((1, bound_count), jnp.int32)],
        hbm=2,
        flops=10**10,
        mib=8,
    )
    before = shifted(high_rows, 1)
    after = shifted(low_rows, -1)
    fars = [exchanged(bound_t, mask_core=1)]
    fars += [exchanged(bound_t, mask_z=mask) for mask in (1, 2, 4)]
    own_rows, recv_rows = call(
        gather_kernel,
        [((width, edge_count), BF), ((width, edge_count), BF)],
        [lat_t, mesh_edges],
        flops=4 * 10**9,
        mib=16,
    )
    before, after, own_rows = tie(before, after, own_rows)
    send_rows, slope, agg = call(
        mesh_kernel,
        [((width, edge_count), BF), ((width, edge_count), F32), ((rows_dev, width), BF)],
        [before, after, own_rows, recv_rows, mesh_edges, weights, edge_feats],
        [((rows_dev, width), F32)],
        flops=3 * 10**9,
        mib=16,
    )
    first = (rounds - 1) * contact_count // rounds
    both, slope_c, aggb = call(
        contact_kernel,
        [((2 * width, first), BF), ((width, first), F32), ((bound_count, width), F32)],
        [contact_counts, bound_t, *fars[:3], weights, contact_edges],
        smem=1,
        flops=3 * 10**9,
        mib=16,
    )
    fars[3], both = tie(fars[3], both)
    new_rows, kept, sent, d_mesh, d_contact, d_node = call(
        functools.partial(main_kernel, scale=scale),
        [
            ((rows_dev, width), BF),
            ((9 * width, width), F32),
            ((9 * width, width), BF),
            ((width, edge_count), BF),
            ((width, contact_count), BF),
            ((rows_dev, width), BF),
        ],
        [contact_counts, latents, lat_t, bound_t, fars[3], both, slope_c, aggb]
        + [send_rows, recv_rows, slope, agg]
        + [edge_feats, cotangent, weights, mesh_edges, contact_edges, bnd],
        [
            ((width, contact_count // rounds), F32),
            ((2 * width, contact_count // rounds), BF),
            ((9 * width, width), F32),
            ((rows_dev, width), BF),
            ((width, rows_dev), BF),
            ((width, rows_dev), BF),
        ],
        smem=1,
        flops=6 * 10**9,
        mib=20,
    )
    by = functools.partial(exchanged, only_core=1)
    other = exchanged(sent, mask_core=1, only_core=0)
    *far_grads, own_grad = call(
        contact_back_kernel,
        [((bound_count, width), BF)] * rounds + [((bound_count, width), F32)],
        [weights, contact_edges, d_contact],
        flops=2 * 10**9,
        mib=16,
    )
    other, *far_grads = tie(other, *far_grads)
    block = kept + wide(other)
    size = block.shape[0] // 4
    pieces = [
        lax.dynamic_slice_in_dim(block, (row_y ^ mask) * size, size, 0) for mask in range(4)
    ]
    found = [by(pieces[mask].astype(BF), mask_y=mask) for mask in (1, 2, 3)]
    pair = exchanged(jnp.concatenate(far_grads[2:], axis=0), mask_z=2)
    in_one = exchanged(far_grads[1], mask_z=1)
    one, two, three, d_mesh = tie(*found, d_mesh)
    block = ((pieces[0] + wide(one)) + (wide(two) + wide(three))).astype(BF)

    other = by(block, mask_z=1)
    part, low, high = call(
        send_back_kernel,
        [((rows_dev, width), F32), ((HB, width), BF), ((HB, width), BF)],
        [weights, mesh_edges, d_mesh],
        [((rows_dev + 2 * HB, width), F32)],
        flops=2 * 10**9,
        mib=16,
    )
    other, part, low, high, in_one = tie(other, part, low, high, in_one)
    block = (wide(block) + wide(other)).astype(BF)
    other = by(block, mask_z=2)
    rims = jnp.concatenate([low, high], axis=0)
    zero_rims = exchanged(rims, mask_core=1, only_core=0)
    (part,) = call(
        recv_back_kernel,
        [((rows_dev, width), F32)],
        [weights, mesh_edges, d_mesh, d_node, cotangent, part],
        [((rows_dev, width), F32)],
        flops=2 * 10**9,
        mib=16,
    )
    other, part, pair, zero_rims = tie(other, part, pair, zero_rims)
    block = (wide(block) + wide(other)).astype(BF)
    other = by(block, mask_z=6)
    in_two = pair[:bound_count]
    in_three = exchanged(pair[bound_count:], mask_z=6)
    in_zero = exchanged(far_grads[0], mask_core=1)
    other, in_zero = tie(other, in_zero)
    block = (wide(block) + wide(other)).astype(BF)

    low = jnp.concatenate([zero_rims[:HB], low], axis=0)
    high = jnp.concatenate([zero_rims[HB:], high], axis=0)
    rim = jnp.where(row_y == 0, low, high)
    one = by(jnp.concatenate([block, rim], axis=0), mask_x=1)
    two, three = [by(block, mask_x=mask) for mask in (2, 3)]
    one, two, three, in_three = tie(one, two, three, in_three)
    rim = one[size:]
    block = ((wide(block) + wide(one[:size])) + (wide(two) + wide(three))).astype(BF)

    rim = jnp.where(row_y == 1, high, jnp.where(row_y == 2, low, rim))
    three = by(jnp.concatenate([block, rim], axis=0), mask_y=3)
    rim = jnp.where(row_y % 2 == 0, high, low)
    one = by(jnp.concatenate([block, rim], axis=0), mask_y=1)
    two = by(block, mask_y=2)
    one, two, three = tie(one, two, three)
    panel = lax.axis_index("panel")
    nothing = jnp.zeros_like(rim)
    from_prev = jnp.where(row_y % 2 == 0, three[size:], one[size:])
    from_prev = jnp.where(panel == 0, nothing, from_prev)
    from_next = jnp.where(row_y % 2 == 0, one[size:], three[size:])
    from_next = jnp.where(panel == lax.axis_size("panel") - 1, nothing, from_next)
    zero_rims = by(jnp.concatenate([from_prev[:HB], from_next[:HB]], axis=0), mask_core=1)
    from_prev = jnp.where(core == 1, from_prev[HB:], zero_rims[:HB])
    from_next = jnp.where(core == 1, from_next[HB:], zero_rims[HB:])
    block = ordered_by_y([block, one[:size], two, three[:size]], row_y)
    other = by(block, mask_core=1)
    (grad_rows,) = call(
        last_kernel,
        [((rows_dev, width), F32)],
        [part, own_grad, in_zero, in_one, in_two, in_three, from_prev, from_next, bnd],
        flops=10**8,
        mib=8,
    )
    block = wide(jnp.where(core == 1, block, other))
    return (new_rows, grad_rows, block.reshape(9, width, width))


def solution(mesh):
    blocks = P(("region", "panel"), None)
    placed = (
        blocks,
        blocks,
        P(),
        blocks,
        P(None, ("region", "panel")),
        P(("region", "panel")),
        P(None, ("region", "panel")),
        blocks,
    )
    return jax.shard_map(
        shards, mesh=mesh, in_specs=placed, out_specs=(blocks, blocks, P()), check_vma=False
    )
```

```python
import functools
import math

import jax
import jax.numpy as jnp
from jax import lax
from jax.experimental import pallas as pl
from jax.experimental.pallas import tpu as pltpu
from jax.sharding import PartitionSpec as P

HB = 64
BF = jnp.bfloat16
F32 = jnp.float32
MESH_SPAN = 1536
NODE_SPAN = 512
MIB = 1024 * 1024


def nn(a, b):
    return lax.dot_general(a, b, (((1,), (0,)), ((), ())), preferred_element_type=F32)


def nt(a, b):
    return lax.dot_general(a, b, (((1,), (1,)), ((), ())), preferred_element_type=F32)


def tn(a, b):
    return lax.dot_general(a, b, (((0,), (0,)), ((), ())), preferred_element_type=F32)


def in_two(values):
    high = values.astype(BF)
    return high, (values - high.astype(F32)).astype(BF)


def wide_nt(a, b):
    high, low = in_two(a)
    return nt(high, b) + nt(low, b)


def wide_nn(a, b):
    high, low = in_two(b)
    return nn(a, high) + nn(a, low)


def identity():
    row = lax.broadcasted_iota(jnp.int32, (128, 128), 0)
    column = lax.broadcasted_iota(jnp.int32, (128, 128), 1)
    return (row == column).astype(BF)


def transposed(a):
    return nt(identity(), a).astype(BF)


def table(count, ids):
    rows = lax.broadcasted_iota(jnp.int32, (count, ids.shape[1]), 0)
    return (rows == ids).astype(BF)


def silu_parts(x):
    s = 0.5 * jnp.tanh(0.5 * x) + 0.5
    return x * s, s * (1.0 + x * (1.0 - s))


def spans(total, size):
    return [slice(first, first + size) for first in range(0, total, size)]


def fetched(pairs, sems):
    copies = [pltpu.make_async_copy(a, b, sems.at[k]) for k, (a, b) in enumerate(pairs)]
    for copy in copies:
        copy.start()
    return copies


def bound_kernel(lat_hbm, bnd_hbm, low_ref, high_ref, lat_t_ref, bound_t_ref, lat, bnd, sems):
    for copy in fetched([(lat_hbm, lat), (bnd_hbm, bnd)], sems):
        copy.wait()
    rows_dev = lat.shape[0]
    low_ref[...] = lat[:HB, :]
    high_ref[...] = lat[rows_dev - HB :, :]
    lat_t = transposed(lat[...])
    lat_t_ref[...] = lat_t
    bound_t_ref[...] = nn(lat_t, table(rows_dev, bnd[...])).astype(BF)


def gather_kernel(lat_t_ref, edges_ref, send_ref, recv_ref):
    rows_dev = lat_t_ref.shape[1]
    for at in spans(edges_ref.shape[1], MESH_SPAN):
        send_ref[:, at] = nn(lat_t_ref[...], table(rows_dev, edges_ref[0:1, at] - HB)).astype(BF)
        recv_ref[:, at] = nn(lat_t_ref[...], table(rows_dev, edges_ref[1:2, at])).astype(BF)


def mesh_kernel(
    before_ref, after_ref, own_ref, recv_ref, edges_ref, w_ref, feats_ref,
    send_ref, slope_ref, agg_ref, sum_ref,
):
    rows_dev = agg_ref.shape[0]
    rim_t = transposed(jnp.concatenate([before_ref[...], after_ref[...]], axis=0))
    w0_t, w1_t, w2_t = transposed(w_ref[0]), transposed(w_ref[1]), transposed(w_ref[2])
    for at in spans(edges_ref.shape[1], MESH_SPAN):
        ids = edges_ref[0:1, at]
        ids = jnp.where(ids < HB, ids, jnp.where(ids < HB + rows_dev, -1, ids - rows_dev))
        rim_rows = nn(rim_t, table(2 * HB, ids))
        send_ref[:, at] = (own_ref[:, at].astype(F32) + rim_rows).astype(BF)
        x = nn(w0_t, send_ref[:, at]) + nn(w1_t, recv_ref[:, at]) + nt(w2_t, feats_ref[at, :])
        message, slope = silu_parts(x)
        slope_ref[:, at] = slope
        part = nt(table(rows_dev, edges_ref[1:2, at]), message.astype(BF))
        if at.start:
            part = part + sum_ref[...]
        sum_ref[...] = part
    agg_ref[...] = sum_ref[...].astype(BF)


def contact_round(count, bound_t, far_t, w_t, self_ids, far_ids, both_ref, slope_ref, at):
    slots = bound_t.shape[1]
    place = lax.broadcasted_iota(jnp.int32, self_ids.shape, 1)
    live = (place < count).astype(F32)
    hits = table(slots, self_ids)
    both_ref[:128, at] = nn(bound_t, hits).astype(BF)
    both_ref[128:, at] = nn(far_t, table(slots, far_ids)).astype(BF)
    message, slope = silu_parts(nn(w_t, both_ref[:, at]))
    slope_ref[:, at] = slope * live
    return nt(hits, (message * live).astype(BF))


def contact_kernel(
    counts_ref, bound_t_ref, far0_ref, far1_ref, far2_ref, w_ref, contacts_ref,
    both_ref, slope_ref, sum_ref,
):
    fars = (far0_ref, far1_ref, far2_ref)
    w_t = jnp.concatenate([transposed(w_ref[3]), transposed(w_ref[4])], axis=1)
    round_rows = both_ref.shape[1] // len(fars)
    for r, at in enumerate(spans(both_ref.shape[1], round_rows)):
        part = contact_round(
            counts_ref[0, r], bound_t_ref[...], fars[r][...], w_t,
            contacts_ref[0:1, at], contacts_ref[1:2, at], both_ref, slope_ref, at,
        )
        sum_ref[...] = part + sum_ref[...] if r else part


def main_kernel(
    counts_ref, core_ref, lat_ref, lat_t_ref, bound_t_ref, far3_ref, both_ref, slope_c_ref,
    aggb_ref, send_ref, recv_ref, slope_m_ref, agg_ref, feats_ref, cot_ref, w_ref, edges_ref,
    contacts_ref, bnd_ref,
    new_ref, kept_ref, sent_ref, dm_ref, dc_ref, dn_ref,
    slope_l_ref, both_l_ref, gw_ref, aggc_ref, dagg_t_ref, daggc_t_ref,
    *, scale,
):
    rows_dev = lat_ref.shape[0]
    bound_count = bnd_ref.shape[1]
    round_rows = both_l_ref.shape[1]
    last = contacts_ref.shape[1] // round_rows - 1
    w_t = jnp.concatenate([transposed(w_ref[3]), transposed(w_ref[4])], axis=1)
    at = slice(last * round_rows, (last + 1) * round_rows)
    aggb = aggb_ref[...] + contact_round(
        counts_ref[0, last], bound_t_ref[...], far3_ref[...], w_t,
        contacts_ref[0:1, at], contacts_ref[1:2, at], both_l_ref, slope_l_ref, slice(None),
    )

    bound_table = table(rows_dev, bnd_ref[...])
    aggc_ref[...] = nn(bound_table, aggb.astype(BF)).astype(BF)
    for at in spans(rows_dev, NODE_SPAN):
        lat = lat_ref[at, :]
        cot = cot_ref[at, :]
        agg = agg_ref[at, :]
        aggc = aggc_ref[at, :]
        x = nn(lat, w_ref[5]) + nn(agg, w_ref[6]) + nn(aggc, w_ref[7])
        message, slope = silu_parts(x)
        hidden = message.astype(BF)
        new_ref[at, :] = (lat.astype(F32) + nn(hidden, w_ref[8])).astype(BF)
        d_node = (nt(cot, w_ref[8]) * slope).astype(BF)
        dn_ref[at, :] = d_node
        dagg_t_ref[:, at] = nt(w_ref[6], d_node).astype(BF)
        daggc_t_ref[:, at] = nt(w_ref[7], d_node).astype(BF)
        parts = [
            nn(lat_t_ref[:, at], d_node), tn(agg, d_node), tn(aggc, d_node), tn(hidden, cot)
        ]
        for k, part in enumerate(parts):
            where = slice(640 + 128 * k, 768 + 128 * k)
            gw_ref[where, :] = part + gw_ref[where, :] if at.start else part

    for at in spans(edges_ref.shape[1], MESH_SPAN):
        gathered = nn(dagg_t_ref[...], table(rows_dev, edges_ref[1:2, at]))
        d = (gathered * slope_m_ref[:, at]).astype(BF)
        dm_ref[:, at] = d
        parts = [nt(send_ref[:, at], d), nt(recv_ref[:, at], d), nn(d, feats_ref[at, :])]
        for k, part in enumerate(parts):
            where = slice(128 * k, 128 * k + 128)
            gw_ref[where, :] = part + gw_ref[where, :] if at.start else part

    gw_ref[256:384, :] = gw_ref[256:384, :].T
    dbg_t = nn(daggc_t_ref[...], bound_table).astype(BF)
    for r, at in enumerate(spans(contacts_ref.shape[1], round_rows)):
        gathered = nn(dbg_t, table(bound_count, contacts_ref[0:1, at]))
        slope = slope_l_ref[...] if r == last else slope_c_ref[:, at]
        both = both_l_ref[...] if r == last else both_ref[:, at]
        d = (gathered * slope).astype(BF)
        dc_ref[:, at] = d
        pair = nt(both, d)
        gw_ref[384:640, :] = pair + gw_ref[384:640, :] if r else pair

    half = gw_ref.shape[0] // 2
    core = core_ref[0]
    kept_ref[...] = gw_ref[pl.ds(pl.multiple_of(core * half, 64), half), :] * scale
    sent = gw_ref[pl.ds(pl.multiple_of((1 - core) * half, 64), half), :] * scale
    sent_ref[...] = sent.astype(BF)


def contact_back_kernel(
    w_ref, contacts_ref, dc_ref, far0_ref, far1_ref, far2_ref, far3_ref, own_ref
):
    outs = (far0_ref, far1_ref, far2_ref, far3_ref)
    bound_count = own_ref.shape[0]
    for r, at in enumerate(spans(contacts_ref.shape[1], contacts_ref.shape[1] // len(outs))):
        d = dc_ref[:, at]
        part = nt(table(bound_count, contacts_ref[0:1, at]), d)
        own_ref[...] = part + own_ref[...] if r else part
        far = nt(table(bound_count, contacts_ref[1:2, at]), d)
        outs[r][...] = wide_nt(far, w_ref[4]).astype(BF)
    own_ref[...] = wide_nt(own_ref[...], w_ref[3])


def send_back_kernel(w_ref, edges_ref, dm_ref, part_ref, low_ref, high_ref, send_ref):
    rows_dev = part_ref.shape[0]
    for at in spans(edges_ref.shape[1], MESH_SPAN):
        send = nt(table(rows_dev + 2 * HB, edges_ref[0:1, at]), dm_ref[:, at])
        send_ref[...] = send + send_ref[...] if at.start else send
    low_ref[...] = wide_nt(send_ref[:HB, :], w_ref[0]).astype(BF)
    high_ref[...] = wide_nt(send_ref[HB + rows_dev :, :], w_ref[0]).astype(BF)
    part_ref[...] = wide_nt(send_ref[HB : HB + rows_dev, :], w_ref[0])


def recv_back_kernel(w_ref, edges_ref, dm_ref, dn_ref, cot_ref, part_ref, grad_ref, recv_ref):
    rows_dev = cot_ref.shape[0]
    for at in spans(edges_ref.shape[1], MESH_SPAN):
        recv = nt(table(rows_dev, edges_ref[1:2, at]), dm_ref[:, at])
        recv_ref[...] = recv + recv_ref[...] if at.start else recv
    grad_ref[...] = (
        cot_ref[...].astype(F32)
        + nt(dn_ref[...], w_ref[5])
        + wide_nt(recv_ref[...], w_ref[1])
        + part_ref[...]
    )


def last_kernel(
    part_ref, own_ref, in0_ref, in1_ref, in2_ref, in3_ref, prev_ref, next_ref, bnd_ref, out_ref
):
    rows_dev = part_ref.shape[0]
    total = own_ref[...]
    for ref in (in0_ref, in1_ref, in2_ref, in3_ref):
        total = total + ref[...].astype(F32)
    out_ref[...] = part_ref[...] + wide_nn(table(rows_dev, bnd_ref[...]), total)
    out_ref[:HB, :] += prev_ref[...].astype(F32)
    out_ref[rows_dev - HB :, :] += next_ref[...].astype(F32)


def call(kernel, outs, args, scratch=(), smem=0, hbm=0, flops=0, mib=32):
    spec = pl.BlockSpec(memory_space=pltpu.VMEM)
    plain = len(args) - smem - hbm
    in_specs = [pl.BlockSpec(memory_space=pltpu.SMEM)] * smem + [spec] * plain
    in_specs += [pl.BlockSpec(memory_space=pltpu.HBM)] * hbm
    scratch_shapes = [pltpu.VMEM(shape, kind) for shape, kind in scratch]
    if hbm:
        scratch_shapes.append(pltpu.SemaphoreType.DMA((hbm,)))
    return pl.pallas_call(
        kernel,
        out_shape=[jax.ShapeDtypeStruct(shape, kind) for shape, kind in outs],
        in_specs=in_specs,
        out_specs=[spec] * len(outs),
        scratch_shapes=scratch_shapes,
        compiler_params=pltpu.CompilerParams(vmem_limit_bytes=mib * MIB),
        cost_estimate=pl.CostEstimate(flops=flops, bytes_accessed=4000000, transcendentals=0),
    )(*args)


def exchanged(block, mask_x=0, mask_y=0, mask_z=0, mask_core=0):
    route = []
    for region in range(32):
        for panel in range(8):
            other_region = region ^ ((mask_x >> 1) << 4 | mask_z << 1 | mask_core)
            other_panel = panel ^ ((mask_x & 1) << 2 | mask_y)
            route.append((region * 8 + panel, other_region * 8 + other_panel))
    return lax.ppermute(block, ("region", "panel"), route)


def shifted(array, by):
    size = lax.axis_size("panel")
    array = lax.ppermute(array, "panel", [(i, (i + by) % size) for i in range(size)])
    end = 0 if by > 0 else size - 1
    return jnp.where(lax.axis_index("panel") == end, jnp.zeros_like(array), array)


def wide(block):
    return block.astype(F32)


def ordered_by_y(found, row_y):
    odd, high = row_y % 2 == 1, row_y >= 2
    low_pair = [jnp.where(odd, found[1], found[0]), jnp.where(odd, found[0], found[1])]
    high_pair = [jnp.where(odd, found[3], found[2]), jnp.where(odd, found[2], found[3])]
    ordered = [jnp.where(high, b, a) for a, b in zip(low_pair, high_pair)]
    ordered += [jnp.where(high, a, b) for a, b in zip(low_pair, high_pair)]
    return jnp.concatenate(ordered, axis=0)


def joined(own, other, which):
    first = jnp.where(which == 0, own, other)
    second = jnp.where(which == 0, other, own)
    return jnp.concatenate([first, second], axis=0)


def tie(*arrays):
    return lax.optimization_barrier(arrays)


def shards(
    latents, edge_feats, weights, cotangent, mesh_edges, boundary, contact_edges, contact_counts
):
    rows_dev, width = latents.shape
    bound_count = boundary.shape[0]
    rounds = contact_counts.shape[1]
    edge_count = mesh_edges.shape[1]
    contact_count = contact_edges.shape[1]
    bnd = boundary.reshape(1, bound_count)
    core = lax.axis_index("region") % 2
    row_y = lax.axis_index("panel") % 4
    scale = 1.0 / math.sqrt(rows_dev * lax.axis_size("region") * lax.axis_size("panel"))

    low_rows, high_rows, lat_t, bound_t = call(
        bound_kernel,
        [((HB, width), BF), ((HB, width), BF), ((width, rows_dev), BF), ((width, bound_count), BF)],
        [latents, bnd],
        [((rows_dev, width), BF), ((1, bound_count), jnp.int32)],
        hbm=2,
        flops=10**10,
        mib=8,
    )
    before = shifted(high_rows, 1)
    after = shifted(low_rows, -1)
    fars = [exchanged(bound_t, mask_core=1)]
    fars += [exchanged(bound_t, mask_z=mask) for mask in (1, 2)]
    own_rows, recv_rows = call(
        gather_kernel,
        [((width, edge_count), BF), ((width, edge_count), BF)],
        [lat_t, mesh_edges],
        flops=4 * 10**9,
        mib=16,
    )
    before, after, own_rows = tie(before, after, own_rows)
    send_rows, slope, agg = call(
        mesh_kernel,
        [((width, edge_count), BF), ((width, edge_count), F32), ((rows_dev, width), BF)],
        [before, after, own_rows, recv_rows, mesh_edges, weights, edge_feats],
        [((rows_dev, width), F32)],
        flops=3 * 10**9,
        mib=16,
    )
    far_two, send_rows = tie(fars[2], send_rows)
    fars.append(exchanged(far_two, mask_z=6))
    first = (rounds - 1) * contact_count // rounds
    both, slope_c, aggb = call(
        contact_kernel,
        [((2 * width, first), BF), ((width, first), F32), ((bound_count, width), F32)],
        [contact_counts, bound_t, *fars[:3], weights, contact_edges],
        smem=1,
        flops=3 * 10**9,
        mib=16,
    )
    fars[3], both = tie(fars[3], both)
    new_rows, kept, sent, d_mesh, d_contact, d_node = call(
        functools.partial(main_kernel, scale=scale),
        [
            ((rows_dev, width), BF),
            ((9 * width // 2, width), F32),
            ((9 * width // 2, width), BF),
            ((width, edge_count), BF),
            ((width, contact_count), BF),
            ((rows_dev, width), BF),
        ],
        [contact_counts, core.reshape(1), latents, lat_t, bound_t, fars[3], both, slope_c, aggb]
        + [send_rows, recv_rows, slope, agg]
        + [edge_feats, cotangent, weights, mesh_edges, contact_edges, bnd],
        [
            ((width, contact_count // rounds), F32),
            ((2 * width, contact_count // rounds), BF),
            ((9 * width, width), F32),
            ((rows_dev, width), BF),
            ((width, rows_dev), BF),
            ((width, rows_dev), BF),
        ],
        smem=2,
        flops=6 * 10**9,
        mib=20,
    )
    other = exchanged(sent, mask_core=1)
    part, low, high = call(
        send_back_kernel,
        [((rows_dev, width), F32), ((HB, width), BF), ((HB, width), BF)],
        [weights, mesh_edges, d_mesh],
        [((rows_dev + 2 * HB, width), F32)],
        flops=2 * 10**9,
        mib=16,
    )
    other, part, low, high, d_contact = tie(other, part, low, high, d_contact)
    block = kept + wide(other)
    size = block.shape[0] // 4
    pieces = [
        lax.dynamic_slice_in_dim(block, (row_y ^ mask) * size, size, 0) for mask in range(4)
    ]
    found = [exchanged(pieces[mask].astype(BF), mask_y=mask) for mask in (1, 2, 3)]
    *far_grads, own_grad = call(
        contact_back_kernel,
        [((bound_count, width), BF)] * rounds + [((bound_count, width), F32)],
        [weights, contact_edges, d_contact],
        flops=2 * 10**9,
        mib=16,
    )
    one, two, three, *far_grads = tie(*found, *far_grads)
    block = ((pieces[0] + wide(one)) + (wide(two) + wide(three))).astype(BF)

    rim = jnp.where(row_y == 0, low, high)
    one = exchanged(jnp.concatenate([block, rim], axis=0), mask_x=1)
    two, three = [exchanged(block, mask_x=mask) for mask in (2, 3)]
    in_one = exchanged(far_grads[1], mask_z=1)
    pair = exchanged(jnp.concatenate(far_grads[2:], axis=0), mask_z=2)
    one, two, three, part = tie(one, two, three, part)
    rim = one[size:]
    block = ((wide(block) + wide(one[:size])) + (wide(two) + wide(three))).astype(BF)

    other = exchanged(block, mask_z=1)
    (part,) = call(
        recv_back_kernel,
        [((rows_dev, width), F32)],
        [weights, mesh_edges, d_mesh, d_node, cotangent, part],
        [((rows_dev, width), F32)],
        flops=2 * 10**9,
        mib=16,
    )
    other, part, in_one = tie(other, part, in_one)
    block = (wide(block) + wide(other)).astype(BF)
    other = exchanged(block, mask_z=2)
    in_zero = exchanged(far_grads[0], mask_core=1)
    other, in_zero, pair = tie(other, in_zero, pair)
    block = (wide(block) + wide(other)).astype(BF)
    in_two = pair[:bound_count]
    other = exchanged(jnp.concatenate([block, pair[bound_count:]], axis=0), mask_z=6)
    in_three = other[size:]
    block = (wide(block) + wide(other[:size])).astype(BF)

    rim = jnp.where(row_y == 1, high, jnp.where(row_y == 2, low, rim))
    three = exchanged(jnp.concatenate([block, rim], axis=0), mask_y=3)
    rim = jnp.where(row_y % 2 == 0, high, low)
    one = exchanged(jnp.concatenate([block, rim], axis=0), mask_y=1)
    two = exchanged(block, mask_y=2)
    one, two, three = tie(one, two, three)
    panel = lax.axis_index("panel")
    nothing = jnp.zeros_like(rim)
    from_prev = jnp.where(row_y % 2 == 0, three[size:], one[size:])
    from_prev = jnp.where(panel == 0, nothing, from_prev)
    from_next = jnp.where(row_y % 2 == 0, one[size:], three[size:])
    from_next = jnp.where(panel == lax.axis_size("panel") - 1, nothing, from_next)
    block = ordered_by_y([block, one[:size], two, three[:size]], row_y)
    other = exchanged(block, mask_core=1)
    (grad_rows,) = call(
        last_kernel,
        [((rows_dev, width), F32)],
        [part, own_grad, in_zero, in_one, in_two, in_three, from_prev, from_next, bnd],
        flops=10**8,
        mib=8,
    )
    block = joined(wide(block), wide(other), core)
    return (new_rows, grad_rows, block.reshape(9, width, width))


def solution(mesh):
    blocks = P(("region", "panel"), None)
    placed = (
        blocks,
        blocks,
        P(),
        blocks,
        P(None, ("region", "panel")),
        P(("region", "panel")),
        P(None, ("region", "panel")),
        blocks,
    )
    return jax.shard_map(
        shards, mesh=mesh, in_specs=placed, out_specs=(blocks, blocks, P()), check_vma=False
    )
```

```python
import functools
import math

import jax
import jax.numpy as jnp
from jax import lax
from jax.experimental import pallas as pl
from jax.experimental.pallas import tpu as pltpu
from jax.sharding import PartitionSpec as P

HB = 64
BF = jnp.bfloat16
F32 = jnp.float32
MESH_SPAN = 1536
NODE_SPAN = 512
MIB = 1024 * 1024


def nn(a, b):
    return lax.dot_general(a, b, (((1,), (0,)), ((), ())), preferred_element_type=F32)


def nt(a, b):
    return lax.dot_general(a, b, (((1,), (1,)), ((), ())), preferred_element_type=F32)


def tn(a, b):
    return lax.dot_general(a, b, (((0,), (0,)), ((), ())), preferred_element_type=F32)


def in_two(values):
    high = values.astype(BF)
    return high, (values - high.astype(F32)).astype(BF)


def wide_nt(a, b):
    high, low = in_two(a)
    return nt(high, b) + nt(low, b)


def wide_nn(a, b):
    high, low = in_two(b)
    return nn(a, high) + nn(a, low)


def identity():
    row = lax.broadcasted_iota(jnp.int32, (128, 128), 0)
    column = lax.broadcasted_iota(jnp.int32, (128, 128), 1)
    return (row == column).astype(BF)


def transposed(a):
    return nt(identity(), a).astype(BF)


def table(count, ids):
    rows = lax.broadcasted_iota(jnp.int32, (count, ids.shape[1]), 0)
    return (rows == ids).astype(BF)


def silu_parts(x):
    s = 0.5 * jnp.tanh(0.5 * x) + 0.5
    return x * s, s * (1.0 + x * (1.0 - s))


def spans(total, size):
    return [slice(first, first + size) for first in range(0, total, size)]


def fetched(pairs, sems):
    copies = [pltpu.make_async_copy(a, b, sems.at[k]) for k, (a, b) in enumerate(pairs)]
    for copy in copies:
        copy.start()
    return copies


def bound_kernel(lat_hbm, bnd_hbm, low_ref, high_ref, lat_t_ref, bound_t_ref, lat, bnd, sems):
    for copy in fetched([(lat_hbm, lat), (bnd_hbm, bnd)], sems):
        copy.wait()
    rows_dev = lat.shape[0]
    low_ref[...] = lat[:HB, :]
    high_ref[...] = lat[rows_dev - HB :, :]
    lat_t = transposed(lat[...])
    lat_t_ref[...] = lat_t
    bound_t_ref[...] = nn(lat_t, table(rows_dev, bnd[...])).astype(BF)


def gather_kernel(lat_t_ref, edges_ref, send_ref, recv_ref):
    rows_dev = lat_t_ref.shape[1]
    for at in spans(edges_ref.shape[1], MESH_SPAN):
        send_ref[:, at] = nn(lat_t_ref[...], table(rows_dev, edges_ref[0:1, at] - HB)).astype(BF)
        recv_ref[:, at] = nn(lat_t_ref[...], table(rows_dev, edges_ref[1:2, at])).astype(BF)


def mesh_kernel(
    before_ref, after_ref, own_ref, recv_ref, edges_ref, w_ref, feats_ref,
    send_ref, slope_ref, agg_ref, sum_ref,
):
    rows_dev = agg_ref.shape[0]
    rim_t = transposed(jnp.concatenate([before_ref[...], after_ref[...]], axis=0))
    w0_t, w1_t, w2_t = transposed(w_ref[0]), transposed(w_ref[1]), transposed(w_ref[2])
    for at in spans(edges_ref.shape[1], MESH_SPAN):
        ids = edges_ref[0:1, at]
        ids = jnp.where(ids < HB, ids, jnp.where(ids < HB + rows_dev, -1, ids - rows_dev))
        rim_rows = nn(rim_t, table(2 * HB, ids))
        send_ref[:, at] = (own_ref[:, at].astype(F32) + rim_rows).astype(BF)
        x = nn(w0_t, send_ref[:, at]) + nn(w1_t, recv_ref[:, at]) + nt(w2_t, feats_ref[at, :])
        message, slope = silu_parts(x)
        slope_ref[:, at] = slope
        part = nt(table(rows_dev, edges_ref[1:2, at]), message.astype(BF))
        if at.start:
            part = part + sum_ref[...]
        sum_ref[...] = part
    agg_ref[...] = sum_ref[...].astype(BF)


def contact_round(count, bound_t, far_t, w_t, self_ids, far_ids, both_ref, slope_ref, at):
    slots = bound_t.shape[1]
    place = lax.broadcasted_iota(jnp.int32, self_ids.shape, 1)
    live = (place < count).astype(F32)
    hits = table(slots, self_ids)
    both_ref[:128, at] = nn(bound_t, hits).astype(BF)
    both_ref[128:, at] = nn(far_t, table(slots, far_ids)).astype(BF)
    message, slope = silu_parts(nn(w_t, both_ref[:, at]))
    slope_ref[:, at] = slope * live
    return nt(hits, (message * live).astype(BF))


def contact_kernel(
    counts_ref, bound_t_ref, far0_ref, far1_ref, far2_ref, w_ref, contacts_ref,
    both_ref, slope_ref, sum_ref,
):
    fars = (far0_ref, far1_ref, far2_ref)
    w_t = jnp.concatenate([transposed(w_ref[3]), transposed(w_ref[4])], axis=1)
    round_rows = both_ref.shape[1] // len(fars)
    for r, at in enumerate(spans(both_ref.shape[1], round_rows)):
        part = contact_round(
            counts_ref[0, r], bound_t_ref[...], fars[r][...], w_t,
            contacts_ref[0:1, at], contacts_ref[1:2, at], both_ref, slope_ref, at,
        )
        sum_ref[...] = part + sum_ref[...] if r else part


def main_kernel(
    counts_ref, core_ref, lat_ref, lat_t_ref, bound_t_ref, far3_ref, both_ref, slope_c_ref,
    aggb_ref, send_ref, recv_ref, slope_m_ref, agg_ref, feats_ref, cot_ref, w_ref, edges_ref,
    contacts_ref, bnd_ref,
    new_ref, kept_ref, sent_ref, dm_ref, dc_ref, dn_ref,
    slope_l_ref, both_l_ref, gw_ref, aggc_ref, dagg_t_ref, daggc_t_ref,
    *, scale,
):
    rows_dev = lat_ref.shape[0]
    bound_count = bnd_ref.shape[1]
    round_rows = both_l_ref.shape[1]
    last = contacts_ref.shape[1] // round_rows - 1
    w_t = jnp.concatenate([transposed(w_ref[3]), transposed(w_ref[4])], axis=1)
    at = slice(last * round_rows, (last + 1) * round_rows)
    aggb = aggb_ref[...] + contact_round(
        counts_ref[0, last], bound_t_ref[...], far3_ref[...], w_t,
        contacts_ref[0:1, at], contacts_ref[1:2, at], both_l_ref, slope_l_ref, slice(None),
    )

    bound_table = table(rows_dev, bnd_ref[...])
    aggc_ref[...] = nn(bound_table, aggb.astype(BF)).astype(BF)
    for at in spans(rows_dev, NODE_SPAN):
        lat = lat_ref[at, :]
        cot = cot_ref[at, :]
        agg = agg_ref[at, :]
        aggc = aggc_ref[at, :]
        x = nn(lat, w_ref[5]) + nn(agg, w_ref[6]) + nn(aggc, w_ref[7])
        message, slope = silu_parts(x)
        hidden = message.astype(BF)
        new_ref[at, :] = (lat.astype(F32) + nn(hidden, w_ref[8])).astype(BF)
        d_node = (nt(cot, w_ref[8]) * slope).astype(BF)
        dn_ref[at, :] = d_node
        dagg_t_ref[:, at] = nt(w_ref[6], d_node).astype(BF)
        daggc_t_ref[:, at] = nt(w_ref[7], d_node).astype(BF)
        parts = [
            nn(lat_t_ref[:, at], d_node), tn(agg, d_node), tn(aggc, d_node), tn(hidden, cot)
        ]
        for k, part in enumerate(parts):
            where = slice(640 + 128 * k, 768 + 128 * k)
            gw_ref[where, :] = part + gw_ref[where, :] if at.start else part

    for at in spans(edges_ref.shape[1], MESH_SPAN):
        gathered = nn(dagg_t_ref[...], table(rows_dev, edges_ref[1:2, at]))
        d = (gathered * slope_m_ref[:, at]).astype(BF)
        dm_ref[:, at] = d
        parts = [nt(send_ref[:, at], d), nt(recv_ref[:, at], d), nn(d, feats_ref[at, :])]
        for k, part in enumerate(parts):
            where = slice(128 * k, 128 * k + 128)
            gw_ref[where, :] = part + gw_ref[where, :] if at.start else part

    gw_ref[256:384, :] = gw_ref[256:384, :].T
    dbg_t = nn(daggc_t_ref[...], bound_table).astype(BF)
    for r, at in enumerate(spans(contacts_ref.shape[1], round_rows)):
        gathered = nn(dbg_t, table(bound_count, contacts_ref[0:1, at]))
        slope = slope_l_ref[...] if r == last else slope_c_ref[:, at]
        both = both_l_ref[...] if r == last else both_ref[:, at]
        d = (gathered * slope).astype(BF)
        dc_ref[:, at] = d
        pair = nt(both, d)
        gw_ref[384:640, :] = pair + gw_ref[384:640, :] if r else pair

    half = gw_ref.shape[0] // 2
    core = core_ref[0]
    kept_ref[...] = gw_ref[pl.ds(pl.multiple_of(core * half, 64), half), :] * scale
    sent = gw_ref[pl.ds(pl.multiple_of((1 - core) * half, 64), half), :] * scale
    sent_ref[...] = sent.astype(BF)


def contact_back_kernel(
    w_ref, contacts_ref, dc_ref, far0_ref, far1_ref, far2_ref, far3_ref, own_ref
):
    outs = (far0_ref, far1_ref, far2_ref, far3_ref)
    bound_count = own_ref.shape[0]
    for r, at in enumerate(spans(contacts_ref.shape[1], contacts_ref.shape[1] // len(outs))):
        d = dc_ref[:, at]
        part = nt(table(bound_count, contacts_ref[0:1, at]), d)
        own_ref[...] = part + own_ref[...] if r else part
        far = nt(table(bound_count, contacts_ref[1:2, at]), d)
        outs[r][...] = wide_nt(far, w_ref[4]).astype(BF)
    own_ref[...] = wide_nt(own_ref[...], w_ref[3])


def send_back_kernel(w_ref, edges_ref, dm_ref, part_ref, low_ref, high_ref, send_ref):
    rows_dev = part_ref.shape[0]
    for at in spans(edges_ref.shape[1], MESH_SPAN):
        send = nt(table(rows_dev + 2 * HB, edges_ref[0:1, at]), dm_ref[:, at])
        send_ref[...] = send + send_ref[...] if at.start else send
    low_ref[...] = wide_nt(send_ref[:HB, :], w_ref[0]).astype(BF)
    high_ref[...] = wide_nt(send_ref[HB + rows_dev :, :], w_ref[0]).astype(BF)
    part_ref[...] = wide_nt(send_ref[HB : HB + rows_dev, :], w_ref[0])


def recv_back_kernel(w_ref, edges_ref, dm_ref, dn_ref, cot_ref, part_ref, grad_ref, recv_ref):
    rows_dev = cot_ref.shape[0]
    for at in spans(edges_ref.shape[1], MESH_SPAN):
        recv = nt(table(rows_dev, edges_ref[1:2, at]), dm_ref[:, at])
        recv_ref[...] = recv + recv_ref[...] if at.start else recv
    grad_ref[...] = (
        cot_ref[...].astype(F32)
        + nt(dn_ref[...], w_ref[5])
        + wide_nt(recv_ref[...], w_ref[1])
        + part_ref[...]
    )


def last_kernel(
    part_ref, own_ref, in0_ref, in1_ref, in2_ref, in3_ref, prev_ref, next_ref, bnd_ref, out_ref
):
    rows_dev = part_ref.shape[0]
    total = own_ref[...]
    for ref in (in0_ref, in1_ref, in2_ref, in3_ref):
        total = total + ref[...].astype(F32)
    out_ref[...] = part_ref[...] + wide_nn(table(rows_dev, bnd_ref[...]), total)
    out_ref[:HB, :] += prev_ref[...].astype(F32)
    out_ref[rows_dev - HB :, :] += next_ref[...].astype(F32)


def call(kernel, outs, args, scratch=(), smem=0, hbm=0, flops=0, mib=32):
    spec = pl.BlockSpec(memory_space=pltpu.VMEM)
    plain = len(args) - smem - hbm
    in_specs = [pl.BlockSpec(memory_space=pltpu.SMEM)] * smem + [spec] * plain
    in_specs += [pl.BlockSpec(memory_space=pltpu.HBM)] * hbm
    scratch_shapes = [pltpu.VMEM(shape, kind) for shape, kind in scratch]
    if hbm:
        scratch_shapes.append(pltpu.SemaphoreType.DMA((hbm,)))
    return pl.pallas_call(
        kernel,
        out_shape=[jax.ShapeDtypeStruct(shape, kind) for shape, kind in outs],
        in_specs=in_specs,
        out_specs=[spec] * len(outs),
        scratch_shapes=scratch_shapes,
        compiler_params=pltpu.CompilerParams(vmem_limit_bytes=mib * MIB),
        cost_estimate=pl.CostEstimate(flops=flops, bytes_accessed=4000000, transcendentals=0),
    )(*args)


def exchanged(block, mask_x=0, mask_y=0, mask_z=0, mask_core=0):
    route = []
    for region in range(32):
        for panel in range(8):
            other_region = region ^ ((mask_x >> 1) << 4 | mask_z << 1 | mask_core)
            other_panel = panel ^ ((mask_x & 1) << 2 | mask_y)
            route.append((region * 8 + panel, other_region * 8 + other_panel))
    return lax.ppermute(block, ("region", "panel"), route)


def shifted(array, by):
    size = lax.axis_size("panel")
    array = lax.ppermute(array, "panel", [(i, (i + by) % size) for i in range(size)])
    end = 0 if by > 0 else size - 1
    return jnp.where(lax.axis_index("panel") == end, jnp.zeros_like(array), array)


def wide(block):
    return block.astype(F32)


def ordered_by_y(found, row_y):
    odd, high = row_y % 2 == 1, row_y >= 2
    low_pair = [jnp.where(odd, found[1], found[0]), jnp.where(odd, found[0], found[1])]
    high_pair = [jnp.where(odd, found[3], found[2]), jnp.where(odd, found[2], found[3])]
    ordered = [jnp.where(high, b, a) for a, b in zip(low_pair, high_pair)]
    ordered += [jnp.where(high, a, b) for a, b in zip(low_pair, high_pair)]
    return jnp.concatenate(ordered, axis=0)


def joined(own, other, which):
    first = jnp.where(which == 0, own, other)
    second = jnp.where(which == 0, other, own)
    return jnp.concatenate([first, second], axis=0)


def tie(*arrays):
    return lax.optimization_barrier(arrays)


def shards(
    latents, edge_feats, weights, cotangent, mesh_edges, boundary, contact_edges, contact_counts
):
    rows_dev, width = latents.shape
    bound_count = boundary.shape[0]
    rounds = contact_counts.shape[1]
    edge_count = mesh_edges.shape[1]
    contact_count = contact_edges.shape[1]
    bnd = boundary.reshape(1, bound_count)
    core = lax.axis_index("region") % 2
    row_y = lax.axis_index("panel") % 4
    scale = 1.0 / math.sqrt(rows_dev * lax.axis_size("region") * lax.axis_size("panel"))

    low_rows, high_rows, lat_t, bound_t = call(
        bound_kernel,
        [((HB, width), BF), ((HB, width), BF), ((width, rows_dev), BF), ((width, bound_count), BF)],
        [latents, bnd],
        [((rows_dev, width), BF), ((1, bound_count), jnp.int32)],
        hbm=2,
        flops=10**10,
        mib=8,
    )
    before = shifted(high_rows, 1)
    after = shifted(low_rows, -1)
    fars = [exchanged(bound_t, mask_core=1)]
    fars += [exchanged(bound_t, mask_z=mask) for mask in (1, 2)]
    own_rows, recv_rows = call(
        gather_kernel,
        [((width, edge_count), BF), ((width, edge_count), BF)],
        [lat_t, mesh_edges],
        flops=4 * 10**9,
        mib=16,
    )
    before, after, own_rows = tie(before, after, own_rows)
    send_rows, slope, agg = call(
        mesh_kernel,
        [((width, edge_count), BF), ((width, edge_count), F32), ((rows_dev, width), BF)],
        [before, after, own_rows, recv_rows, mesh_edges, weights, edge_feats],
        [((rows_dev, width), F32)],
        flops=3 * 10**9,
        mib=16,
    )
    far_two, send_rows = tie(fars[2], send_rows)
    fars.append(exchanged(far_two, mask_z=6))
    first = (rounds - 1) * contact_count // rounds
    both, slope_c, aggb = call(
        contact_kernel,
        [((2 * width, first), BF), ((width, first), F32), ((bound_count, width), F32)],
        [contact_counts, bound_t, *fars[:3], weights, contact_edges],
        smem=1,
        flops=3 * 10**9,
        mib=16,
    )
    fars[3], both = tie(fars[3], both)
    new_rows, kept, sent, d_mesh, d_contact, d_node = call(
        functools.partial(main_kernel, scale=scale),
        [
            ((rows_dev, width), BF),
            ((9 * width // 2, width), F32),
            ((9 * width // 2, width), BF),
            ((width, edge_count), BF),
            ((width, contact_count), BF),
            ((rows_dev, width), BF),
        ],
        [contact_counts, core.reshape(1), latents, lat_t, bound_t, fars[3], both, slope_c, aggb]
        + [send_rows, recv_rows, slope, agg]
        + [edge_feats, cotangent, weights, mesh_edges, contact_edges, bnd],
        [
            ((width, contact_count // rounds), F32),
            ((2 * width, contact_count // rounds), BF),
            ((9 * width, width), F32),
            ((rows_dev, width), BF),
            ((width, rows_dev), BF),
            ((width, rows_dev), BF),
        ],
        smem=2,
        flops=6 * 10**9,
        mib=20,
    )
    other = exchanged(sent, mask_core=1)
    part, low, high = call(
        send_back_kernel,
        [((rows_dev, width), F32), ((HB, width), BF), ((HB, width), BF)],
        [weights, mesh_edges, d_mesh],
        [((rows_dev + 2 * HB, width), F32)],
        flops=2 * 10**9,
        mib=16,
    )
    other, part, low, high, d_contact = tie(other, part, low, high, d_contact)
    block = kept + wide(other)
    size = block.shape[0] // 4
    pieces = [
        lax.dynamic_slice_in_dim(block, (row_y ^ mask) * size, size, 0) for mask in range(4)
    ]
    two, one, three = [exchanged(pieces[mask].astype(BF), mask_y=mask) for mask in (2, 1, 3)]
    *far_grads, own_grad = call(
        contact_back_kernel,
        [((bound_count, width), BF)] * rounds + [((bound_count, width), F32)],
        [weights, contact_edges, d_contact],
        flops=2 * 10**9,
        mib=16,
    )
    two, one, three, *far_grads = tie(two, one, three, *far_grads)
    block = ((pieces[0] + wide(one)) + (wide(two) + wide(three))).astype(BF)

    rim = jnp.where(row_y == 0, low, high)
    two = exchanged(block, mask_x=2)
    one = exchanged(jnp.concatenate([block, rim], axis=0), mask_x=1)
    three = exchanged(block, mask_x=3)
    in_one = exchanged(far_grads[1], mask_z=1)
    pair = exchanged(jnp.concatenate(far_grads[2:], axis=0), mask_z=2)
    one, two, three, part = tie(one, two, three, part)
    rim = one[size:]
    block = ((wide(block) + wide(one[:size])) + (wide(two) + wide(three))).astype(BF)

    other = exchanged(block, mask_z=1)
    (part,) = call(
        recv_back_kernel,
        [((rows_dev, width), F32)],
        [weights, mesh_edges, d_mesh, d_node, cotangent, part],
        [((rows_dev, width), F32)],
        flops=2 * 10**9,
        mib=16,
    )
    other, part, in_one = tie(other, part, in_one)
    block = (wide(block) + wide(other)).astype(BF)
    other = exchanged(block, mask_z=2)
    in_zero = exchanged(far_grads[0], mask_core=1)
    other, in_zero, pair = tie(other, in_zero, pair)
    block = (wide(block) + wide(other)).astype(BF)
    in_two = pair[:bound_count]
    other = exchanged(block, mask_z=6)
    in_three = exchanged(pair[bound_count:], mask_z=6)
    block = (wide(block) + wide(other)).astype(BF)

    rim = jnp.where(row_y == 1, high, jnp.where(row_y == 2, low, rim))
    near = jnp.where(row_y % 2 == 0, high, low)
    two = exchanged(jnp.concatenate([block, near, near[:16]], axis=0), mask_y=2)
    one = exchanged(jnp.concatenate([block, near], axis=0), mask_y=1)
    three = exchanged(jnp.concatenate([block, rim], axis=0), mask_y=3)
    two, one, three, in_three = tie(two, one, three, in_three)
    panel = lax.axis_index("panel")
    nothing = jnp.zeros_like(rim)
    from_prev = jnp.where(row_y % 2 == 0, three[size:], one[size:])
    from_prev = jnp.where(panel == 0, nothing, from_prev)
    from_next = jnp.where(row_y % 2 == 0, one[size:], three[size:])
    from_next = jnp.where(panel == lax.axis_size("panel") - 1, nothing, from_next)
    block = ordered_by_y([block, one[:size], two[:size], three[:size]], row_y)
    other = exchanged(block, mask_core=1)
    (grad_rows,) = call(
        last_kernel,
        [((rows_dev, width), F32)],
        [part, own_grad, in_zero, in_one, in_two, in_three, from_prev, from_next, bnd],
        flops=10**8,
        mib=8,
    )
    block = joined(wide(block), wide(other), core)
    return (new_rows, grad_rows, block.reshape(9, width, width))


def solution(mesh):
    blocks = P(("region", "panel"), None)
    placed = (
        blocks,
        blocks,
        P(),
        blocks,
        P(None, ("region", "panel")),
        P(("region", "panel")),
        P(None, ("region", "panel")),
        blocks,
    )
    return jax.shard_map(
        shards, mesh=mesh, in_specs=placed, out_specs=(blocks, blocks, P()), check_vma=False
    )
```

```python
import functools
import math

import jax
import jax.numpy as jnp
from jax import lax
from jax.experimental import pallas as pl
from jax.experimental.pallas import tpu as pltpu
from jax.sharding import PartitionSpec as P

HB = 64
BF = jnp.bfloat16
F32 = jnp.float32
MESH_SPAN = 1536
NODE_SPAN = 512
MIB = 1024 * 1024


def nn(a, b):
    return lax.dot_general(a, b, (((1,), (0,)), ((), ())), preferred_element_type=F32)


def nt(a, b):
    return lax.dot_general(a, b, (((1,), (1,)), ((), ())), preferred_element_type=F32)


def tn(a, b):
    return lax.dot_general(a, b, (((0,), (0,)), ((), ())), preferred_element_type=F32)


def in_two(values):
    high = values.astype(BF)
    return high, (values - high.astype(F32)).astype(BF)


def wide_nt(a, b):
    high, low = in_two(a)
    return nt(high, b) + nt(low, b)


def wide_nn(a, b):
    high, low = in_two(b)
    return nn(a, high) + nn(a, low)


def identity():
    row = lax.broadcasted_iota(jnp.int32, (128, 128), 0)
    column = lax.broadcasted_iota(jnp.int32, (128, 128), 1)
    return (row == column).astype(BF)


def transposed(a):
    return nt(identity(), a).astype(BF)


def table(count, ids):
    rows = lax.broadcasted_iota(jnp.int32, (count, ids.shape[1]), 0)
    return (rows == ids).astype(BF)


def silu_parts(x):
    s = 0.5 * jnp.tanh(0.5 * x) + 0.5
    return x * s, s * (1.0 + x * (1.0 - s))


def spans(total, size):
    return [slice(first, first + size) for first in range(0, total, size)]


def fetched(pairs, sems):
    copies = [pltpu.make_async_copy(a, b, sems.at[k]) for k, (a, b) in enumerate(pairs)]
    for copy in copies:
        copy.start()
    return copies


def bound_kernel(lat_hbm, bnd_hbm, low_ref, high_ref, lat_t_ref, bound_t_ref, lat, bnd, sems):
    for copy in fetched([(lat_hbm, lat), (bnd_hbm, bnd)], sems):
        copy.wait()
    rows_dev = lat.shape[0]
    low_ref[...] = lat[:HB, :]
    high_ref[...] = lat[rows_dev - HB :, :]
    lat_t = transposed(lat[...])
    lat_t_ref[...] = lat_t
    bound_t_ref[...] = nn(lat_t, table(rows_dev, bnd[...])).astype(BF)


def gather_kernel(lat_t_ref, edges_ref, send_ref, recv_ref):
    rows_dev = lat_t_ref.shape[1]
    for at in spans(edges_ref.shape[1], MESH_SPAN):
        send_ref[:, at] = nn(lat_t_ref[...], table(rows_dev, edges_ref[0:1, at] - HB)).astype(BF)
        recv_ref[:, at] = nn(lat_t_ref[...], table(rows_dev, edges_ref[1:2, at])).astype(BF)


def mesh_kernel(
    before_ref, after_ref, own_ref, recv_ref, edges_ref, w_ref, feats_ref,
    send_ref, slope_ref, agg_ref, sum_ref,
):
    rows_dev = agg_ref.shape[0]
    rim_t = transposed(jnp.concatenate([before_ref[...], after_ref[...]], axis=0))
    w0_t, w1_t, w2_t = transposed(w_ref[0]), transposed(w_ref[1]), transposed(w_ref[2])
    for at in spans(edges_ref.shape[1], MESH_SPAN):
        ids = edges_ref[0:1, at]
        ids = jnp.where(ids < HB, ids, jnp.where(ids < HB + rows_dev, -1, ids - rows_dev))
        rim_rows = nn(rim_t, table(2 * HB, ids))
        send_ref[:, at] = (own_ref[:, at].astype(F32) + rim_rows).astype(BF)
        x = nn(w0_t, send_ref[:, at]) + nn(w1_t, recv_ref[:, at]) + nt(w2_t, feats_ref[at, :])
        message, slope = silu_parts(x)
        slope_ref[:, at] = slope
        part = nt(table(rows_dev, edges_ref[1:2, at]), message.astype(BF))
        if at.start:
            part = part + sum_ref[...]
        sum_ref[...] = part
    agg_ref[...] = sum_ref[...].astype(BF)


def contact_round(count, bound_t, far_t, w_t, self_ids, far_ids, both_ref, slope_ref, at):
    slots = bound_t.shape[1]
    place = lax.broadcasted_iota(jnp.int32, self_ids.shape, 1)
    live = (place < count).astype(F32)
    hits = table(slots, self_ids)
    both_ref[:128, at] = nn(bound_t, hits).astype(BF)
    both_ref[128:, at] = nn(far_t, table(slots, far_ids)).astype(BF)
    message, slope = silu_parts(nn(w_t, both_ref[:, at]))
    slope_ref[:, at] = slope * live
    return nt(hits, (message * live).astype(BF))


def contact_kernel(
    counts_ref, bound_t_ref, far0_ref, far1_ref, far2_ref, w_ref, contacts_ref,
    both_ref, slope_ref, sum_ref,
):
    fars = (far0_ref, far1_ref, far2_ref)
    w_t = jnp.concatenate([transposed(w_ref[3]), transposed(w_ref[4])], axis=1)
    round_rows = both_ref.shape[1] // len(fars)
    for r, at in enumerate(spans(both_ref.shape[1], round_rows)):
        part = contact_round(
            counts_ref[0, r], bound_t_ref[...], fars[r][...], w_t,
            contacts_ref[0:1, at], contacts_ref[1:2, at], both_ref, slope_ref, at,
        )
        sum_ref[...] = part + sum_ref[...] if r else part


def main_kernel(
    counts_ref, core_ref, lat_ref, lat_t_ref, bound_t_ref, far3_ref, both_ref, slope_c_ref,
    aggb_ref, send_ref, recv_ref, slope_m_ref, agg_ref, feats_ref, cot_ref, w_ref, edges_ref,
    contacts_ref, bnd_ref,
    new_ref, kept_ref, sent_ref, dm_ref, dc_ref, dn_ref,
    slope_l_ref, both_l_ref, gw_ref, aggc_ref, dagg_t_ref, daggc_t_ref,
    *, scale,
):
    rows_dev = lat_ref.shape[0]
    bound_count = bnd_ref.shape[1]
    round_rows = both_l_ref.shape[1]
    last = contacts_ref.shape[1] // round_rows - 1
    w_t = jnp.concatenate([transposed(w_ref[3]), transposed(w_ref[4])], axis=1)
    at = slice(last * round_rows, (last + 1) * round_rows)
    aggb = aggb_ref[...] + contact_round(
        counts_ref[0, last], bound_t_ref[...], far3_ref[...], w_t,
        contacts_ref[0:1, at], contacts_ref[1:2, at], both_l_ref, slope_l_ref, slice(None),
    )

    bound_table = table(rows_dev, bnd_ref[...])
    aggc_ref[...] = nn(bound_table, aggb.astype(BF)).astype(BF)
    for at in spans(rows_dev, NODE_SPAN):
        lat = lat_ref[at, :]
        cot = cot_ref[at, :]
        agg = agg_ref[at, :]
        aggc = aggc_ref[at, :]
        x = nn(lat, w_ref[5]) + nn(agg, w_ref[6]) + nn(aggc, w_ref[7])
        message, slope = silu_parts(x)
        hidden = message.astype(BF)
        new_ref[at, :] = (lat.astype(F32) + nn(hidden, w_ref[8])).astype(BF)
        d_node = (nt(cot, w_ref[8]) * slope).astype(BF)
        dn_ref[at, :] = d_node
        dagg_t_ref[:, at] = nt(w_ref[6], d_node).astype(BF)
        daggc_t_ref[:, at] = nt(w_ref[7], d_node).astype(BF)
        parts = [
            nn(lat_t_ref[:, at], d_node), tn(agg, d_node), tn(aggc, d_node), tn(hidden, cot)
        ]
        for k, part in enumerate(parts):
            where = slice(640 + 128 * k, 768 + 128 * k)
            gw_ref[where, :] = part + gw_ref[where, :] if at.start else part

    for at in spans(edges_ref.shape[1], MESH_SPAN):
        gathered = nn(dagg_t_ref[...], table(rows_dev, edges_ref[1:2, at]))
        d = (gathered * slope_m_ref[:, at]).astype(BF)
        dm_ref[:, at] = d
        parts = [nt(send_ref[:, at], d), nt(recv_ref[:, at], d), nn(d, feats_ref[at, :])]
        for k, part in enumerate(parts):
            where = slice(128 * k, 128 * k + 128)
            gw_ref[where, :] = part + gw_ref[where, :] if at.start else part

    gw_ref[256:384, :] = gw_ref[256:384, :].T
    dbg_t = nn(daggc_t_ref[...], bound_table).astype(BF)
    for r, at in enumerate(spans(contacts_ref.shape[1], round_rows)):
        gathered = nn(dbg_t, table(bound_count, contacts_ref[0:1, at]))
        slope = slope_l_ref[...] if r == last else slope_c_ref[:, at]
        both = both_l_ref[...] if r == last else both_ref[:, at]
        d = (gathered * slope).astype(BF)
        dc_ref[:, at] = d
        pair = nt(both, d)
        gw_ref[384:640, :] = pair + gw_ref[384:640, :] if r else pair

    half = gw_ref.shape[0] // 2
    core = core_ref[0]
    kept_ref[...] = gw_ref[pl.ds(pl.multiple_of(core * half, 64), half), :] * scale
    sent = gw_ref[pl.ds(pl.multiple_of((1 - core) * half, 64), half), :] * scale
    sent_ref[...] = sent.astype(BF)


def contact_back_kernel(
    w_ref, contacts_ref, dc_ref, far0_ref, far1_ref, far2_ref, far3_ref, own_ref
):
    outs = (far0_ref, far1_ref, far2_ref, far3_ref)
    bound_count = own_ref.shape[0]
    for r, at in enumerate(spans(contacts_ref.shape[1], contacts_ref.shape[1] // len(outs))):
        d = dc_ref[:, at]
        part = nt(table(bound_count, contacts_ref[0:1, at]), d)
        own_ref[...] = part + own_ref[...] if r else part
        far = nt(table(bound_count, contacts_ref[1:2, at]), d)
        outs[r][...] = wide_nt(far, w_ref[4]).astype(BF)
    own_ref[...] = wide_nt(own_ref[...], w_ref[3])


def send_back_kernel(w_ref, edges_ref, dm_ref, part_ref, low_ref, high_ref, send_ref):
    rows_dev = part_ref.shape[0]
    for at in spans(edges_ref.shape[1], MESH_SPAN):
        send = nt(table(rows_dev + 2 * HB, edges_ref[0:1, at]), dm_ref[:, at])
        send_ref[...] = send + send_ref[...] if at.start else send
    low_ref[...] = wide_nt(send_ref[:HB, :], w_ref[0]).astype(BF)
    high_ref[...] = wide_nt(send_ref[HB + rows_dev :, :], w_ref[0]).astype(BF)
    part_ref[...] = wide_nt(send_ref[HB : HB + rows_dev, :], w_ref[0])


def recv_back_kernel(w_ref, edges_ref, dm_ref, dn_ref, cot_ref, part_ref, grad_ref, recv_ref):
    rows_dev = cot_ref.shape[0]
    for at in spans(edges_ref.shape[1], MESH_SPAN):
        recv = nt(table(rows_dev, edges_ref[1:2, at]), dm_ref[:, at])
        recv_ref[...] = recv + recv_ref[...] if at.start else recv
    grad_ref[...] = (
        cot_ref[...].astype(F32)
        + nt(dn_ref[...], w_ref[5])
        + wide_nt(recv_ref[...], w_ref[1])
        + part_ref[...]
    )


def last_kernel(
    part_ref, own_ref, in0_ref, in1_ref, in2_ref, in3_ref, prev_ref, next_ref, bnd_ref, out_ref
):
    rows_dev = part_ref.shape[0]
    total = own_ref[...]
    for ref in (in0_ref, in1_ref, in2_ref, in3_ref):
        total = total + ref[...].astype(F32)
    out_ref[...] = part_ref[...] + wide_nn(table(rows_dev, bnd_ref[...]), total)
    out_ref[:HB, :] += prev_ref[...].astype(F32)
    out_ref[rows_dev - HB :, :] += next_ref[...].astype(F32)


def call(kernel, outs, args, scratch=(), smem=0, hbm=0, flops=0, mib=32):
    spec = pl.BlockSpec(memory_space=pltpu.VMEM)
    plain = len(args) - smem - hbm
    in_specs = [pl.BlockSpec(memory_space=pltpu.SMEM)] * smem + [spec] * plain
    in_specs += [pl.BlockSpec(memory_space=pltpu.HBM)] * hbm
    scratch_shapes = [pltpu.VMEM(shape, kind) for shape, kind in scratch]
    if hbm:
        scratch_shapes.append(pltpu.SemaphoreType.DMA((hbm,)))
    return pl.pallas_call(
        kernel,
        out_shape=[jax.ShapeDtypeStruct(shape, kind) for shape, kind in outs],
        in_specs=in_specs,
        out_specs=[spec] * len(outs),
        scratch_shapes=scratch_shapes,
        compiler_params=pltpu.CompilerParams(vmem_limit_bytes=mib * MIB),
        cost_estimate=pl.CostEstimate(flops=flops, bytes_accessed=4000000, transcendentals=0),
    )(*args)


def exchanged(block, mask_x=0, mask_y=0, mask_z=0, mask_core=0):
    route = []
    for region in range(32):
        for panel in range(8):
            other_region = region ^ ((mask_x >> 1) << 4 | mask_z << 1 | mask_core)
            other_panel = panel ^ ((mask_x & 1) << 2 | mask_y)
            route.append((region * 8 + panel, other_region * 8 + other_panel))
    return lax.ppermute(block, ("region", "panel"), route)


def shifted(array, by):
    size = lax.axis_size("panel")
    array = lax.ppermute(array, "panel", [(i, (i + by) % size) for i in range(size)])
    end = 0 if by > 0 else size - 1
    return jnp.where(lax.axis_index("panel") == end, jnp.zeros_like(array), array)


def wide(block):
    return block.astype(F32)


def ordered_by_y(found, row_y):
    odd, high = row_y % 2 == 1, row_y >= 2
    low_pair = [jnp.where(odd, found[1], found[0]), jnp.where(odd, found[0], found[1])]
    high_pair = [jnp.where(odd, found[3], found[2]), jnp.where(odd, found[2], found[3])]
    ordered = [jnp.where(high, b, a) for a, b in zip(low_pair, high_pair)]
    ordered += [jnp.where(high, a, b) for a, b in zip(low_pair, high_pair)]
    return jnp.concatenate(ordered, axis=0)


def joined(own, other, which):
    first = jnp.where(which == 0, own, other)
    second = jnp.where(which == 0, other, own)
    return jnp.concatenate([first, second], axis=0)


def tie(*arrays):
    return lax.optimization_barrier(arrays)


def shards(
    latents, edge_feats, weights, cotangent, mesh_edges, boundary, contact_edges, contact_counts
):
    rows_dev, width = latents.shape
    bound_count = boundary.shape[0]
    rounds = contact_counts.shape[1]
    edge_count = mesh_edges.shape[1]
    contact_count = contact_edges.shape[1]
    bnd = boundary.reshape(1, bound_count)
    core = lax.axis_index("region") % 2
    row_y = lax.axis_index("panel") % 4
    scale = 1.0 / math.sqrt(rows_dev * lax.axis_size("region") * lax.axis_size("panel"))

    low_rows, high_rows, lat_t, bound_t = call(
        bound_kernel,
        [((HB, width), BF), ((HB, width), BF), ((width, rows_dev), BF), ((width, bound_count), BF)],
        [latents, bnd],
        [((rows_dev, width), BF), ((1, bound_count), jnp.int32)],
        hbm=2,
        flops=10**10,
        mib=8,
    )
    before = shifted(high_rows, 1)
    after = shifted(low_rows, -1)
    fars = [exchanged(bound_t, mask_core=1)]
    fars += [exchanged(bound_t, mask_z=mask) for mask in (1, 2)]
    own_rows, recv_rows = call(
        gather_kernel,
        [((width, edge_count), BF), ((width, edge_count), BF)],
        [lat_t, mesh_edges],
        flops=4 * 10**9,
        mib=16,
    )
    before, after, own_rows = tie(before, after, own_rows)
    send_rows, slope, agg = call(
        mesh_kernel,
        [((width, edge_count), BF), ((width, edge_count), F32), ((rows_dev, width), BF)],
        [before, after, own_rows, recv_rows, mesh_edges, weights, edge_feats],
        [((rows_dev, width), F32)],
        flops=3 * 10**9,
        mib=16,
    )
    far_two, send_rows = tie(fars[2], send_rows)
    fars.append(exchanged(far_two, mask_z=6))
    first = (rounds - 1) * contact_count // rounds
    both, slope_c, aggb = call(
        contact_kernel,
        [((2 * width, first), BF), ((width, first), F32), ((bound_count, width), F32)],
        [contact_counts, bound_t, *fars[:3], weights, contact_edges],
        smem=1,
        flops=3 * 10**9,
        mib=16,
    )
    fars[3], both = tie(fars[3], both)
    new_rows, kept, sent, d_mesh, d_contact, d_node = call(
        functools.partial(main_kernel, scale=scale),
        [
            ((rows_dev, width), BF),
            ((9 * width // 2, width), F32),
            ((9 * width // 2, width), BF),
            ((width, edge_count), BF),
            ((width, contact_count), BF),
            ((rows_dev, width), BF),
        ],
        [contact_counts, core.reshape(1), latents, lat_t, bound_t, fars[3], both, slope_c, aggb]
        + [send_rows, recv_rows, slope, agg]
        + [edge_feats, cotangent, weights, mesh_edges, contact_edges, bnd],
        [
            ((width, contact_count // rounds), F32),
            ((2 * width, contact_count // rounds), BF),
            ((9 * width, width), F32),
            ((rows_dev, width), BF),
            ((width, rows_dev), BF),
            ((width, rows_dev), BF),
        ],
        smem=2,
        flops=6 * 10**9,
        mib=20,
    )
    other = exchanged(sent, mask_core=1)
    part, low, high = call(
        send_back_kernel,
        [((rows_dev, width), F32), ((HB, width), BF), ((HB, width), BF)],
        [weights, mesh_edges, d_mesh],
        [((rows_dev + 2 * HB, width), F32)],
        flops=2 * 10**9,
        mib=16,
    )
    other, part, low, high, d_contact = tie(other, part, low, high, d_contact)
    block = kept + wide(other)
    size = block.shape[0] // 4
    pieces = [
        lax.dynamic_slice_in_dim(block, (row_y ^ mask) * size, size, 0) for mask in range(4)
    ]
    two, one, three = [exchanged(pieces[mask].astype(BF), mask_y=mask) for mask in (2, 1, 3)]
    *far_grads, own_grad = call(
        contact_back_kernel,
        [((bound_count, width), BF)] * rounds + [((bound_count, width), F32)],
        [weights, contact_edges, d_contact],
        flops=2 * 10**9,
        mib=16,
    )
    two, one, three, *far_grads = tie(two, one, three, *far_grads)
    block = ((pieces[0] + wide(one)) + (wide(two) + wide(three))).astype(BF)

    rim = jnp.where(row_y == 0, low, high)
    two = exchanged(block, mask_x=2)
    one = exchanged(jnp.concatenate([block, rim], axis=0), mask_x=1)
    three = exchanged(block, mask_x=3)
    pair = exchanged(jnp.concatenate(far_grads[2:], axis=0), mask_z=2)
    one, two, three, part = tie(one, two, three, part)
    rim = one[size:]
    block = ((wide(block) + wide(one[:size])) + (wide(two) + wide(three))).astype(BF)

    other = exchanged(block, mask_z=1)
    (part,) = call(
        recv_back_kernel,
        [((rows_dev, width), F32)],
        [weights, mesh_edges, d_mesh, d_node, cotangent, part],
        [((rows_dev, width), F32)],
        flops=2 * 10**9,
        mib=16,
    )
    other, part, far_one = tie(other, part, far_grads[1])
    block = (wide(block) + wide(other)).astype(BF)
    other = exchanged(block, mask_z=2)
    in_one = exchanged(far_one, mask_z=1)
    in_zero = exchanged(far_grads[0], mask_core=1)
    other, in_zero, pair = tie(other, in_zero, pair)
    block = (wide(block) + wide(other)).astype(BF)
    in_two = pair[:bound_count]
    other = exchanged(block, mask_z=6)
    in_three = exchanged(pair[bound_count:], mask_z=6)
    other, in_one = tie(other, in_one)
    block = (wide(block) + wide(other)).astype(BF)

    rim = jnp.where(row_y == 1, high, jnp.where(row_y == 2, low, rim))
    near = jnp.where(row_y % 2 == 0, high, low)
    two = exchanged(jnp.concatenate([block, near, near[:16]], axis=0), mask_y=2)
    one = exchanged(jnp.concatenate([block, near], axis=0), mask_y=1)
    three = exchanged(jnp.concatenate([block, rim], axis=0), mask_y=3)
    two, one, three, in_three = tie(two, one, three, in_three)
    panel = lax.axis_index("panel")
    nothing = jnp.zeros_like(rim)
    from_prev = jnp.where(row_y % 2 == 0, three[size:], one[size:])
    from_prev = jnp.where(panel == 0, nothing, from_prev)
    from_next = jnp.where(row_y % 2 == 0, one[size:], three[size:])
    from_next = jnp.where(panel == lax.axis_size("panel") - 1, nothing, from_next)
    block = ordered_by_y([block, one[:size], two[:size], three[:size]], row_y)
    other = exchanged(block, mask_core=1)
    (grad_rows,) = call(
        last_kernel,
        [((rows_dev, width), F32)],
        [part, own_grad, in_zero, in_one, in_two, in_three, from_prev, from_next, bnd],
        flops=10**8,
        mib=8,
    )
    block = joined(wide(block), wide(other), core)
    return (new_rows, grad_rows, block.reshape(9, width, width))


def solution(mesh):
    blocks = P(("region", "panel"), None)
    placed = (
        blocks,
        blocks,
        P(),
        blocks,
        P(None, ("region", "panel")),
        P(("region", "panel")),
        P(None, ("region", "panel")),
        blocks,
    )
    return jax.shard_map(
        shards, mesh=mesh, in_specs=placed, out_specs=(blocks, blocks, P()), check_vma=False
    )
```
